32 devices in a mesh: dp: 8 (over y, x, core), tensor: 4 (over z).
Axes of the slice: x: 2, y: 2, z: 4, core: 2. Of those that a mesh axis runs over, the one named last changes fastest.
Arguments:
- inputs: bfloat16 [8192, 768], P(('dp', 'tensor')), may hold values from -6 to 6
- cotangent: bfloat16 [8192, 768], P(('dp', 'tensor')), may hold values from -6 to 6
- lengths: int32 [16], P('dp'), may hold values from 1 to 512, 5120 in all
- w_query: bfloat16 [768, 768], P(None, 'tensor'), may hold values from -0.21875 to 0.21875
- w_key: bfloat16 [768, 768], P(None, 'tensor'), may hold values from -0.21875 to 0.21875
- w_value: bfloat16 [768, 768], P(None, 'tensor'), may hold values from -0.21875 to 0.21875
- b_query: float32 [768], P('tensor'), may hold values from -3 to 3
- b_value: float32 [768], P('tensor'), may hold values from -2 to 2
- w_output: bfloat16 [768, 768], P('tensor'), may hold values from -1.75 to 1.75
- b_output: float32 [768], replicated, may hold values from -2 to 2
- gain_one: float32 [768], replicated, may hold values from 0.5 to 1.5
- shift_one: float32 [768], replicated, may hold values from -2 to 2
- w_hidden: bfloat16 [768, 3072], P(None, 'tensor'), may hold values from -0.21875 to 0.21875
- b_hidden: float32 [3072], P('tensor'), may hold values from -3 to 3
- w_back: bfloat16 [3072, 768], P('tensor'), may hold values from -0.109375 to 0.109375
- b_back: float32 [768], replicated, may hold values from -2 to 2
- gain_two: float32 [768], replicated, may hold values from 0.5 to 1.5
- shift_two: float32 [768], replicated, may hold values from -2 to 2
Outputs:
- outputs: bfloat16 [8192, 768], P(('dp', 'tensor'))
- input_grad: bfloat16 [8192, 768], P(('dp', 'tensor'))
- grad_w_query: float32 [768, 768], P(None, 'tensor')
- grad_w_key: float32 [768, 768], P(None, 'tensor')
- grad_w_value: float32 [768, 768], P(None, 'tensor')
- grad_b_query: float32 [768], P('tensor')
- grad_b_value: float32 [768], P('tensor')
- grad_w_output: float32 [768, 768], P('tensor')
- grad_b_output: float32 [768], replicated
- grad_gain_one: float32 [768], replicated
- grad_shift_one: float32 [768], replicated
- grad_w_hidden: float32 [768, 3072], P(None, 'tensor')
- grad_b_hidden: float32 [3072], P('tensor')
- grad_w_back: float32 [3072, 768], P('tensor')
- grad_b_back: float32 [768], replicated
- grad_gain_two: float32 [768], replicated
- grad_shift_two: float32 [768], replicated
The draws below stay inside these ranges and needn't reach their ends.
Inputs may be any that keep to these rules, and one draw needn't show every extreme that they name: lengths[s] counts the live rows at the start of slot s; the longest is exactly 512.
All inputs are finite; a program needn't handle non-finite values. No bound on the sum of `lengths` on one device may be relied on, other than what follows from the above.
Results may differ from the reference program's by a relative error of at most 0.02.
Values may be sent and summed in bfloat16 or wider, within the bound.
No kernel may reach another device: no remote copies, remote signals or barrier semaphores. Data moves between devices by JAX's collectives and lax.ppermute only.
A program may use at most 128 MiB of HBM per device.

```python
import math
import jax
import jax.numpy as jnp
import numpy as np
from jax import lax

D = 768
H = 12
HD = 64
FF = 3072
LSEQ = 512
SLOTS = 2
SEQS = 16
TOKENS = 8192
N_DP = 8


def level_of(own_key, shape, split, low, largest):
    loudness = 1.0
    for axis_at, shards_of in split:
        steps = jax.random.uniform(jax.random.fold_in(jax.random.fold_in(own_key, 6), axis_at), (shards_of,), jnp.float32, low / len(split), largest / len(split))
        loudness = loudness * jnp.repeat(jnp.exp(steps), shape[axis_at] // shards_of).reshape((-1,) + (1,) * (len(shape) - 1 - axis_at))
    return loudness


def profile(number_of, total, reach, slope):
    weights = [(1 << 20) // math.isqrt(rank ** slope) + 1 for rank in range(2, number_of + 1)]
    rest, counts = total - reach - (number_of - 1), [1] * (number_of - 1)
    while rest > 0:
        candidates = [i for i in range(number_of - 1) if counts[i] < reach]
        mass, left = sum([weights[i] for i in candidates]), rest
        for i in candidates:
            extra = min(reach - counts[i], max(1, left * weights[i] // mass), rest)
            counts[i] = counts[i] + extra
            rest = rest - extra
    return np.array([reach] + counts)


def ragged_sizes(own_key, count, total, reach, lean):
    if count == 2:
        one = jax.random.randint(own_key, (), max(1, total - reach), min(reach, total - 1) + 1)
        return jnp.stack([one, total - one])
    sizes = jnp.asarray(profile(count, total, reach, lean), jnp.int32)
    couples = (count - 1) // 2
    source_of, sink = sizes[1:1 + 2 * couples:2], sizes[2:2 + 2 * couples:2]
    room = jnp.minimum(source_of - 1, reach - sink)
    moved = jax.random.randint(jax.random.fold_in(own_key, 1), (couples,), 0, 1 << 20) % (room + 1)
    sizes = sizes.at[1:1 + 2 * couples:2].set(source_of - moved).at[2:2 + 2 * couples:2].set(sink + moved)
    return sizes[jax.random.permutation(jax.random.fold_in(own_key, 2), count)]


def normal_values(rng, shape, deviation, most, shards=(), held_as=jnp.bfloat16):
    loudness = level_of(rng, shape, shards, -0.22, 0.18) if shards else 1.0
    drawn = jax.random.normal(rng, shape, jnp.float32) * deviation * loudness
    return jnp.minimum(jnp.maximum(drawn, -most), most).astype(held_as)


def setup_inputs(seed: int = 0) -> dict:
    seeds = jax.random.split(jax.random.key(seed), 19)
    inputs = normal_values(seeds[0], (TOKENS, D), 1.0, 6.0, ((0, 32),))
    cotangent = normal_values(seeds[1], (TOKENS, D), 1.0, 6.0, ((0, 32),))
    lengths = ragged_sizes(seeds[2], SEQS, N_DP * SLOTS * LSEQ * 5 // 8, LSEQ, 2).astype(jnp.int32)
    w_query = normal_values(seeds[3], (D, D), D ** -0.5, 0.21875, ((1, 4),))
    w_key = normal_values(seeds[4], (D, D), D ** -0.5, 0.21875, ((1, 4),))
    w_value = normal_values(seeds[5], (D, D), D ** -0.5, 0.21875, ((1, 4),))
    b_query = normal_values(seeds[6], (D,), 0.5, 3.0, ((0, 4),), jnp.float32)
    b_value = normal_values(seeds[7], (D,), 0.3, 2.0, ((0, 4),), jnp.float32)
    w_output = normal_values(seeds[8], (D, D), (D // 64) ** -0.5, 1.75, ((0, 4),))
    b_output = normal_values(seeds[9], (D,), 0.3, 2.0, (), jnp.float32)
    gain_one = jnp.clip(1.0 + 0.1 * jax.random.normal(seeds[10], (D,), jnp.float32), 0.5, 1.5)
    shift_one = normal_values(seeds[11], (D,), 0.3, 2.0, (), jnp.float32)
    w_hidden = normal_values(seeds[12], (D, FF), D ** -0.5, 0.21875, ((1, 4),))
    b_hidden = normal_values(seeds[13], (FF,), 0.5, 3.0, ((0, 4),), jnp.float32)
    w_back = normal_values(seeds[14], (FF, D), FF ** -0.5, 0.109375, ((0, 4),))
    b_back = normal_values(seeds[15], (D,), 0.3, 2.0, (), jnp.float32)
    gain_two = jnp.clip(1.0 + 0.1 * jax.random.normal(seeds[16], (D,), jnp.float32), 0.5, 1.5)
    shift_two = normal_values(seeds[17], (D,), 0.3, 2.0, (), jnp.float32)
    return {"inputs": inputs, "cotangent": cotangent, "lengths": lengths, "w_query": w_query, "w_key": w_key, "w_value": w_value, "b_query": b_query, "b_value": b_value, "w_output": w_output, "b_output": b_output, "gain_one": gain_one, "shift_one": shift_one, "w_hidden": w_hidden, "b_hidden": b_hidden, "w_back": w_back, "b_back": b_back, "gain_two": gain_two, "shift_two": shift_two}


@jax.custom_vjp
def low(v):
    return lax.optimization_barrier(v.astype(jnp.bfloat16)).astype(jnp.float32)

@jax.custom_vjp
def low_back(v):
    return v

def low_keep(v):
    return (low(v), None)

def low_pass(kept, grad):
    return (grad,)

def back_keep(v):
    return (v, None)

def back_low(kept, grad):
    return (low(grad),)
low.defvjp(low_keep, low_pass)
low_back.defvjp(back_keep, back_low)
highest = lax.Precision.HIGHEST

def matmul(left_side, right_side):
    return jnp.dot(left_side, right_side, precision=highest, preferred_element_type=jnp.float32)

def layer_norm(rows_in, scales, offset):
    center = rows_in - lax.optimization_barrier(jnp.mean(rows_in, axis=-1, keepdims=True))
    spread = lax.optimization_barrier(jnp.mean(center * center, axis=-1, keepdims=True))
    return center * lax.rsqrt(spread + 1e-05) * scales + offset

def gelu_exact(pre_act):
    return jax.nn.gelu(pre_act, approximate=False)

def attend(pieces):
    queries, key_rows, values, key_live = pieces
    scores = low_back(jnp.einsum('qhd,khd->hqk', queries, key_rows, precision=highest) * 0.125)
    masked = jnp.where(key_live[None, None, :], scores, -1e+30)
    row_max = lax.optimization_barrier(jnp.max(masked, axis=-1, keepdims=True))
    exponent = jnp.exp(masked - row_max)
    attn_probs = exponent / lax.optimization_barrier(jnp.sum(exponent, axis=-1, keepdims=True))
    context = jnp.einsum('hqk,khd->qhd', low(attn_probs), values, precision=highest)
    return low(low_back(context))

def block_forward(inputs, params, key_live):
    w_query, w_key, w_value, b_query, b_value, w_output, b_output, gain_one, shift_one, w_hidden, b_hidden, w_back, b_back, gain_two, shift_two = params
    group_rows = inputs.shape[0]
    slot_count = key_live.shape[0]
    split_shape = (slot_count, group_rows // slot_count, H, HD)
    queries = low(low_back(matmul(inputs, w_query) + b_query))
    key_rows = low(low_back(matmul(inputs, w_key)))
    values = low(low_back(matmul(inputs, w_value) + b_value))
    context = lax.map(jax.checkpoint(attend), (queries.reshape(split_shape), key_rows.reshape(split_shape), values.reshape(split_shape), key_live))
    context = context.reshape(group_rows, D)
    attn_out = low_back(matmul(context, w_output) + b_output)
    mid = low(layer_norm(inputs + attn_out, gain_one, shift_one))
    pre_act = low_back(matmul(mid, w_hidden) + b_hidden)
    activation = low(gelu_exact(pre_act))
    branch = low_back(matmul(activation, w_back) + b_back)
    return layer_norm(mid + branch, gain_two, shift_two)

def reference(inputs, cotangent, lengths, w_query, w_key, w_value, b_query, b_value, w_output, b_output, gain_one, shift_one, w_hidden, b_hidden, w_back, b_back, gain_two, shift_two):
    params = tuple((weight.astype(jnp.float32) for weight in (w_query, w_key, w_value, b_query, b_value, w_output, b_output, gain_one, shift_one, w_hidden, b_hidden, w_back, b_back, gain_two, shift_two)))
    group_rows = SLOTS * LSEQ
    input_blocks = inputs.astype(jnp.float32).reshape(N_DP, group_rows, D)
    cot_blocks = cotangent.astype(jnp.float32).reshape(N_DP, group_rows, D)
    length_blocks = lengths.reshape(N_DP, SLOTS)
    positions = jnp.arange(LSEQ, dtype=jnp.int32)

    def block_step(totals, block_data):
        input_rows, cot_rows, slot_lengths = block_data
        key_live = positions[None, :] < slot_lengths[:, None]
        result, pull_back = jax.vjp(lambda rows_in, weights: block_forward(rows_in, weights, key_live), input_rows, params)
        grad_rows, grad_params = pull_back(cot_rows)
        totals = tuple((total + grad for total, grad in zip(totals, grad_params)))
        return (totals, (result.astype(jnp.bfloat16), grad_rows.astype(jnp.bfloat16)))
    start_totals = tuple((jnp.zeros_like(weight) for weight in params))
    totals, (results, grad_inputs) = lax.scan(block_step, start_totals, (input_blocks, cot_blocks, length_blocks))
    g_wq, g_wk, g_wv, g_bq, g_bv, g_wo, g_bo, g_gone, g_sone, g_wh, g_bh, g_wb, g_bb, g_gtwo, g_stwo = totals
    return (results.reshape(N_DP * group_rows, D), grad_inputs.reshape(N_DP * group_rows, D), g_wq, g_wk, g_wv, g_bq, g_bv, g_wo, g_bo, g_gone, g_sone, g_wh, g_bh, g_wb, g_bb, g_gtwo, g_stwo)
```

```python
import functools

import jax
import jax.numpy as jnp
from jax import lax
from jax.experimental import pallas as pl
from jax.experimental.pallas import tpu as pltpu
from jax.sharding import PartitionSpec as P

HD = 64
LANES = 128
PLANE = 8
CORE, XBIT, YBIT = 1, 2, 4
BF16, F32 = jnp.bfloat16, jnp.float32


def dot_nn(a, b):
    return lax.dot_general(a, b, (((1,), (0,)), ((), ())), preferred_element_type=F32)


def dot_nt(a, b):
    return lax.dot_general(a, b, (((1,), (1,)), ((), ())), preferred_element_type=F32)


def dot_tn(a, b):
    return lax.dot_general(a, b, (((0,), (0,)), ((), ())), preferred_element_type=F32)


def swap(v, axis, bit):
    count = lax.axis_size(axis)
    return lax.ppermute(v, axis, [(i, i ^ bit) for i in range(count)])


def plane_gather(v):
    half = v.shape[1] // 2
    a, b = v[:, :half], v[:, half:]
    a_x, b_y = swap(a, "dp", XBIT), swap(b, "dp", YBIT)
    a2, b2 = jnp.stack([a, a_x]), jnp.stack([b, b_y])
    a_y, b_x = swap(a2, "dp", YBIT), swap(b2, "dp", XBIT)
    four = jnp.stack(
        [
            jnp.concatenate([a, b], axis=1),
            jnp.concatenate([a_x, b_x[0]], axis=1),
            jnp.concatenate([a_y[0], b_y], axis=1),
            jnp.concatenate([a_y[1], b_x[1]], axis=1),
        ]
    )
    return jnp.concatenate([four, swap(four, "dp", CORE)], axis=0)


def shard_gather(slice_of):
    shards = lax.axis_size("tensor")
    others = jnp.stack([swap(slice_of, "tensor", k) for k in range(1, shards)])
    return plane_gather(others)


def plane_reduce(grads):
    shards = lax.axis_size("tensor")
    grads = grads.astype(BF16)
    got = swap(grads[4:], "dp", CORE)
    kept = grads[:4].astype(F32) + got.astype(F32)
    kept = kept.astype(BF16).reshape((2, 2) + grads.shape[1:])
    a, b = kept[:, :, : shards // 2], kept[:, :, shards // 2 :]
    a_got = swap(a[:, 1], "dp", XBIT)
    b_got = swap(b[1], "dp", YBIT)
    a = (a[:, 0].astype(F32) + a_got.astype(F32)).astype(BF16)
    b = (b[0].astype(F32) + b_got.astype(F32)).astype(BF16)
    a_got, b_got = swap(a[1], "dp", YBIT), swap(b[1], "dp", XBIT)
    a = a[0].astype(F32) + a_got.astype(F32)
    b = b[0].astype(F32) + b_got.astype(F32)
    pieces = [a[i] for i in range(shards // 2)] + [b[i] for i in range(shards - shards // 2)]
    total = pieces[0]
    for k in range(1, shards):
        total = total + swap(pieces[k].astype(BF16), "tensor", k).astype(F32)
    step = PLANE
    while step < lax.axis_size("dp"):
        total = total + swap(total, "dp", step)
        step *= 2
    return total


def relative(v, axis, where_me):
    size = v.shape[axis]
    bits = size.bit_length() - 1
    shape = v.shape
    v = v.reshape(shape[:axis] + (2,) * bits + shape[axis + 1 :])
    for b in range(bits):
        on = (where_me >> (bits - 1 - b)) & 1
        v = jnp.where(on == 1, jnp.flip(v, axis + b), v)
    return v.reshape(shape)


def relative_blocks(v, where_me):
    return jnp.stack(
        [lax.dynamic_index_in_dim(v, j ^ where_me, 0, keepdims=False) for j in range(v.shape[0])]
    )


def attend_kernel(length_ref, q_ref, k_ref, v_ref, out_ref, lse_ref, *, half_rows):
    rows, keys = q_ref.shape[0], k_ref.shape[0]
    q, k, v = q_ref[...], k_ref[...], v_ref[...]
    lane = lax.broadcasted_iota(jnp.int32, (rows, LANES), 1)
    spot = lax.broadcasted_iota(jnp.int32, (rows, keys), 1)
    first = length_ref[1]
    spot = jnp.where(spot < half_rows, spot + first, spot - first)
    live = spot < length_ref[0]
    outs, sums = [], []
    for h in range(LANES // HD):
        mine = (lane // HD) == h
        qh = jnp.where(mine, q, jnp.zeros_like(q))
        s = jnp.where(live, dot_nt(qh, k) * 0.125, -1e30)
        top = jnp.max(s, axis=-1, keepdims=True)
        e = jnp.exp(s - top)
        total = jnp.sum(e, axis=-1, keepdims=True)
        p = (e / total).astype(BF16)
        outs.append(dot_nn(p, v))
        sums.append(jnp.broadcast_to(top + jnp.log(total), (rows, LANES)))
    low_half = lane < HD
    out_ref[...] = jnp.where(low_half, outs[0], outs[1]).astype(BF16)
    lse_ref[...] = jnp.where(low_half, sums[0], sums[1])


def attend_back_kernel(
    length_ref, q_ref, k_ref, v_ref, lse_ref, do_ref, dq_ref, dk_ref, dv_ref, *, half_rows
):
    rows, keys = q_ref.shape[0], k_ref.shape[0]
    q, k, v, do = q_ref[...], k_ref[...], v_ref[...], do_ref[...]
    lane = lax.broadcasted_iota(jnp.int32, (rows, LANES), 1)
    key_lane = lax.broadcasted_iota(jnp.int32, (keys, LANES), 1)
    spot = lax.broadcasted_iota(jnp.int32, (rows, keys), 1)
    first = length_ref[1]
    spot = jnp.where(spot < half_rows, spot + first, spot - first)
    live = spot < length_ref[0]
    dqs, dks, dvs = [], [], []
    for h in range(LANES // HD):
        mine = (lane // HD) == h
        qh = jnp.where(mine, q, jnp.zeros_like(q))
        doh = jnp.where(mine, do, jnp.zeros_like(do))
        s = jnp.where(live, dot_nt(qh, k) * 0.125, -1e30)
        p = jnp.exp(s - lse_ref[:, h * HD : h * HD + 1])
        dp = dot_nt(doh, v)
        inner = jnp.sum(p * dp, axis=-1, keepdims=True)
        ds = (p * (dp - inner)).astype(BF16)
        dqs.append(dot_nn(ds, k))
        dks.append(dot_tn(ds, q))
        dvs.append(dot_tn(p.astype(BF16), do))
    low_half, key_low = lane < HD, key_lane < HD
    dq_ref[...] = (jnp.where(low_half, dqs[0], dqs[1]) * 0.125).astype(BF16)
    dk_ref[...] = (jnp.where(key_low, dks[0], dks[1]) * 0.125).astype(BF16)
    dv_ref[...] = jnp.where(key_low, dvs[0], dvs[1]).astype(BF16)


def attend(place, q, k, v):
    rows, width = q.shape
    keys = k.shape[0]
    q_spec = pl.BlockSpec((rows, LANES), lambda i: (0, i))
    k_spec = pl.BlockSpec((keys, LANES), lambda i: (0, i))
    return pl.pallas_call(
        functools.partial(attend_kernel, half_rows=rows),
        grid=(width // LANES,),
        in_specs=[pl.BlockSpec(memory_space=pltpu.SMEM), q_spec, k_spec, k_spec],
        out_specs=[q_spec, q_spec],
        out_shape=[
            jax.ShapeDtypeStruct((rows, width), BF16),
            jax.ShapeDtypeStruct((rows, width), F32),
        ],
        compiler_params=pltpu.CompilerParams(vmem_limit_bytes=32 * 1024 * 1024),
        cost_estimate=pl.CostEstimate(
            flops=4 * rows * keys * width, bytes_accessed=8 * rows * width, transcendentals=0
        ),
    )(place, q, k, v)


def attend_back(place, q, k, v, lse, do):
    rows, width = q.shape
    keys = k.shape[0]
    q_spec = pl.BlockSpec((rows, LANES), lambda i: (0, i))
    k_spec = pl.BlockSpec((keys, LANES), lambda i: (0, i))
    return pl.pallas_call(
        functools.partial(attend_back_kernel, half_rows=rows),
        grid=(width // LANES,),
        in_specs=[
            pl.BlockSpec(memory_space=pltpu.SMEM),
            q_spec,
            k_spec,
            k_spec,
            q_spec,
            q_spec,
        ],
        out_specs=[q_spec, k_spec, k_spec],
        out_shape=[
            jax.ShapeDtypeStruct((rows, width), BF16),
            jax.ShapeDtypeStruct((keys, width), BF16),
            jax.ShapeDtypeStruct((keys, width), BF16),
        ],
        compiler_params=pltpu.CompilerParams(vmem_limit_bytes=32 * 1024 * 1024),
        cost_estimate=pl.CostEstimate(
            flops=10 * rows * keys * width, bytes_accessed=16 * rows * width, transcendentals=0
        ),
    )(place, q, k, v, lse, do)


def layer_norm(rows_in, scales, offset):
    center = rows_in - jnp.mean(rows_in, axis=-1, keepdims=True)
    spread = jnp.mean(center * center, axis=-1, keepdims=True)
    return center * lax.rsqrt(spread + 1e-05) * scales + offset


def gelu_pair(v):
    cdf = 0.5 * (1.0 + lax.erf(v * (0.5**0.5)))
    density = jnp.exp(-0.5 * v * v) * 0.3989422804014327
    return v * cdf, cdf + v * density


def local(
    inputs,
    cotangent,
    lengths,
    w_query,
    w_key,
    w_value,
    b_query,
    b_value,
    w_output,
    b_output,
    gain_one,
    shift_one,
    w_hidden,
    b_hidden,
    w_back,
    b_back,
    gain_two,
    shift_two,
):
    rows, width = inputs.shape
    shards = lax.axis_size("tensor")
    head_cols = w_query.shape[1]
    hidden = w_hidden.shape[1]
    heads = head_cols // HD
    part = HD // PLANE
    att_rows = 4 * heads * part
    ffn_rows = hidden // PLANE
    per_slot = shards // lengths.shape[0]
    assert per_slot == 2 and shards == 4 and lax.axis_size("dp") % PLANE == 0
    dp = lax.axis_index("dp")
    me = ((dp & 1) << 2) | (((dp >> 2) & 1) << 1) | ((dp >> 1) & 1)
    t = lax.axis_index("tensor")

    att_i = (
        jnp.stack([w_query.T, w_key.T, w_value.T, w_output])
        .reshape(4, heads, PLANE, part, width)
        .transpose(2, 0, 1, 3, 4)
        .reshape(PLANE, att_rows, width)
    )
    hid_i = w_hidden.T.reshape(PLANE, ffn_rows, width)
    back_i = w_back.reshape(PLANE, ffn_rows, width)
    att_own = lax.dynamic_index_in_dim(att_i, me, 0, keepdims=False)
    hid_own = lax.dynamic_index_in_dim(hid_i, me, 0, keepdims=False)
    back_own = lax.dynamic_index_in_dim(back_i, me, 0, keepdims=False)

    rows_other = swap(inputs, "tensor", 1)
    att_far = shard_gather(att_own)
    biases = jnp.concatenate([b_query, b_value, b_hidden])
    biases = jnp.stack([biases] + [swap(biases, "tensor", k) for k in range(1, shards)])
    hid_far = shard_gather(hid_own)
    back_far = shard_gather(back_own)

    att_all = jnp.concatenate([relative_blocks(att_i, me)[:, None], att_far], axis=1)
    att_all = (
        att_all.reshape(PLANE, shards, 4, heads, part, width)
        .transpose(2, 1, 3, 0, 4, 5)
        .reshape(4, shards * head_cols, width)
    )
    wq, wk, wv, wo = att_all[0], att_all[1], att_all[2], att_all[3]
    bq = relative(biases[:, :head_cols].reshape(shards * heads, PLANE, part), 1, me).reshape(-1)
    bv = relative(
        biases[:, head_cols : 2 * head_cols].reshape(shards * heads, PLANE, part), 1, me
    ).reshape(-1)
    bh = (
        relative(biases[:, 2 * head_cols :].reshape(shards, PLANE, ffn_rows), 1, me)
        .transpose(1, 0, 2)
        .reshape(-1)
    )

    both = jnp.concatenate([inputs, rows_other], axis=0)
    queries = (dot_nt(inputs, wq) + bq).astype(BF16)
    key_rows = dot_nt(both, wk).astype(BF16)
    values = (dot_nt(both, wv) + bv).astype(BF16)
    place = jnp.stack([lengths[t // per_slot], (t % per_slot) * rows]).astype(jnp.int32)
    context, logsum = attend(place, queries, key_rows, values)
    first_sum = dot_nn(context, wo) + b_output + inputs.astype(F32)
    mid_full, norm_one_pull = jax.vjp(layer_norm, first_sum, gain_one, shift_one)
    mid = mid_full.astype(BF16)
    w_hid = jnp.concatenate([relative_blocks(hid_i, me)[:, None], hid_far], axis=1)
    w_hid = w_hid.reshape(shards * hidden, width)
    w_bak = jnp.concatenate([relative_blocks(back_i, me)[:, None], back_far], axis=1)
    w_bak = w_bak.reshape(shards * hidden, width)
    act, slope = gelu_pair(dot_nt(mid, w_hid) + bh)
    act, slope = act.astype(BF16), slope.astype(BF16)
    second_sum = dot_nn(act, w_bak) + b_back + mid.astype(F32)
    outputs, norm_two_pull = jax.vjp(layer_norm, second_sum, gain_two, shift_two)

    grad_second, grad_gain_two, grad_shift_two = norm_two_pull(cotangent.astype(F32))
    grad_branch = grad_second.astype(BF16)
    grad_b_back = jnp.sum(grad_branch, axis=0, dtype=F32)
    grad_w_back = dot_tn(act, grad_branch)
    grad_pre = (dot_nt(grad_branch, w_bak) * slope.astype(F32)).astype(BF16)
    grad_b_hidden = jnp.sum(grad_pre, axis=0, dtype=F32)
    grad_w_hidden = dot_tn(grad_pre, mid)
    grad_mid = dot_nn(grad_pre, w_hid) + grad_second
    grad_first, grad_gain_one, grad_shift_one = norm_one_pull(grad_mid)
    grad_attn = grad_first.astype(BF16)
    grad_b_output = jnp.sum(grad_attn, axis=0, dtype=F32)
    grad_w_output = dot_tn(context, grad_attn)
    grad_context = dot_nt(grad_attn, wo).astype(BF16)
    grad_queries, grad_keys, grad_values = attend_back(
        place, queries, key_rows, values, logsum, grad_context
    )
    grad_b_query = jnp.sum(grad_queries, axis=0, dtype=F32)
    grad_b_value = jnp.sum(grad_values, axis=0, dtype=F32)
    grad_w_query = dot_tn(grad_queries, inputs)
    grad_w_key = dot_tn(grad_keys, both)
    grad_w_value = dot_tn(grad_values, both)
    total = dot_nn(grad_keys, wk) + dot_nn(grad_values, wv)
    returned = swap(total[rows:].astype(BF16), "tensor", 1).astype(F32)
    input_grad = (total[:rows] + dot_nn(grad_queries, wq) + returned + grad_first).astype(BF16)

    back_sum = plane_reduce(grad_w_back.reshape(PLANE, shards, ffn_rows, width))
    hid_sum = plane_reduce(grad_w_hidden.reshape(PLANE, shards, ffn_rows, width))
    att_grad = jnp.stack([grad_w_query, grad_w_key, grad_w_value, grad_w_output])
    att_grad = (
        att_grad.reshape(4, shards, heads, PLANE, part, width)
        .transpose(3, 1, 0, 2, 4, 5)
        .reshape(PLANE, shards, att_rows, width)
    )
    att_sum = plane_reduce(att_grad)

    def spread(total_slice):
        return relative_blocks(plane_gather(total_slice.astype(BF16)[None])[:, 0], me)

    back_out = spread(back_sum).reshape(hidden, width).astype(F32)
    hid_out = spread(hid_sum).reshape(hidden, width).T.astype(F32)
    att_out = (
        spread(att_sum)
        .reshape(PLANE, 4, heads, part, width)
        .transpose(1, 2, 0, 3, 4)
        .reshape(4, head_cols, width)
    )

    def absolute_heads(v):
        return relative(relative(v.reshape(shards, heads, PLANE, part), 2, me), 0, t).reshape(-1)

    small = jnp.concatenate(
        [
            absolute_heads(grad_b_query),
            absolute_heads(grad_b_value),
            relative(
                relative(grad_b_hidden.reshape(PLANE, shards, ffn_rows), 0, me), 1, t
            )
            .transpose(1, 0, 2)
            .reshape(-1),
            grad_b_output,
            grad_gain_one,
            grad_shift_one,
            grad_b_back,
            grad_gain_two,
            grad_shift_two,
        ]
    ).reshape(-1, LANES)
    for axis in ("dp", "tensor"):
        step = 1
        while step < lax.axis_size(axis):
            small = small + swap(small, axis, step)
            step *= 2
    small = small.reshape(-1)
    wide = shards * head_cols
    grad_b_query = lax.dynamic_slice_in_dim(small, t * head_cols, head_cols)
    grad_b_value = lax.dynamic_slice_in_dim(small, wide + t * head_cols, head_cols)
    grad_b_hidden = lax.dynamic_slice_in_dim(small, 2 * wide + t * hidden, hidden)
    rest = small[2 * wide + shards * hidden :].reshape(6, width)
    return (
        outputs.astype(BF16),
        input_grad,
        att_out[0].T.astype(F32),
        att_out[1].T.astype(F32),
        att_out[2].T.astype(F32),
        grad_b_query,
        grad_b_value,
        att_out[3].astype(F32),
        rest[0],
        rest[1],
        rest[2],
        hid_out,
        grad_b_hidden,
        back_out,
        rest[3],
        rest[4],
        rest[5],
    )


def solution(mesh):
    rows = P(("dp", "tensor"), None)
    columns, depth, vector = P(None, "tensor"), P("tensor", None), P("tensor")
    return jax.shard_map(
        local,
        mesh=mesh,
        in_specs=(
            rows,
            rows,
            P("dp"),
            columns,
            columns,
            columns,
            vector,
            vector,
            depth,
            P(),
            P(),
            P(),
            columns,
            vector,
            depth,
            P(),
            P(),
            P(),
        ),
        out_specs=(
            rows,
            rows,
            columns,
            columns,
            columns,
            vector,
            vector,
            depth,
            P(),
            P(),
            P(),
            columns,
            vector,
            depth,
            P(),
            P(),
            P(),
        ),
        check_vma=False,
    )
```

```python
import functools

import jax
import jax.numpy as jnp
from jax import lax
from jax.experimental import pallas as pl
from jax.experimental.pallas import tpu as pltpu
from jax.sharding import PartitionSpec as P

HD = 64
LANES = 128
PLANE = 8
CORE, XBIT, YBIT = 1, 2, 4
BF16, F32 = jnp.bfloat16, jnp.float32


def dot_nn(a, b):
    return lax.dot_general(a, b, (((1,), (0,)), ((), ())), preferred_element_type=F32)


def dot_nt(a, b):
    return lax.dot_general(a, b, (((1,), (1,)), ((), ())), preferred_element_type=F32)


def dot_tn(a, b):
    return lax.dot_general(a, b, (((0,), (0,)), ((), ())), preferred_element_type=F32)


def swap(v, axis, bit):
    count = lax.axis_size(axis)
    return lax.ppermute(v, axis, [(i, i ^ bit) for i in range(count)])


def pack_kernel(moves, count, place_ref, *refs):
    out_ref, sem = refs[-2], refs[-1]
    core, chip = place_ref[0], place_ref[1]
    copies = []
    for k, (which, source, target) in enumerate(moves):
        src = refs[which].at[source(core, chip)]
        dst = out_ref.at[target]
        copies.append(pltpu.make_async_copy(src, dst, sem.at[k]))
    for copy in copies:
        copy.start()
    for copy in copies:
        copy.wait()


def pack(where, shape, moves, arrays, earlier=()):
    space = pl.BlockSpec(memory_space=pl.ANY)
    return pl.pallas_call(
        functools.partial(pack_kernel, moves, len(arrays)),
        in_specs=[pl.BlockSpec(memory_space=pltpu.SMEM)] + [space] * (len(arrays) + len(earlier)),
        out_specs=pl.BlockSpec(memory_space=pltpu.VMEM),
        out_shape=jax.ShapeDtypeStruct(shape, BF16),
        scratch_shapes=[pltpu.SemaphoreType.DMA((len(moves),))],
        compiler_params=pltpu.CompilerParams(vmem_limit_bytes=16 * 1024 * 1024),
    )(where, *arrays, *earlier)


def at(*index):
    return lambda core, chip: index


def stacked(where, arrays, rows, earlier=()):
    top = pl.ds(0, rows)
    moves = [(i, at(top), (i,)) for i in range(len(arrays))]
    return pack(where, (len(arrays), rows) + arrays[0].shape[1:], moves, arrays, earlier)


def from_shards(v):
    return [swap(v, "tensor", k) for k in range(1, lax.axis_size("tensor"))]


def halves_from_chips(where, v, between=()):
    v_x, v_y = swap(v, "dp", XBIT), swap(v, "dp", YBIT)
    half = v.shape[1] // 2
    low, high = (slice(None), pl.ds(0, half)), (slice(None), pl.ds(half, half))
    shape = (v.shape[0], half) + v.shape[2:]
    v_xy = swap(pack(where, shape, [(0, at(*low), ())], [v_x], between), "dp", YBIT)
    v_yx = swap(pack(where, shape, [(0, at(*high), ())], [v_y], between), "dp", XBIT)
    return [v, v_x, v_y, v_xy, v_yx]


def from_chips(v):
    return [v] + [swap(v, "dp", bits) for bits in (XBIT, YBIT, XBIT | YBIT)]


def add(a, b):
    return (a.astype(F32) + b.astype(F32)).astype(BF16)


def shards_reduce(pieces):
    total = pieces[0].astype(F32)
    for k in range(1, len(pieces)):
        total = total + swap(pieces[k], "tensor", k).astype(F32)
    step = PLANE
    while step < lax.axis_size("dp"):
        total = total + swap(total, "dp", step)
        step *= 2
    return total.astype(BF16)


def relative(v, axis, where_me):
    size = v.shape[axis]
    bits = size.bit_length() - 1
    shape = v.shape
    v = v.reshape(shape[:axis] + (2,) * bits + shape[axis + 1 :])
    for b in range(bits):
        on = (where_me >> (bits - 1 - b)) & 1
        v = jnp.where(on == 1, jnp.flip(v, axis + b), v)
    return v.reshape(shape)


def qkv_kernel(
    place_ref, own, other, x_ref, xo_ref, bq_ref, bv_ref, q_ref, k_ref, v_ref, *refs
):
    weights, sem = refs[:4], refs[4]
    core = place_ref[0]
    rows, width = x_ref.shape

    def copies(src, group):
        return [
            pltpu.make_async_copy(
                src.at[j, :, m], weights[2 * group + m].at[:, :, j], sem.at[group, m, j]
            )
            for m in range(2)
            for j in range(4)
        ]

    for group in (0, 1):

        @pl.when(core == group)
        def _():
            for copy in copies(own, group):
                copy.start()

        @pl.when(core != group)
        def _():
            for copy in copies(other, group):
                copy.start()

    def landed(group):
        @pl.when(core == group)
        def _():
            for copy in copies(own, group):
                copy.wait()

        @pl.when(core != group)
        def _():
            for copy in copies(other, group):
                copy.wait()

    landed(0)
    x, xo = x_ref[...], xo_ref[...]
    q_ref[...] = (dot_nt(x, weights[0][...].reshape(width, width)) + bq_ref[...]).astype(BF16)
    w = weights[1][...].reshape(width, width)
    k_ref[:rows] = dot_nt(x, w).astype(BF16)
    k_ref[rows:] = dot_nt(xo, w).astype(BF16)
    landed(1)
    w = weights[2][...].reshape(width, width)
    v_ref[:rows] = (dot_nt(x, w) + bv_ref[...]).astype(BF16)
    v_ref[rows:] = (dot_nt(xo, w) + bv_ref[...]).astype(BF16)


def project(where, own, other, x, xo, bq, bv):
    rows, width = x.shape
    _, shards, _, heads, part, _ = own.shape
    vmem = pl.BlockSpec(memory_space=pltpu.VMEM)
    space = pl.BlockSpec(memory_space=pl.ANY)
    weight = jax.ShapeDtypeStruct((shards, heads, 4, part, width), BF16)
    return pl.pallas_call(
        qkv_kernel,
        in_specs=[pl.BlockSpec(memory_space=pltpu.SMEM), space, space] + [vmem] * 4,
        out_specs=[vmem] * 7,
        out_shape=[
            jax.ShapeDtypeStruct((rows, width), BF16),
            jax.ShapeDtypeStruct((2 * rows, width), BF16),
            jax.ShapeDtypeStruct((2 * rows, width), BF16),
        ]
        + [weight] * 4,
        scratch_shapes=[pltpu.SemaphoreType.DMA((2, 2, 4))],
        compiler_params=pltpu.CompilerParams(vmem_limit_bytes=40 * 1024 * 1024),
        cost_estimate=pl.CostEstimate(flops=4 * 10**9, bytes_accessed=10**7, transcendentals=0),
    )(where, own, other, x, xo, bq, bv)


def att_out_kernel(place_ref, own_ref, other_ref, gq_ref, gk_ref, gv_ref, go_ref, extra_ref):
    core, chip = place_ref[0], place_ref[1]
    head_cols, width = go_ref.shape
    heads, part = head_cols // HD, HD // 4
    rows = own_ref.shape[1]
    for group in (0, 1):
        blocks = []
        for c in range(4):
            block = jnp.where(core == group, own_ref[c ^ chip], other_ref[c ^ chip])
            spot = (group * 4 + c) * rows
            extra_ref[spot : spot + rows] = block[:, width:].astype(F32)
            blocks.append(block[:, :width])
        for m in range(2):
            pieces = [
                blocks[c][(m * heads + h) * part : (m * heads + h + 1) * part]
                for h in range(heads)
                for c in range(4)
            ]
            whole = jnp.concatenate(pieces, axis=0).astype(F32)
            if group == 1 and m == 1:
                go_ref[...] = whole
            else:
                (gq_ref, gk_ref, gv_ref)[2 * group + m][...] = whole.T


def att_outputs(where, own, other, head_cols, width):
    vmem = pl.BlockSpec(memory_space=pltpu.VMEM)
    turned = jax.ShapeDtypeStruct((width, head_cols), F32)
    return pl.pallas_call(
        att_out_kernel,
        in_specs=[pl.BlockSpec(memory_space=pltpu.SMEM), vmem, vmem],
        out_specs=[vmem] * 5,
        out_shape=[
            turned,
            turned,
            turned,
            jax.ShapeDtypeStruct((head_cols, width), F32),
            jax.ShapeDtypeStruct((2 * 4 * own.shape[1], own.shape[2] - width), F32),
        ],
        compiler_params=pltpu.CompilerParams(vmem_limit_bytes=32 * 1024 * 1024),
    )(where, own, other)


def ffn_out_kernel(place_ref, own_ref, other_ref, back_ref, hid_ref):
    core, chip = place_ref[0], place_ref[1]
    rows = own_ref.shape[2]
    blocks = []
    for group in (0, 1):
        for c in range(4):
            block = jnp.where(core == group, own_ref[c ^ chip], other_ref[c ^ chip])
            spot = (group * 4 + c) * rows
            back_ref[spot : spot + rows] = block[0].astype(F32)
            blocks.append(block[1])
    hid_ref[...] = jnp.concatenate(blocks, axis=0).astype(F32).T


def ffn_outputs(where, own, other, hidden, width):
    vmem = pl.BlockSpec(memory_space=pltpu.VMEM)
    return pl.pallas_call(
        ffn_out_kernel,
        in_specs=[pl.BlockSpec(memory_space=pltpu.SMEM), vmem, vmem],
        out_specs=[vmem] * 2,
        out_shape=[
            jax.ShapeDtypeStruct((hidden, width), F32),
            jax.ShapeDtypeStruct((width, hidden), F32),
        ],
        compiler_params=pltpu.CompilerParams(vmem_limit_bytes=32 * 1024 * 1024),
    )(where, own, other)


def live_keys(place_ref, keys, half_rows):
    spot = lax.broadcasted_iota(jnp.int32, (keys, 1), 0)
    first = place_ref[1]
    spot = jnp.where(spot < half_rows, spot + first, spot - first)
    return spot < place_ref[0]


def attend_kernel(place_ref, q_ref, k_ref, v_ref, _, out_ref, lse_ref, *, half_rows):
    rows, keys = q_ref.shape[0], k_ref.shape[0]
    q = q_ref[...] * jnp.asarray(0.125, BF16)
    k = k_ref[...]
    v_turned = v_ref[...].T
    live = live_keys(place_ref, keys, half_rows)
    lane = lax.broadcasted_iota(jnp.int32, (rows, LANES), 1)
    outs, sums = [], []
    for h in range(LANES // HD):
        qh = jnp.where((lane // HD) == h, q, jnp.zeros_like(q))
        s = jnp.where(live, dot_nt(k, qh), -1e30)
        top = jnp.max(s, axis=0, keepdims=True)
        e = jnp.exp(s - top)
        total = jnp.sum(e, axis=0, keepdims=True)
        p = (e * (1.0 / total)).astype(BF16)
        outs.append(dot_nn(v_turned, p)[h * HD : (h + 1) * HD])
        sums.append(top + jnp.log(total))
    out_ref[...] = jnp.concatenate(outs, axis=0).T.astype(BF16)
    lse_ref[...] = jnp.concatenate(sums + [jnp.zeros((6, rows), F32)], axis=0)


def attend_back_kernel(
    place_ref, q_ref, k_ref, v_ref, lse_ref, do_ref, _, dq_ref, dk_ref, dv_ref, *, half_rows
):
    rows, keys = q_ref.shape[0], k_ref.shape[0]
    k, v, do = k_ref[...], v_ref[...], do_ref[...]
    q = q_ref[...] * jnp.asarray(0.125, BF16)
    k_turned = k.T
    live = live_keys(place_ref, keys, half_rows)
    lane = lax.broadcasted_iota(jnp.int32, (rows, LANES), 1)
    dqs, dks, dvs = [], [], []
    for h in range(LANES // HD):
        mine = (lane // HD) == h
        qh = jnp.where(mine, q, jnp.zeros_like(q))
        doh = jnp.where(mine, do, jnp.zeros_like(do))
        s = jnp.where(live, dot_nt(k, qh), -1e30)
        p = jnp.exp(s - lse_ref[h : h + 1, :])
        dp = dot_nt(v, doh)
        inner = jnp.sum(p * dp, axis=0, keepdims=True)
        ds = (p * (dp - inner)).astype(BF16)
        dqs.append(dot_nn(k_turned, ds)[h * HD : (h + 1) * HD])
        dks.append(dot_nn(ds, qh))
        dvs.append(dot_nn(p.astype(BF16), doh))
    dq_ref[...] = (jnp.concatenate(dqs, axis=0).T * 0.125).astype(BF16)
    dk_ref[...] = (dks[0] + dks[1]).astype(BF16)
    dv_ref[...] = (dvs[0] + dvs[1]).astype(BF16)


def attend(place, q, k, v, earlier):
    rows, width = q.shape
    keys = k.shape[0]
    q_spec = pl.BlockSpec((rows, LANES), lambda i: (0, i))
    k_spec = pl.BlockSpec((keys, LANES), lambda i: (0, i))
    lse_spec = pl.BlockSpec((8, rows), lambda i: (i, 0))
    pairs = width // LANES
    return pl.pallas_call(
        functools.partial(attend_kernel, half_rows=rows),
        grid=(pairs,),
        in_specs=[
            pl.BlockSpec(memory_space=pltpu.SMEM),
            q_spec,
            k_spec,
            k_spec,
            pl.BlockSpec(memory_space=pl.ANY),
        ],
        out_specs=[q_spec, lse_spec],
        out_shape=[
            jax.ShapeDtypeStruct((rows, width), BF16),
            jax.ShapeDtypeStruct((8 * pairs, rows), F32),
        ],
        compiler_params=pltpu.CompilerParams(vmem_limit_bytes=32 * 1024 * 1024),
        cost_estimate=pl.CostEstimate(
            flops=70 * rows * keys * width, bytes_accessed=8 * rows * width, transcendentals=0
        ),
    )(place, q, k, v, earlier)


def attend_back(place, q, k, v, lse, do, earlier):
    rows, width = q.shape
    keys = k.shape[0]
    q_spec = pl.BlockSpec((rows, LANES), lambda i: (0, i))
    k_spec = pl.BlockSpec((keys, LANES), lambda i: (0, i))
    lse_spec = pl.BlockSpec((8, rows), lambda i: (i, 0))
    return pl.pallas_call(
        functools.partial(attend_back_kernel, half_rows=rows),
        grid=(width // LANES,),
        in_specs=[
            pl.BlockSpec(memory_space=pltpu.SMEM),
            q_spec,
            k_spec,
            k_spec,
            lse_spec,
            q_spec,
            pl.BlockSpec(memory_space=pl.ANY),
        ],
        out_specs=[q_spec, k_spec, k_spec],
        out_shape=[
            jax.ShapeDtypeStruct((rows, width), BF16),
            jax.ShapeDtypeStruct((keys, width), BF16),
            jax.ShapeDtypeStruct((keys, width), BF16),
        ],
        compiler_params=pltpu.CompilerParams(vmem_limit_bytes=32 * 1024 * 1024),
        cost_estimate=pl.CostEstimate(
            flops=90 * rows * keys * width, bytes_accessed=16 * rows * width, transcendentals=0
        ),
    )(place, q, k, v, lse, do, earlier)


def weights_kernel(
    core_ref,
    dq_ref,
    dk_ref,
    dv_ref,
    context_ref,
    ga_ref,
    x_ref,
    xo_ref,
    extra_ref,
    keep_ref,
    send_ref,
):
    rows, width = dq_ref.shape
    shards = keep_ref.shape[1]
    group = width // shards
    heads = group // HD
    part = HD // 4
    core = core_ref[0]
    span = 2 * group
    lane = lax.broadcasted_iota(jnp.int32, (part, LANES), 1)
    spots = lax.broadcasted_iota(jnp.int32, (8, LANES), 0)
    spots = (spots == lax.broadcasted_iota(jnp.int32, (8, LANES), 1)).astype(BF16)
    extra_all = dot_tn(extra_ref[...], spots)
    att_rows = keep_ref.shape[2]

    def put(which, m, left_ref, rights, with_sum):
        ones = jnp.ones((rows, LANES), BF16)
        for first in range(0, width, span):
            out, sums = None, None
            for k, right in enumerate(rights):
                left = left_ref[k * rows : (k + 1) * rows, first : first + span]
                more = dot_tn(left, right[...])
                out = more if out is None else out + more
                if with_sum:
                    more = dot_tn(left, ones)
                    sums = more if sums is None else sums + more

            def store(dst, base):
                for at in range(0, span, part):
                    row = first + at
                    shard, rest = row // group, row % group
                    head, j = rest // HD, (rest % HD) // part
                    spot = (m * heads + head) * part
                    dst[j, shard, spot : spot + part, :width] = out[at : at + part].astype(BF16)
                    line = base + (j * shards + shard) * att_rows + spot
                    tail = extra_all[line : line + part]
                    if with_sum:
                        tail = jnp.where(lane == 0, sums[at : at + part], tail)
                    dst[j, shard, spot : spot + part, width:] = tail.astype(BF16)

            @pl.when(core == which)
            def _():
                store(keep_ref, 0)

            @pl.when(core != which)
            def _():
                store(send_ref, 4 * shards * att_rows)

    put(0, 0, dq_ref, [x_ref], True)
    put(0, 1, dk_ref, [x_ref, xo_ref], False)
    put(1, 0, dv_ref, [x_ref, xo_ref], True)
    put(1, 1, context_ref, [ga_ref], False)


def attention_weight_grads(core, dq, dk, dv, context, ga, x, xo, extra, shards):
    width = dq.shape[1]
    full = jax.ShapeDtypeStruct((4, shards, width // (2 * shards), width + LANES), BF16)
    vmem = pl.BlockSpec(memory_space=pltpu.VMEM)
    return pl.pallas_call(
        weights_kernel,
        in_specs=[pl.BlockSpec(memory_space=pltpu.SMEM)] + [vmem] * 8,
        out_specs=[vmem, vmem],
        out_shape=[full, full],
        compiler_params=pltpu.CompilerParams(vmem_limit_bytes=40 * 1024 * 1024),
        cost_estimate=pl.CostEstimate(
            flops=6 * 10**9, bytes_accessed=12 * 10**6, transcendentals=0
        ),
    )(core, dq, dk, dv, context, ga, x, xo, extra)


def whole_call(kernel, outs, args, flops):
    vmem = pl.BlockSpec(memory_space=pltpu.VMEM)
    return pl.pallas_call(
        kernel,
        in_specs=[vmem] * len(args),
        out_specs=[vmem] * len(outs),
        out_shape=[jax.ShapeDtypeStruct(shape, dtype) for shape, dtype in outs],
        compiler_params=pltpu.CompilerParams(vmem_limit_bytes=48 * 1024 * 1024),
        cost_estimate=pl.CostEstimate(flops=flops, bytes_accessed=10**6, transcendentals=0),
    )(*args)


def normalize(z):
    center = z - jnp.mean(z, axis=-1, keepdims=True)
    spread = jnp.mean(center * center, axis=-1, keepdims=True)
    scale = lax.rsqrt(spread + 1e-05)
    return center * scale, scale


def norm_back(grad, zhat, scale, gain):
    e = grad * gain
    inner = jnp.mean(e * zhat, axis=-1, keepdims=True)
    return (e - jnp.mean(e, axis=-1, keepdims=True) - zhat * inner) * scale


def column_sums(v):
    return jnp.sum(v, axis=0, keepdims=True)


def mid_kernel(context_ref, wo_ref, x_ref, b_ref, gain_ref, shift_ref, mid_ref, zhat_ref, scale_ref):
    z = dot_nn(context_ref[...], wo_ref[...]) + b_ref[...] + x_ref[...].astype(F32)
    zhat, scale = normalize(z)
    mid_ref[...] = (zhat * gain_ref[...] + shift_ref[...]).astype(BF16)
    zhat_ref[...] = zhat
    scale_ref[...] = jnp.broadcast_to(scale, scale_ref.shape)


def hidden_kernel(mid_ref, w_ref, b_ref, act_ref, slope_ref):
    block = 512
    for first in range(0, w_ref.shape[0], block):
        cols = slice(first, first + block)
        act, slope = gelu_pair(dot_nt(mid_ref[...], w_ref[cols]) + b_ref[:, cols])
        act_ref[:, cols] = act.astype(BF16)
        slope_ref[:, cols] = slope.astype(BF16)


def branch_kernel(
    act_own_ref,
    act_other_ref,
    w_own_ref,
    w_other_ref,
    mid_ref,
    b_ref,
    gain_ref,
    shift_ref,
    cotangent_ref,
    out_ref,
    grad_ref,
    low_ref,
    sums_ref,
):
    z = dot_nn(act_own_ref[...], w_own_ref[...]) + dot_nn(act_other_ref[...], w_other_ref[...])
    zhat, scale = normalize(z + b_ref[...] + mid_ref[...].astype(F32))
    out_ref[...] = (zhat * gain_ref[...] + shift_ref[...]).astype(BF16)
    c = cotangent_ref[...].astype(F32)
    grad = norm_back(c, zhat, scale, gain_ref[...])
    low = grad.astype(BF16)
    grad_ref[...] = grad
    low_ref[...] = low
    sums_ref[...] = jnp.concatenate(
        [column_sums(low.astype(F32)), column_sums(c * zhat), column_sums(c)], axis=0
    )


def pair_grads_kernel(left_own_ref, left_other_ref, right_ref, keep_ref, send_ref):
    send_ref[...] = dot_tn(left_other_ref[...], right_ref[...]).astype(BF16)
    keep_ref[...] = dot_tn(left_own_ref[...], right_ref[...]).astype(BF16)


def pre_kernel(
    low_ref, w_own_ref, w_other_ref, slope_own_ref, slope_other_ref, own_ref, other_ref, sums_ref
):
    half = own_ref.shape[1]
    for k, (w, slope, out) in enumerate(
        ((w_own_ref, slope_own_ref, own_ref), (w_other_ref, slope_other_ref, other_ref))
    ):
        grad = (dot_nt(low_ref[...], w[...]) * slope[...].astype(F32)).astype(BF16)
        out[...] = grad
        sums_ref[:, k * half : (k + 1) * half] = column_sums(grad.astype(F32))


def first_kernel(
    pre_own_ref,
    pre_other_ref,
    w_own_ref,
    w_other_ref,
    grad_ref,
    zhat_ref,
    scale_ref,
    gain_ref,
    wo_ref,
    first_ref,
    low_ref,
    context_ref,
    sums_ref,
):
    grad = dot_nn(pre_own_ref[...], w_own_ref[...]) + dot_nn(pre_other_ref[...], w_other_ref[...])
    grad = grad + grad_ref[...]
    zhat = zhat_ref[...]
    first = norm_back(grad, zhat, scale_ref[:, :1], gain_ref[...])
    low = first.astype(BF16)
    first_ref[...] = first
    low_ref[...] = low
    context_ref[...] = dot_nt(low, wo_ref[...]).astype(BF16)
    sums_ref[...] = jnp.concatenate(
        [column_sums(low.astype(F32)), column_sums(grad * zhat), column_sums(grad)], axis=0
    )


def gelu_pair(v):
    cdf = 0.5 * (1.0 + lax.erf(v * (0.5**0.5)))
    density = jnp.exp(-0.5 * v * v) * 0.3989422804014327
    return v * cdf, cdf + v * density


def local(
    inputs,
    cotangent,
    lengths,
    w_query,
    w_key,
    w_value,
    b_query,
    b_value,
    w_output,
    b_output,
    gain_one,
    shift_one,
    w_hidden,
    b_hidden,
    w_back,
    b_back,
    gain_two,
    shift_two,
):
    rows, width = inputs.shape
    shards = lax.axis_size("tensor")
    head_cols = w_query.shape[1]
    hidden = w_hidden.shape[1]
    heads = head_cols // HD
    part = HD // 4
    ffn_rows = hidden // PLANE
    per_slot = shards // lengths.shape[0]
    assert per_slot == 2 and shards == 4 and lax.axis_size("dp") % PLANE == 0
    dp = lax.axis_index("dp")
    core = dp & 1
    chip = (((dp >> 2) & 1) << 1) | ((dp >> 1) & 1)
    me = core * 4 + chip
    t = lax.axis_index("tensor")

    where = jnp.stack([core, chip]).astype(jnp.int32)
    att_rows = 2 * heads * part
    far = pl.ds(1, shards - 1)

    by_head = (heads, 4, part, width)
    pair = [
        jnp.where(core == 0, w_query, w_value).T.reshape(by_head),
        jnp.where(core == 0, w_key.T, w_output).reshape(by_head),
    ]
    hid_near = lax.dynamic_slice_in_dim(w_hidden, core * (hidden // 2), hidden // 2, 1)
    hid_near = hid_near.T.reshape(4, ffn_rows, width)
    back_near = w_back.reshape(PLANE, ffn_rows, width)
    bias = jnp.concatenate([b_query, b_value, b_hidden]).reshape(-1, LANES)
    bias_high = lax.reduce_precision(bias, 8, 7)
    bias_rows = jnp.concatenate([bias_high, bias - bias_high]).astype(BF16).reshape(-1, width)
    bias_rows = jnp.pad(bias_rows, ((0, 16 - bias_rows.shape[0]), (0, 0)))

    def near_heads(j):
        return lambda core, chip: (slice(None), chip ^ j)

    def near_hid(j):
        return lambda core, chip: (chip ^ j,)

    def near_back(j):
        return lambda core, chip: (core * 4 + (chip ^ j),)

    att_send = pack(
        where, (2, heads, part, width), [(0, near_heads(0), (0,)), (1, near_heads(0), (1,))], pair
    )
    att_z = from_shards(att_send.reshape(att_rows, width))
    packed = pack(
        where,
        (ffn_rows + 16, width),
        [(0, near_hid(0), (pl.ds(0, ffn_rows),)), (1, at(), (pl.ds(ffn_rows, 16),))],
        [hid_near, bias_rows],
        att_z,
    )
    hid_z = from_shards(packed)
    rows_other = swap(pack(where, inputs.shape, [(0, at(), ())], [inputs], hid_z[:1]), "tensor", 1)
    back_send = pack(where, (ffn_rows, width), [(0, near_back(0), ())], [back_near], hid_z)
    back_z = from_shards(back_send)

    att_far = from_chips(stacked(where, att_z, att_rows))
    shape = (4, shards, 2, heads, part, width)
    moves = [(m, near_heads(j), (j, 0, m)) for j in range(4) for m in range(2)]
    moves += [(2 + j, at(), (j, far)) for j in range(4)]
    att_far = [v.reshape(shards - 1, 2, heads, part, width) for v in att_far]
    att_own = pack(where, shape, moves, pair + att_far, hid_z)
    att_swap = swap(att_own, "dp", CORE)

    def ffn_half(near, near_index, far_slices, earlier):
        halves = [pl.ds(0, ffn_rows // 2), pl.ds(ffn_rows // 2, ffn_rows // 2)]
        moves = [(0, near_index(j), (j, 0)) for j in range(4)]
        moves += [(1 + j, at(), (j, far)) for j in range(3)]
        moves += [(4 + k, at(), (3, far, halves[k])) for k in range(2)]
        own = pack(where, (4, shards, ffn_rows, width), moves, [near] + far_slices, earlier)
        own = own.reshape(-1, width)
        return own, swap(own, "dp", CORE)

    hid_far = halves_from_chips(where, stacked(where, hid_z, ffn_rows, att_far[1:]))
    hid_own, hid_swap = ffn_half(hid_near, near_hid, hid_far, ())

    bias = jnp.stack([packed[ffn_rows:]] + [v[ffn_rows:] for v in hid_z]).astype(F32)
    bias = bias.reshape(shards, -1)
    count = 2 * head_cols + hidden
    bias = bias[:, :count] + bias[:, count : 2 * count]

    def relative_heads(v):
        return relative(v.reshape(shards * heads, 4, part), 1, chip).reshape(-1)

    bq = relative_heads(bias[:, :head_cols])
    bv = relative_heads(bias[:, head_cols : 2 * head_cols])
    bh = relative(bias[:, 2 * head_cols :].reshape(shards, PLANE, ffn_rows), 1, me)
    bh = bh.transpose(1, 0, 2).reshape(2, 4 * hidden // 2)

    queries, key_rows, values, wq, wk, wv, wo = project(
        where, att_own, att_swap, inputs, rows_other, bq[None], bv[None]
    )
    wq, wk, wv, wo = (w.reshape(shards * head_cols, width) for w in (wq, wk, wv, wo))
    place = jnp.stack([lengths[t // per_slot], (t % per_slot) * rows]).astype(jnp.int32)
    back_stack = stacked(where, back_z, ffn_rows, (queries, hid_far[1], hid_far[2]))
    context, logsum = attend(place, queries, key_rows, values, back_stack)
    back_far = halves_from_chips(where, back_stack, (context,))
    back_own, back_swap = ffn_half(back_near, near_back, back_far, ())
    full, low = ((rows, width), F32), ((rows, width), BF16)
    half_low = ((rows, 2 * hidden), BF16)
    three = ((3, width), F32)
    mid, zhat_one, scale_one = whole_call(
        mid_kernel,
        [low, full, ((rows, LANES), F32)],
        (context, wo, inputs, b_output[None], gain_one[None], shift_one[None]),
        10**9,
    )
    act_own, slope_own = whole_call(
        hidden_kernel, [half_low, half_low], (mid, hid_own, bh[:1]), 3 * 10**9
    )
    act_swap, slope_swap = whole_call(
        hidden_kernel, [half_low, half_low], (mid, hid_swap, bh[1:]), 3 * 10**9
    )
    outputs, grad_second, grad_branch, sums_two = whole_call(
        branch_kernel,
        [low, full, low, three],
        (
            act_own,
            act_swap,
            back_own,
            back_swap,
            mid,
            b_back[None],
            gain_two[None],
            shift_two[None],
            cotangent,
        ),
        3 * 10**9,
    )

    quarter = (2, 2, shards, ffn_rows, width)
    pair_out = [((2 * hidden, width), BF16)] * 2
    back_keep, back_send = whole_call(
        pair_grads_kernel, pair_out, (act_own, act_swap, grad_branch), 2 * 10**9
    )
    back_part = add(back_keep, swap(back_send, "dp", CORE)).reshape(quarter)
    pre_own, pre_swap, grad_b_hidden = whole_call(
        pre_kernel,
        [half_low, half_low, ((1, 4 * hidden), F32)],
        (grad_branch, back_own, back_swap, slope_own, slope_swap),
        2 * 10**9,
    )
    hid_keep, hid_send = whole_call(pair_grads_kernel, pair_out, (pre_own, pre_swap, mid), 2 * 10**9)
    hid_part = add(hid_keep, swap(hid_send, "dp", CORE)).reshape(quarter)
    back_x = swap(back_part[:, 1], "dp", XBIT)
    hid_y = swap(hid_part[1], "dp", YBIT)
    grad_first, grad_attn, grad_context, sums_one = whole_call(
        first_kernel,
        [full, low, low, three],
        (
            pre_own,
            pre_swap,
            hid_own,
            hid_swap,
            grad_second,
            zhat_one,
            scale_one,
            gain_one[None],
            wo,
        ),
        3 * 10**9,
    )
    grad_queries, grad_keys, grad_values = attend_back(
        place, queries, key_rows, values, logsum, grad_context, hid_part
    )

    whole = jnp.concatenate([sums_one, sums_two], axis=0)
    whole = relative(whole.reshape(6, PLANE, 1, ffn_rows), 1, me)
    whole = jnp.broadcast_to(whole, (6, PLANE, shards, ffn_rows)).reshape(6, -1)
    extra = jnp.concatenate([jnp.zeros_like(grad_b_hidden), grad_b_hidden, whole], axis=0)
    extra = extra.astype(BF16)
    att_keep, att_send = attention_weight_grads(
        core.astype(jnp.int32).reshape(1),
        grad_queries,
        grad_keys,
        grad_values,
        context,
        grad_attn,
        inputs,
        rows_other,
        extra,
        shards,
    )
    wide = att_keep.shape[-1]
    att_part = add(att_keep, swap(att_send, "dp", CORE)).reshape(2, 2, shards, -1, wide)

    total = dot_nn(grad_keys, wk) + dot_nn(grad_values, wv)
    returned = swap(total[rows:].astype(BF16), "tensor", 1).astype(F32)
    input_grad = (total[:rows] + dot_nn(grad_queries, wq) + returned + grad_first).astype(BF16)

    back_part = add(back_part[:, 0], back_x)
    hid_part = add(hid_part[0], hid_y)

    def later(v):
        return pack(where, v.shape, [(0, at(), ())], [v], (att_send,))

    back_sum = add(back_part[0], swap(later(back_part[1]), "dp", YBIT))
    hid_sum = add(hid_part[0], swap(later(hid_part[1]), "dp", XBIT))
    two = shards // 2
    att_a, att_b = att_part[:, :, :two], att_part[:, :, two:]
    att_a = add(att_a[:, 0], swap(att_a[:, 1], "dp", XBIT))
    att_b = add(att_b[0], swap(att_b[1], "dp", YBIT))
    att_a = add(att_a[0], swap(att_a[1], "dp", YBIT))
    att_b = add(att_b[0], swap(att_b[1], "dp", XBIT))
    ffn_sum = shards_reduce([jnp.stack([back_sum[k], hid_sum[k]]) for k in range(shards)])
    halves = [pl.ds(0, ffn_rows // 2), pl.ds(ffn_rows // 2, ffn_rows // 2)]
    moves = [(j, at(), (j,)) for j in range(3)]
    moves += [(3 + k, at(), (3, slice(None), halves[k])) for k in range(2)]
    ffn_out = pack(where, (4, 2, ffn_rows, width), moves, halves_from_chips(where, ffn_sum))
    back_out, hid_out = ffn_outputs(where, ffn_out, swap(ffn_out, "dp", CORE), hidden, width)
    att_sum = shards_reduce([(att_a if k < two else att_b)[k % two] for k in range(shards)])
    att_out = stacked(where, from_chips(att_sum), att_rows)
    gq, gk, gv, go, vectors = att_outputs(
        where, att_out, swap(att_out, "dp", CORE), head_cols, width
    )
    vectors = vectors[:, :8].T
    sums = vectors[0].reshape(2, 4, 2, heads, part)

    def head_sums(g):
        return sums[g, :, 0].transpose(1, 0, 2).reshape(-1)

    return (
        outputs,
        input_grad,
        gq,
        gk,
        gv,
        head_sums(0),
        head_sums(1),
        go,
        vectors[2],
        vectors[3],
        vectors[4],
        hid_out,
        vectors[1],
        back_out,
        vectors[5],
        vectors[6],
        vectors[7],
    )


def solution(mesh):
    rows = P(("dp", "tensor"), None)
    columns, depth, vector = P(None, "tensor"), P("tensor", None), P("tensor")
    return jax.shard_map(
        local,
        mesh=mesh,
        in_specs=(
            rows,
            rows,
            P("dp"),
            columns,
            columns,
            columns,
            vector,
            vector,
            depth,
            P(),
            P(),
            P(),
            columns,
            vector,
            depth,
            P(),
            P(),
            P(),
        ),
        out_specs=(
            rows,
            rows,
            columns,
            columns,
            columns,
            vector,
            vector,
            depth,
            P(),
            P(),
            P(),
            columns,
            vector,
            depth,
            P(),
            P(),
            P(),
        ),
        check_vma=False,
    )
```

```python
import functools

import jax
import jax.numpy as jnp
from jax import lax
from jax.experimental import pallas as pl
from jax.experimental.pallas import tpu as pltpu
from jax.sharding import PartitionSpec as P

HD = 64
LANES = 128
PLANE = 8
CORE, XBIT, YBIT = 1, 2, 4
BF16, F32 = jnp.bfloat16, jnp.float32
MIB = 1024 * 1024
FREE = pl.CostEstimate(flops=1, bytes_accessed=1, transcendentals=0)


def dot_nn(a, b):
    return lax.dot_general(a, b, (((1,), (0,)), ((), ())), preferred_element_type=F32)


def dot_nt(a, b):
    return lax.dot_general(a, b, (((1,), (1,)), ((), ())), preferred_element_type=F32)


def dot_tn(a, b):
    return lax.dot_general(a, b, (((0,), (0,)), ((), ())), preferred_element_type=F32)


def swap(v, axis, bit):
    count = lax.axis_size(axis)
    return lax.ppermute(v, axis, [(i, i ^ bit) for i in range(count)])


def pack_kernel(moves, place_ref, *refs):
    out_ref, sem = refs[-2], refs[-1]
    core, chip = place_ref[0], place_ref[1]
    copies = [
        pltpu.make_async_copy(refs[which].at[source(core, chip)], out_ref.at[target], sem.at[k])
        for k, (which, source, target) in enumerate(moves)
    ]
    for copy in copies:
        copy.start()
    for copy in copies:
        copy.wait()


def pack(where, shape, moves, arrays, earlier=(), far=0):
    vmem, space = pl.BlockSpec(memory_space=pltpu.VMEM), pl.BlockSpec(memory_space=pl.ANY)
    return pl.pallas_call(
        functools.partial(pack_kernel, moves),
        in_specs=[pl.BlockSpec(memory_space=pltpu.SMEM)]
        + [pl.BlockSpec(memory_space=pltpu.HBM)] * far
        + [space] * (len(arrays) - far + len(earlier)),
        out_specs=vmem,
        out_shape=jax.ShapeDtypeStruct(shape, BF16),
        scratch_shapes=[pltpu.SemaphoreType.DMA((len(moves),))],
        compiler_params=pltpu.CompilerParams(vmem_limit_bytes=6 * MIB),
        cost_estimate=FREE,
    )(where, *arrays, *earlier)


def nothing_kernel(*refs):
    del refs


def after(v, *earlier):
    space = pl.BlockSpec(memory_space=pl.ANY)
    return pl.pallas_call(
        nothing_kernel,
        in_specs=[space] * (1 + len(earlier)),
        out_specs=space,
        out_shape=jax.ShapeDtypeStruct(v.shape, v.dtype),
        input_output_aliases={0: 0},
    )(v, *earlier)


def fold_kernel(plan, place_ref, *refs):
    del place_ref
    outs = refs[len(refs) - sum(len(picks) for picks in plan) :]
    spot = 0
    for k, picks in enumerate(plan):
        for pick in picks:
            total = refs[2 * k][pick].astype(F32) + refs[2 * k + 1][pick].astype(F32)
            outs[spot][...] = total.astype(BF16)
            spot += 1


def fold(where, groups, earlier=()):
    vmem, space = pl.BlockSpec(memory_space=pltpu.VMEM), pl.BlockSpec(memory_space=pl.ANY)
    arrays = [v for a, b, _ in groups for v in (a, b)]
    outs = [
        jax.ShapeDtypeStruct(jax.eval_shape(lambda v, p=pick: v[p], a).shape, BF16)
        for a, _, picks in groups
        for pick in picks
    ]
    return pl.pallas_call(
        functools.partial(fold_kernel, [picks for _, _, picks in groups]),
        in_specs=[pl.BlockSpec(memory_space=pltpu.SMEM)]
        + [vmem] * len(arrays)
        + [space] * len(earlier),
        out_specs=[vmem] * len(outs),
        out_shape=outs,
        compiler_params=pltpu.CompilerParams(vmem_limit_bytes=14 * MIB),
        cost_estimate=FREE,
    )(where, *arrays, *earlier)


def sum_kernel(first_ref, a_ref, b_ref, c_ref, *refs):
    total = first_ref[...].astype(F32) + a_ref[...].astype(F32)
    total = total + b_ref[...].astype(F32) + c_ref[...].astype(F32)
    refs[-1][...] = total.astype(refs[-1].dtype)


def at(*index):
    return lambda core, chip: index


def stacked(where, arrays, rows, earlier=()):
    top = pl.ds(0, rows)
    moves = [(i, at(top), (i,)) for i in range(len(arrays))]
    return pack(where, (len(arrays), rows) + arrays[0].shape[1:], moves, arrays, earlier)


def from_shards(v):
    return [swap(v, "tensor", k) for k in range(1, lax.axis_size("tensor"))]


def halves_from_chips(where, v, between=(), sent=False):
    v_x, v_y = swap(v, "dp", XBIT), swap(v, "dp", YBIT)
    half = v.shape[1] // 2
    low, high = (slice(None), pl.ds(0, half)), (slice(None), pl.ds(half, half))
    shape = (v.shape[0], half) + v.shape[2:]
    on_y = pack(where, shape, [(0, at(*low), ())], [v_x], between)
    on_x = pack(where, shape, [(0, at(*high), ())], [v_y], between)
    got = [v, v_x, v_y, swap(on_y, "dp", YBIT), swap(on_x, "dp", XBIT)]
    return (got, [on_y, on_x]) if sent else got


def from_chips(v):
    return [v] + [swap(v, "dp", bits) for bits in (XBIT, YBIT, XBIT | YBIT)]


def shards_reduce(pieces, got, earlier=()):
    more = lax.axis_size("dp") > PLANE
    vmem, space = pl.BlockSpec(memory_space=pltpu.VMEM), pl.BlockSpec(memory_space=pl.ANY)
    total = pl.pallas_call(
        sum_kernel,
        in_specs=[vmem] * len(pieces) + [space] * len(earlier),
        out_specs=vmem,
        out_shape=jax.ShapeDtypeStruct(pieces[0].shape, F32 if more else BF16),
        compiler_params=pltpu.CompilerParams(vmem_limit_bytes=6 * MIB),
        cost_estimate=FREE,
    )(pieces[0], *got, *earlier)
    step = PLANE
    while step < lax.axis_size("dp"):
        total = total + swap(total, "dp", step)
        step *= 2
    return total.astype(BF16)


def send_pieces(pieces):
    return [swap(pieces[k], "tensor", k) for k in range(1, len(pieces))]


def relative_lanes(v, where_me, bits, block):
    width = v.shape[-1]
    spot = lax.broadcasted_iota(jnp.int32, v.shape, 1) // block
    for b in range(bits):
        shift = block << b
        right, left = pltpu.roll(v, shift, 1), pltpu.roll(v, width - shift, 1)
        flipped = jnp.where(((spot >> b) & 1) == 1, right, left)
        v = jnp.where(((where_me >> b) & 1) == 1, flipped, v)
    return v


def bias_kernel(place_ref, *refs):
    sources, (bq_ref, bv_ref, bh_ref) = refs[:4], refs[4:]
    core, chip = place_ref[0], place_ref[1]
    rows = sources[0].shape[0] - 16
    width = bq_ref.shape[1]
    group = width // 4
    hidden, heads = [], []
    for ref in sources:
        tail = ref[rows : rows + 16].astype(F32)
        hidden.append(tail[0:1] + tail[1:2])
        heads.append(tail[2:3] + tail[3:4])
    hidden = jnp.concatenate(hidden + hidden, axis=0)
    hidden = relative_lanes(hidden, core * 4 + chip, 3, hidden.shape[1] // PLANE)
    half = hidden.shape[1] // 2
    for s in range(4):
        bh_ref[0:1, s * half : (s + 1) * half] = hidden[s : s + 1, :half]
        bh_ref[1:2, s * half : (s + 1) * half] = hidden[s : s + 1, half:]
    for k, out in enumerate((bq_ref, bv_ref)):
        row = jnp.concatenate([h[:, k * group : (k + 1) * group] for h in heads], axis=1)
        row = jnp.broadcast_to(row, (8, width))
        out[...] = relative_lanes(row, chip, 2, HD // 4)[0:1]


def biases(where, sources, width, hidden):
    vmem = pl.BlockSpec(memory_space=pltpu.VMEM)
    return pl.pallas_call(
        bias_kernel,
        in_specs=[pl.BlockSpec(memory_space=pltpu.SMEM)] + [vmem] * 4,
        out_specs=[vmem] * 3,
        out_shape=[
            jax.ShapeDtypeStruct((1, width), F32),
            jax.ShapeDtypeStruct((1, width), F32),
            jax.ShapeDtypeStruct((2, 2 * hidden), F32),
        ],
        compiler_params=pltpu.CompilerParams(vmem_limit_bytes=4 * MIB),
        cost_estimate=FREE,
    )(where, *sources)


def qkv_kernel(place_ref, own, other, x_ref, xo_ref, bq_ref, bv_ref, *refs):
    outs, scratch, sem, out_sem = refs[:7], refs[7:14], refs[14], refs[15]
    (q_ref, k_ref, v_ref), weights = scratch[:3], scratch[3:]
    core = place_ref[0]
    rows, width = x_ref.shape

    def copies(src, group):
        return [
            pltpu.make_async_copy(
                src.at[j, :, m], weights[2 * group + m].at[:, :, j], sem.at[group, m, j]
            )
            for m in range(2)
            for j in range(4)
        ]

    for group in (0, 1):

        @pl.when(core == group)
        def _():
            for copy in copies(own, group):
                copy.start()

        @pl.when(core != group)
        def _():
            for copy in copies(other, group):
                copy.start()

    def landed(group):
        @pl.when(core == group)
        def _():
            for copy in copies(own, group):
                copy.wait()

        @pl.when(core != group)
        def _():
            for copy in copies(other, group):
                copy.wait()

    leaving = [pltpu.make_async_copy(scratch[k], outs[k], out_sem.at[k]) for k in range(7)]
    landed(0)
    leaving[3].start()
    leaving[4].start()
    x, xo = x_ref[...], xo_ref[...]
    q_ref[...] = (dot_nt(x, weights[0][...].reshape(width, width)) + bq_ref[...]).astype(BF16)
    leaving[0].start()
    w = weights[1][...].reshape(width, width)
    k_ref[:rows] = dot_nt(x, w).astype(BF16)
    k_ref[rows:] = dot_nt(xo, w).astype(BF16)
    leaving[1].start()
    landed(1)
    leaving[5].start()
    leaving[6].start()
    w = weights[2][...].reshape(width, width)
    v_ref[:rows] = (dot_nt(x, w) + bv_ref[...]).astype(BF16)
    v_ref[rows:] = (dot_nt(xo, w) + bv_ref[...]).astype(BF16)
    leaving[2].start()
    for copy in leaving:
        copy.wait()


def project(where, own, other, x, xo, bq, bv):
    rows, width = x.shape
    _, shards, _, heads, part, _ = own.shape
    vmem, hbm = pl.BlockSpec(memory_space=pltpu.VMEM), pl.BlockSpec(memory_space=pltpu.HBM)
    space = pl.BlockSpec(memory_space=pl.ANY)
    shapes = [(rows, width), (2 * rows, width), (2 * rows, width)]
    shapes += [(shards, heads, 4, part, width)] * 4
    return pl.pallas_call(
        qkv_kernel,
        in_specs=[pl.BlockSpec(memory_space=pltpu.SMEM), space, space] + [vmem] * 4,
        out_specs=[hbm] * 7,
        out_shape=[jax.ShapeDtypeStruct(shape, BF16) for shape in shapes],
        scratch_shapes=[pltpu.VMEM(shape, BF16) for shape in shapes]
        + [pltpu.SemaphoreType.DMA((2, 2, 4)), pltpu.SemaphoreType.DMA((7,))],
        compiler_params=pltpu.CompilerParams(vmem_limit_bytes=18 * MIB),
        cost_estimate=FREE,
    )(where, own, other, x, xo, bq, bv)


def att_out_kernel(place_ref, own_ref, other_ref, gq_ref, gk_ref, gv_ref, go_ref, *sums):
    core, chip = place_ref[0], place_ref[1]
    head_cols, width = go_ref.shape
    heads, part = head_cols // HD, HD // 4
    extras = []
    for group in (0, 1):
        blocks = []
        for c in range(4):
            block = jnp.where(core == group, own_ref[c ^ chip], other_ref[c ^ chip])
            extras.append(block[:, width:])
            blocks.append(block)
        for m in range(2):
            pieces = [
                blocks[c][(m * heads + h) * part : (m * heads + h + 1) * part]
                for h in range(heads)
                for c in range(4)
            ]
            whole = jnp.concatenate(pieces, axis=0)
            (gq_ref, gk_ref, gv_ref, go_ref)[2 * group + m][...] = whole[:, :width].astype(F32)
            if m == 0:
                sums[group][...] = whole[:, width:].astype(F32).T[0]
    extras = jnp.concatenate(extras, axis=0).astype(F32).T
    for k in range(1, 8):
        sums[1 + k][...] = extras[k]


def att_outputs(where, own, other, head_cols, width):
    vmem = pl.BlockSpec(memory_space=pltpu.VMEM)
    weight = jax.ShapeDtypeStruct((head_cols, width), F32)
    vector = jax.ShapeDtypeStruct((width,), F32)
    few = jax.ShapeDtypeStruct((head_cols,), F32)
    return pl.pallas_call(
        att_out_kernel,
        in_specs=[pl.BlockSpec(memory_space=pltpu.SMEM), vmem, vmem],
        out_specs=[vmem] * 13,
        out_shape=[weight] * 4 + [few] * 2 + [vector] * 7,
        compiler_params=pltpu.CompilerParams(vmem_limit_bytes=14 * MIB),
    )(where, own, other)


def ffn_out_kernel(place_ref, own_ref, other_ref, back_ref, hid_ref):
    core, chip = place_ref[0], place_ref[1]
    rows = own_ref.shape[2]
    blocks = []
    for group in (0, 1):
        for c in range(4):
            block = jnp.where(core == group, own_ref[c ^ chip], other_ref[c ^ chip])
            spot = (group * 4 + c) * rows
            back_ref[spot : spot + rows] = block[0].astype(F32)
            blocks.append(block[1])
    hid_ref[...] = jnp.concatenate(blocks, axis=0).astype(F32).T


def ffn_outputs(where, own, other, hidden, width):
    vmem = pl.BlockSpec(memory_space=pltpu.VMEM)
    return pl.pallas_call(
        ffn_out_kernel,
        in_specs=[pl.BlockSpec(memory_space=pltpu.SMEM), vmem, vmem],
        out_specs=[vmem] * 2,
        out_shape=[
            jax.ShapeDtypeStruct((hidden, width), F32),
            jax.ShapeDtypeStruct((width, hidden), F32),
        ],
        compiler_params=pltpu.CompilerParams(vmem_limit_bytes=20 * MIB),
    )(where, own, other)


def live_keys(place_ref, keys, half_rows):
    spot = lax.broadcasted_iota(jnp.int32, (keys, 1), 0)
    first = place_ref[1]
    spot = jnp.where(spot < half_rows, spot + first, spot - first)
    return spot < place_ref[0]


def attend_kernel(place_ref, q_ref, k_ref, v_ref, *refs, half_rows):
    out_ref, lse_ref = refs[-2:]
    rows, keys = q_ref.shape[0], k_ref.shape[0]
    q = q_ref[...] * jnp.asarray(0.125, BF16)
    k = k_ref[...]
    v_turned = v_ref[...].T
    live = live_keys(place_ref, keys, half_rows)
    lane = lax.broadcasted_iota(jnp.int32, (rows, LANES), 1)
    outs, sums = [], []
    for h in range(LANES // HD):
        qh = jnp.where((lane // HD) == h, q, jnp.zeros_like(q))
        s = jnp.where(live, dot_nt(k, qh), -1e30)
        top = jnp.max(s, axis=0, keepdims=True)
        e = jnp.exp(s - top)
        total = jnp.sum(e, axis=0, keepdims=True)
        p = (e * (1.0 / total)).astype(BF16)
        outs.append(dot_nn(v_turned, p)[h * HD : (h + 1) * HD])
        sums.append(top + jnp.log(total))
    out_ref[...] = jnp.concatenate(outs, axis=0).T.astype(BF16)
    lse_ref[...] = jnp.concatenate(sums + [jnp.zeros((6, rows), F32)], axis=0)


def attend_back_kernel(
    place_ref, q_ref, k_ref, v_ref, lse_ref, do_ref, _, dq_ref, dk_ref, dv_ref, *, half_rows
):
    rows, keys = q_ref.shape[0], k_ref.shape[0]
    k, v, do = k_ref[...], v_ref[...], do_ref[...]
    q = q_ref[...] * jnp.asarray(0.125, BF16)
    k_turned = k.T
    live = live_keys(place_ref, keys, half_rows)
    lane = lax.broadcasted_iota(jnp.int32, (rows, LANES), 1)
    dqs, dks, dvs = [], [], []
    for h in range(LANES // HD):
        mine = (lane // HD) == h
        qh = jnp.where(mine, q, jnp.zeros_like(q))
        doh = jnp.where(mine, do, jnp.zeros_like(do))
        s = jnp.where(live, dot_nt(k, qh), -1e30)
        p = jnp.exp(s - lse_ref[h : h + 1, :])
        dp = dot_nt(v, doh)
        inner = jnp.sum(p * dp, axis=0, keepdims=True)
        ds = (p * (dp - inner)).astype(BF16)
        dqs.append(dot_nn(k_turned, ds)[h * HD : (h + 1) * HD])
        dks.append(dot_nn(ds, qh))
        dvs.append(dot_nn(p.astype(BF16), doh))
    dq_ref[...] = (jnp.concatenate(dqs, axis=0).T * 0.125).astype(BF16)
    dk_ref[...] = (dks[0] + dks[1]).astype(BF16)
    dv_ref[...] = (dvs[0] + dvs[1]).astype(BF16)


def attend(place, q, k, v, first, pairs, earlier):
    rows, width = q.shape[0], pairs * LANES
    keys = k.shape[0]
    q_spec = pl.BlockSpec((rows, LANES), lambda i: (0, i + first))
    k_spec = pl.BlockSpec((keys, LANES), lambda i: (0, i + first))
    out_spec = pl.BlockSpec((rows, LANES), lambda i: (0, i))
    lse_spec = pl.BlockSpec((8, rows), lambda i: (i, 0))
    return pl.pallas_call(
        functools.partial(attend_kernel, half_rows=rows),
        grid=(pairs,),
        in_specs=[
            pl.BlockSpec(memory_space=pltpu.SMEM),
            q_spec,
            k_spec,
            k_spec,
        ]
        + [pl.BlockSpec(memory_space=pl.ANY)] * len(earlier),
        out_specs=[out_spec, lse_spec],
        out_shape=[
            jax.ShapeDtypeStruct((rows, width), BF16),
            jax.ShapeDtypeStruct((8 * pairs, rows), F32),
        ],
        compiler_params=pltpu.CompilerParams(vmem_limit_bytes=10 * MIB),
        cost_estimate=FREE,
    )(place, q, k, v, *earlier)


def attend_back(place, q, k, v, lse, do, earlier):
    rows, width = q.shape
    keys = k.shape[0]
    q_spec = pl.BlockSpec((rows, LANES), lambda i: (0, i))
    k_spec = pl.BlockSpec((keys, LANES), lambda i: (0, i))
    lse_spec = pl.BlockSpec((8, rows), lambda i: (i, 0))
    return pl.pallas_call(
        functools.partial(attend_back_kernel, half_rows=rows),
        grid=(width // LANES,),
        in_specs=[
            pl.BlockSpec(memory_space=pltpu.SMEM),
            q_spec,
            k_spec,
            k_spec,
            lse_spec,
            q_spec,
            pl.BlockSpec(memory_space=pl.ANY),
        ],
        out_specs=[q_spec, k_spec, k_spec],
        out_shape=[
            jax.ShapeDtypeStruct((rows, width), BF16),
            jax.ShapeDtypeStruct((keys, width), BF16),
            jax.ShapeDtypeStruct((keys, width), BF16),
        ],
        compiler_params=pltpu.CompilerParams(vmem_limit_bytes=10 * MIB),
        cost_estimate=FREE,
    )(place, q, k, v, lse, do, earlier)


def weights_kernel(
    place_ref,
    dq_ref,
    dk_ref,
    dv_ref,
    context_ref,
    context_two_ref,
    ga_ref,
    x_ref,
    xo_ref,
    one_ref,
    two_ref,
    hid_ref,
    _,
    keep_ref,
    send_ref,
):
    rows, width = dq_ref.shape
    shards = keep_ref.shape[1]
    group = width // shards
    heads = group // HD
    part = HD // 4
    core, chip = place_ref[0], place_ref[1]
    span = 2 * group
    lane = lax.broadcasted_iota(jnp.int32, (part, LANES), 1)
    spots = lax.broadcasted_iota(jnp.int32, (8, LANES), 0)
    spots = (spots == lax.broadcasted_iota(jnp.int32, (8, LANES), 1)).astype(BF16)
    att_rows = keep_ref.shape[2]
    half = 4 * att_rows
    whole = jnp.concatenate([jnp.zeros((2, width), F32), one_ref[...], two_ref[...]], axis=0)
    whole = relative_lanes(whole, core * 4 + chip, 3, att_rows)
    line = lax.broadcasted_iota(jnp.int32, (8, half), 0)
    extra = []
    for g in range(2):
        extra.append([])
        for s in range(shards):
            mine = hid_ref[g : g + 1, s * half : (s + 1) * half]
            mine = jnp.where(line == 1, mine, whole[:, g * half : (g + 1) * half])
            extra[g].append(dot_tn(mine.astype(BF16), spots))

    def put(which, m, left_ref, rights, with_sum):
        ones = jnp.ones((rows, LANES), BF16)
        for first in range(0, width, span):
            out, sums = None, None
            for k, right in enumerate(rights):
                if isinstance(left_ref, tuple):
                    left = left_ref[first // span][...]
                else:
                    left = left_ref[k * rows : (k + 1) * rows, first : first + span]
                more = dot_tn(left, right[...])
                out = more if out is None else out + more
                if with_sum:
                    more = dot_tn(left, ones)
                    sums = more if sums is None else sums + more

            def store(dst, base):
                for at in range(0, span, part):
                    row = first + at
                    shard, rest = row // group, row % group
                    head, j = rest // HD, (rest % HD) // part
                    spot = (m * heads + head) * part
                    dst[j, shard, spot : spot + part, :width] = out[at : at + part].astype(BF16)
                    tail = extra[base][shard][j * att_rows + spot : j * att_rows + spot + part]
                    if with_sum:
                        tail = jnp.where(lane == 0, sums[at : at + part], tail)
                    dst[j, shard, spot : spot + part, width:] = tail.astype(BF16)

            @pl.when(core == which)
            def _():
                store(keep_ref, 0)

            @pl.when(core != which)
            def _():
                store(send_ref, 1)

    put(0, 0, dq_ref, [x_ref], True)
    put(0, 1, dk_ref, [x_ref, xo_ref], False)
    put(1, 0, dv_ref, [x_ref, xo_ref], True)
    put(1, 1, (context_ref, context_two_ref), [ga_ref], False)


def attention_weight_grads(where, dq, dk, dv, contexts, ga, x, xo, sums, shards, earlier):
    width = dq.shape[1]
    full = jax.ShapeDtypeStruct((4, shards, width // (2 * shards), width + LANES), BF16)
    vmem = pl.BlockSpec(memory_space=pltpu.VMEM)
    return pl.pallas_call(
        weights_kernel,
        in_specs=[pl.BlockSpec(memory_space=pltpu.SMEM)] + [vmem] * 11 + [pl.BlockSpec(memory_space=pl.ANY)],
        out_specs=[vmem, vmem],
        out_shape=[full, full],
        compiler_params=pltpu.CompilerParams(vmem_limit_bytes=22 * MIB),
        cost_estimate=FREE,
    )(where, dq, dk, dv, *contexts, ga, x, xo, *sums, earlier)


def whole_call(kernel, outs, args, flops, earlier=()):
    vmem, space = pl.BlockSpec(memory_space=pltpu.VMEM), pl.BlockSpec(memory_space=pl.ANY)
    if earlier:
        inner, count = kernel, len(args)
        kernel = lambda *refs: inner(*refs[:count], *refs[count + len(earlier) :])
    return pl.pallas_call(
        kernel,
        in_specs=[vmem] * len(args) + [space] * len(earlier),
        out_specs=[vmem] * len(outs),
        out_shape=[jax.ShapeDtypeStruct(shape, dtype) for shape, dtype in outs],
        compiler_params=pltpu.CompilerParams(vmem_limit_bytes=22 * MIB),
        cost_estimate=FREE,
    )(*args, *earlier)


def normalize(z):
    center = z - jnp.mean(z, axis=-1, keepdims=True)
    spread = jnp.mean(center * center, axis=-1, keepdims=True)
    scale = lax.rsqrt(spread + 1e-05)
    return center * scale, scale


def norm_back(grad, zhat, scale, gain):
    e = grad * gain
    inner = jnp.mean(e * zhat, axis=-1, keepdims=True)
    return (e - jnp.mean(e, axis=-1, keepdims=True) - zhat * inner) * scale


def column_sums(v):
    return jnp.sum(v, axis=0, keepdims=True)


def mid_kernel(
    context_ref,
    context_two_ref,
    wo_ref,
    x_ref,
    b_ref,
    gain_ref,
    shift_ref,
    mid_ref,
    zhat_ref,
    scale_ref,
):
    half = context_ref.shape[1]
    z = dot_nn(context_ref[...], wo_ref[:half]) + dot_nn(context_two_ref[...], wo_ref[half:])
    z = z + b_ref[...] + x_ref[...].astype(F32)
    zhat, scale = normalize(z)
    mid_ref[...] = (zhat * gain_ref[...] + shift_ref[...]).astype(BF16)
    zhat_ref[...] = zhat
    scale_ref[...] = jnp.broadcast_to(scale, scale_ref.shape)


def hidden_kernel(mid_ref, w_ref, b_ref, act_ref, slope_ref):
    block = 512
    for first in range(0, w_ref.shape[0], block):
        cols = slice(first, first + block)
        act, slope = gelu_pair(dot_nt(mid_ref[...], w_ref[cols]) + b_ref[:, cols])
        act_ref[:, cols] = act.astype(BF16)
        slope_ref[:, cols] = slope.astype(BF16)


def branch_kernel(
    act_own_ref,
    act_other_ref,
    w_own_ref,
    w_other_ref,
    mid_ref,
    b_ref,
    gain_ref,
    shift_ref,
    cotangent_ref,
    out_ref,
    grad_ref,
    low_ref,
    sums_ref,
):
    z = dot_nn(act_own_ref[...], w_own_ref[...]) + dot_nn(act_other_ref[...], w_other_ref[...])
    zhat, scale = normalize(z + b_ref[...] + mid_ref[...].astype(F32))
    out_ref[...] = (zhat * gain_ref[...] + shift_ref[...]).astype(BF16)
    c = cotangent_ref[...].astype(F32)
    grad = norm_back(c, zhat, scale, gain_ref[...])
    low = grad.astype(BF16)
    grad_ref[...] = grad
    low_ref[...] = low
    sums_ref[...] = jnp.concatenate(
        [column_sums(low.astype(F32)), column_sums(c * zhat), column_sums(c)], axis=0
    )


def pair_grads_kernel(left_own_ref, left_other_ref, right_ref, keep_ref, send_ref):
    send_ref[...] = dot_tn(left_other_ref[...], right_ref[...]).astype(BF16)
    keep_ref[...] = dot_tn(left_own_ref[...], right_ref[...]).astype(BF16)


def input_kernel(
    dq_ref, dk_ref, dv_ref, wq_ref, wk_ref, wv_ref, first_ref, own_ref, other_ref
):
    rows = dq_ref.shape[0]
    total = dot_nn(dk_ref[rows:], wk_ref[...]) + dot_nn(dv_ref[rows:], wv_ref[...])
    other_ref[...] = total.astype(BF16)
    total = dot_nn(dk_ref[:rows], wk_ref[...]) + dot_nn(dv_ref[:rows], wv_ref[...])
    own_ref[...] = total + dot_nn(dq_ref[...], wq_ref[...]) + first_ref[...]


def pre_kernel(
    low_ref, w_own_ref, w_other_ref, slope_own_ref, slope_other_ref, own_ref, other_ref, sums_ref
):
    for k, (w, slope, out) in enumerate(
        ((w_own_ref, slope_own_ref, own_ref), (w_other_ref, slope_other_ref, other_ref))
    ):
        grad = (dot_nt(low_ref[...], w[...]) * slope[...].astype(F32)).astype(BF16)
        out[...] = grad
        sums_ref[k : k + 1] = column_sums(grad.astype(F32))


def first_kernel(
    pre_own_ref,
    pre_other_ref,
    w_own_ref,
    w_other_ref,
    grad_ref,
    zhat_ref,
    scale_ref,
    gain_ref,
    wo_ref,
    first_ref,
    low_ref,
    context_ref,
    sums_ref,
):
    grad = dot_nn(pre_own_ref[...], w_own_ref[...]) + dot_nn(pre_other_ref[...], w_other_ref[...])
    grad = grad + grad_ref[...]
    zhat = zhat_ref[...]
    first = norm_back(grad, zhat, scale_ref[:, :1], gain_ref[...])
    low = first.astype(BF16)
    first_ref[...] = first
    low_ref[...] = low
    context_ref[...] = dot_nt(low, wo_ref[...]).astype(BF16)
    sums_ref[...] = jnp.concatenate(
        [column_sums(low.astype(F32)), column_sums(grad * zhat), column_sums(grad)], axis=0
    )


def gelu_pair(v):
    cdf = 0.5 * (1.0 + lax.erf(v * (0.5**0.5)))
    density = jnp.exp(-0.5 * v * v) * 0.3989422804014327
    return v * cdf, cdf + v * density


def local(
    inputs,
    cotangent,
    lengths,
    w_query,
    w_key,
    w_value,
    b_query,
    b_value,
    w_output,
    b_output,
    gain_one,
    shift_one,
    w_hidden,
    b_hidden,
    w_back,
    b_back,
    gain_two,
    shift_two,
):
    rows, width = inputs.shape
    shards = lax.axis_size("tensor")
    head_cols = w_query.shape[1]
    hidden = w_hidden.shape[1]
    heads = head_cols // HD
    part = HD // 4
    ffn_rows = hidden // PLANE
    per_slot = shards // lengths.shape[0]
    assert per_slot == 2 and shards == 4 and lax.axis_size("dp") % PLANE == 0
    dp = lax.axis_index("dp")
    core = dp & 1
    chip = (((dp >> 2) & 1) << 1) | ((dp >> 1) & 1)
    me = core * 4 + chip
    t = lax.axis_index("tensor")

    where = jnp.stack([core, chip]).astype(jnp.int32)
    att_rows = 2 * heads * part
    far = pl.ds(1, shards - 1)

    by_head = (heads, 4, part, width)
    pair = [
        jnp.where(core == 0, w_query, w_value).T.reshape(by_head),
        jnp.where(core == 0, w_key.T, w_output).reshape(by_head),
    ]
    hid_near = lax.dynamic_slice_in_dim(w_hidden, core * (hidden // 2), hidden // 2, 1)
    hid_near = hid_near.T.reshape(4, ffn_rows, width)
    back_near = w_back.reshape(PLANE, ffn_rows, width)
    bias = jnp.pad(jnp.concatenate([b_query, b_value]), (0, width - 2 * head_cols))
    bias = jnp.stack([b_hidden, b_hidden, bias, bias])
    bias_high = lax.reduce_precision(bias, 8, 7)
    bias_rows = jnp.where(jnp.arange(4)[:, None] % 2 == 0, bias_high, bias - bias_high)
    bias_rows = jnp.pad(bias_rows.astype(BF16), ((0, 12), (0, 0)))

    def near_heads(j):
        return lambda core, chip: (slice(None), chip ^ j)

    def near_hid(j):
        return lambda core, chip: (chip ^ j,)

    def near_back(j):
        return lambda core, chip: (core * 4 + (chip ^ j),)

    att_send = pack(
        where, (2, heads, part, width), [(0, near_heads(0), (0,)), (1, near_heads(0), (1,))], pair, (), 2
    )
    att_z = from_shards(att_send.reshape(att_rows, width))
    packed = pack(
        where,
        (ffn_rows + 16, width),
        [(0, near_hid(0), (pl.ds(0, ffn_rows),)), (1, at(), (pl.ds(ffn_rows, 16),))],
        [hid_near, bias_rows],
        (),
        1,
    )
    back_send = pack(where, (ffn_rows, width), [(0, near_back(0), ())], [back_near], (), 1)
    rows_send = pack(where, inputs.shape, [(0, at(), ())], [inputs], (), 1)
    att_stack = stacked(where, att_z, att_rows, (packed, back_send, rows_send))
    hid_z = from_shards(after(packed, att_stack))
    rows_other = swap(after(rows_send, *hid_z), "tensor", 1)

    hid_stack = stacked(where, hid_z, ffn_rows)
    att_far = halves_from_chips(where, att_stack, hid_z[:1])
    shape = (4, shards, 2, heads, part, width)
    moves = [(m, near_heads(j), (j, 0, m)) for j in range(4) for m in range(2)]
    moves += [(2 + j, at(), (j, far)) for j in range(3)]
    moves += [(5 + m, at(), (3, far, m)) for m in range(2)]
    att_far = [v.reshape(shards - 1, -1, heads, part, width) for v in att_far[:3]] + [
        v.reshape(shards - 1, heads, part, width) for v in att_far[3:]
    ]
    att_own = pack(where, shape, moves, pair + att_far, (rows_other,), 2)
    att_swap = swap(att_own, "dp", CORE)

    def ffn_half(near, near_index, far_slices, earlier):
        halves = [pl.ds(0, ffn_rows // 2), pl.ds(ffn_rows // 2, ffn_rows // 2)]
        moves = [(0, near_index(j), (0, j)) for j in range(4)]
        moves += [(1 + j, at(), (far, j)) for j in range(3)]
        moves += [(4 + k, at(), (far, 3, halves[k])) for k in range(2)]
        own = pack(where, (shards, 4, ffn_rows, width), moves, [near] + far_slices, earlier, 1)
        own = own.reshape(-1, width)
        return own, swap(own, "dp", CORE)

    bq, bv, bh = biases(where, [packed] + hid_z, width, hidden)

    queries, key_rows, values, wq, wk, wv, wo = project(
        where, att_own, att_swap, inputs, rows_other, bq, bv
    )
    wq, wk, wv, wo = (w.reshape(shards * head_cols, width) for w in (wq, wk, wv, wo))
    place = jnp.stack([lengths[t // per_slot], (t % per_slot) * rows]).astype(jnp.int32)
    back_z = from_shards(after(back_send, rows_other, att_swap))
    hid_far, hid_sent = halves_from_chips(where, after(hid_stack, *att_far[3:]), [queries], True)
    pairs = width // LANES // 2
    context_one, logsum_one = attend(place, queries, key_rows, values, 0, pairs, hid_sent)
    back_stack = stacked(where, back_z, ffn_rows, [context_one])
    hid_own, hid_swap = ffn_half(hid_near, near_hid, hid_far, [back_stack])
    context_two, logsum_two = attend(place, queries, key_rows, values, pairs, pairs, [hid_own])
    logsum = jnp.concatenate([logsum_one, logsum_two], axis=0)
    contexts = (context_one, context_two)
    full, low = ((rows, width), F32), ((rows, width), BF16)
    half_low = ((rows, 2 * hidden), BF16)
    three = ((3, width), F32)
    mid, zhat_one, scale_one = whole_call(
        mid_kernel,
        [low, full, ((rows, LANES), F32)],
        (*contexts, wo, inputs, b_output[None], gain_one[None], shift_one[None]),
        2 * 10**8,
    )
    act_own, slope_own = whole_call(
        hidden_kernel, [half_low, half_low], (mid, hid_own, bh[:1]), 10**9
    )
    back_far = halves_from_chips(where, back_stack, [act_own])
    back_own, back_swap = ffn_half(back_near, near_back, back_far, ())
    act_swap, slope_swap = whole_call(
        hidden_kernel, [half_low, half_low], (mid, hid_swap, bh[1:]), 10**9
    )
    outputs, grad_second, grad_branch, sums_two = whole_call(
        branch_kernel,
        [low, full, low, three],
        (
            act_own,
            act_swap,
            back_own,
            back_swap,
            mid,
            b_back[None],
            gain_two[None],
            shift_two[None],
            cotangent,
        ),
        3 * 10**9,
    )

    two = shards // 2
    every = slice(None)
    low_half, high_half = pl.ds(0, two), pl.ds(two, shards - two)
    each = [(k,) for k in range(shards)]

    def first_step(keep, got, picks, earlier):
        a_keep, a_send, b_keep, b_send = fold(where, [(keep, got, picks)], earlier)
        return a_keep, b_keep, swap(a_send, "dp", XBIT), swap(b_send, "dp", YBIT), a_send

    def second_step(step, a_picks, b_picks, earlier):
        a_keep, b_keep, a_got, b_got, _ = step
        a_keep, a_send, b_keep, b_send = fold(
            where, [(a_keep, a_got, a_picks), (b_keep, b_got, b_picks)], earlier
        )
        return a_keep, b_keep, swap(a_send, "dp", YBIT), swap(b_send, "dp", XBIT), a_send

    def third_step(step, earlier):
        a_keep, b_keep, a_got, b_got, _ = step
        return fold(
            where, [(a_keep, a_got, each[:two]), (b_keep, b_got, each[: shards - two])], earlier
        )

    quarter = (shards, 2, 2, ffn_rows, width)
    ffn_picks = [
        (low_half, every, 0),
        (low_half, every, 1),
        (high_half, 0),
        (high_half, 1),
    ]
    ffn_again = [(every, 0), (every, 1)]
    pair_out = [((2 * hidden, width), BF16)] * 2
    back_keep, back_send = whole_call(
        pair_grads_kernel, pair_out, (act_own, act_swap, grad_branch), 10**9
    )
    back_got = swap(back_send, "dp", CORE)
    pre_own, pre_swap, grad_b_hidden = whole_call(
        pre_kernel,
        [half_low, half_low, ((2, 2 * hidden), F32)],
        (grad_branch, back_own, back_swap, slope_own, slope_swap),
        10**9,
    )
    back_step = first_step(back_keep.reshape(quarter), back_got.reshape(quarter), ffn_picks, ())
    hid_keep, hid_send = whole_call(
        pair_grads_kernel, pair_out, (pre_own, pre_swap, mid), 3 * 10**8, (back_step[4],)
    )
    hid_got = swap(hid_send, "dp", CORE)
    grad_first, grad_attn, grad_context, sums_one = whole_call(
        first_kernel,
        [full, low, low, three],
        (
            pre_own,
            pre_swap,
            hid_own,
            hid_swap,
            grad_second,
            zhat_one,
            scale_one,
            gain_one[None],
            wo,
        ),
        3 * 10**8,
        (hid_send,),
    )
    hid_step = first_step(
        hid_keep.reshape(quarter), hid_got.reshape(quarter), ffn_picks, (grad_first,)
    )
    grad_queries, grad_keys, grad_values = attend_back(
        place, queries, key_rows, values, logsum, grad_context, hid_step[4]
    )
    total, returned_send = whole_call(
        input_kernel,
        [full, low],
        (grad_queries, grad_keys, grad_values, wq, wk, wv, grad_first),
        3 * 10**8,
    )
    returned = swap(returned_send, "tensor", 1)
    back_step = second_step(back_step, ffn_again, ffn_again, (returned_send,))

    att_keep, att_send = attention_weight_grads(
        where,
        grad_queries,
        grad_keys,
        grad_values,
        contexts,
        grad_attn,
        inputs,
        rows_other,
        (sums_one, sums_two, grad_b_hidden),
        shards,
        back_step[4],
    )
    wide = att_keep.shape[-1]

    back_pieces = third_step(back_step, (att_keep, returned))
    back_got = send_pieces(back_pieces)
    hid_step = second_step(hid_step, ffn_again, ffn_again, (back_pieces[0],))
    att_got = swap(after(att_send, hid_step[4]), "dp", CORE)
    att_shape = (2, 2) + att_keep.shape[1:]
    att_picks = [
        (every, 0, low_half),
        (every, 1, low_half),
        (0, every, high_half),
        (1, every, high_half),
    ]
    att_step = first_step(att_keep.reshape(att_shape), att_got.reshape(att_shape), att_picks, ())
    hid_pieces = third_step(hid_step, ())
    back_sum = shards_reduce(back_pieces, back_got)
    hid_got = send_pieces(hid_pieces)
    att_step = second_step(att_step, [(0,), (1,)], [(0,), (1,)], (back_sum,))
    hid_sum = shards_reduce(hid_pieces, hid_got)
    att_pieces = third_step(att_step, (hid_sum,))
    att_got = send_pieces(att_pieces)
    input_grad = (total + returned.astype(F32)).astype(BF16)
    top = pl.ds(0, ffn_rows)
    ffn_sum = pack(
        where,
        (2, ffn_rows, width),
        [(0, at(top), (0,)), (1, at(top), (1,))],
        [back_sum, hid_sum],
        att_got[:1],
    )
    halves = [pl.ds(0, ffn_rows // 2), pl.ds(ffn_rows // 2, ffn_rows // 2)]
    moves = [(j, at(), (j,)) for j in range(3)]
    moves += [(3 + k, at(), (3, slice(None), halves[k])) for k in range(2)]
    att_sum = shards_reduce(att_pieces, att_got)
    ffn_far = halves_from_chips(where, ffn_sum, [att_sum])
    ffn_out = pack(where, (4, 2, ffn_rows, width), moves, ffn_far)
    back_out, hid_out = ffn_outputs(where, ffn_out, swap(ffn_out, "dp", CORE), hidden, width)
    att_out = stacked(where, from_chips(att_sum), att_rows, (back_out,))
    gq, gk, gv, go, sum_q, sum_v, sum_hid, *vectors = att_outputs(
        where, att_out, swap(att_out, "dp", CORE), head_cols, width
    )
    return (
        outputs,
        input_grad,
        gq.T,
        gk.T,
        gv.T,
        sum_q,
        sum_v,
        go,
        vectors[0],
        vectors[1],
        vectors[2],
        hid_out,
        sum_hid,
        back_out,
        vectors[3],
        vectors[4],
        vectors[5],
    )


def solution(mesh):
    rows = P(("dp", "tensor"), None)
    columns, depth, vector = P(None, "tensor"), P("tensor", None), P("tensor")
    return jax.shard_map(
        local,
        mesh=mesh,
        in_specs=(
            rows,
            rows,
            P("dp"),
            columns,
            columns,
            columns,
            vector,
            vector,
            depth,
            P(),
            P(),
            P(),
            columns,
            vector,
            depth,
            P(),
            P(),
            P(),
        ),
        out_specs=(
            rows,
            rows,
            columns,
            columns,
            columns,
            vector,
            vector,
            depth,
            P(),
            P(),
            P(),
            columns,
            vector,
            depth,
            P(),
            P(),
            P(),
        ),
        check_vma=False,
    )
```

```python
import functools

import jax
import jax.numpy as jnp
from jax import lax
from jax.experimental import pallas as pl
from jax.experimental.pallas import tpu as pltpu
from jax.sharding import PartitionSpec as P

HD = 64
LANES = 128
PLANE = 8
CORE, XBIT, YBIT = 1, 2, 4
BF16, F32 = jnp.bfloat16, jnp.float32
MIB = 1024 * 1024
FREE = pl.CostEstimate(flops=1, bytes_accessed=1, transcendentals=0)


def dot_nn(a, b):
    return lax.dot_general(a, b, (((1,), (0,)), ((), ())), preferred_element_type=F32)


def dot_nt(a, b):
    return lax.dot_general(a, b, (((1,), (1,)), ((), ())), preferred_element_type=F32)


def dot_tn(a, b):
    return lax.dot_general(a, b, (((0,), (0,)), ((), ())), preferred_element_type=F32)


def swap(v, axis, bit):
    count = lax.axis_size(axis)
    return lax.ppermute(v, axis, [(i, i ^ bit) for i in range(count)])


def pack_kernel(plan, far, place_ref, *refs):
    outs, sem = refs[len(refs) - len(plan) - 1 : -1], refs[-1]
    core, chip = place_ref[0], place_ref[1]
    copies = []
    for out_ref, moves in zip(outs, plan):
        for which, source, target in moves:
            if which < far:
                src, dst = refs[which].at[source(core, chip)], out_ref.at[target]
                copies.append(pltpu.make_async_copy(src, dst, sem.at[len(copies)]))
    for copy in copies:
        copy.start()
    for out_ref, moves in zip(outs, plan):
        for which, source, target in moves:
            if which >= far:
                out_ref[target or ...] = refs[which][source(core, chip) or ...]
    for copy in copies:
        copy.wait()


def packs(where, shapes, plan, arrays, earlier=(), far=0):
    vmem, space = pl.BlockSpec(memory_space=pltpu.VMEM), pl.BlockSpec(memory_space=pl.ANY)
    count = sum(which < far for moves in plan for which, _, _ in moves)
    return pl.pallas_call(
        functools.partial(pack_kernel, plan, far),
        in_specs=[pl.BlockSpec(memory_space=pltpu.SMEM)]
        + [pl.BlockSpec(memory_space=pltpu.HBM)] * far
        + [vmem] * (len(arrays) - far)
        + [space] * len(earlier),
        out_specs=[vmem] * len(shapes),
        out_shape=[jax.ShapeDtypeStruct(shape, BF16) for shape in shapes],
        scratch_shapes=[pltpu.SemaphoreType.DMA((max(count, 1),))],
        compiler_params=pltpu.CompilerParams(vmem_limit_bytes=10 * MIB),
        cost_estimate=FREE,
    )(where, *arrays, *earlier)


def pack(where, shape, moves, arrays, earlier=(), far=0):
    return packs(where, [shape], [moves], arrays, earlier, far)[0]


def nothing_kernel(*refs):
    del refs


def after(v, *earlier):
    space = pl.BlockSpec(memory_space=pl.ANY)
    return pl.pallas_call(
        nothing_kernel,
        in_specs=[space] * (1 + len(earlier)),
        out_specs=space,
        out_shape=jax.ShapeDtypeStruct(v.shape, v.dtype),
        input_output_aliases={0: 0},
    )(v, *earlier)


def fold_kernel(plan, beside, place_ref, *refs):
    del place_ref
    count = sum(len(picks) for picks in plan)
    outs = refs[len(refs) - count :]
    others = refs[2 * len(plan) : 2 * len(plan) + beside]
    spot = 0
    for k, picks in enumerate(plan):
        for pick in picks:
            total = refs[2 * k][pick].astype(F32) + refs[2 * k + 1][pick].astype(F32)
            if beside:
                outs[spot][0] = others[spot][...]
                outs[spot][1] = total.astype(BF16)
            else:
                outs[spot][...] = total.astype(BF16)
            spot += 1


def fold(where, groups, earlier=(), beside=()):
    vmem, space = pl.BlockSpec(memory_space=pltpu.VMEM), pl.BlockSpec(memory_space=pl.ANY)
    arrays = [v for a, b, _ in groups for v in (a, b)] + list(beside)
    outs = [
        jax.ShapeDtypeStruct(
            ((2,) if beside else ()) + jax.eval_shape(lambda v, p=pick: v[p], a).shape, BF16
        )
        for a, _, picks in groups
        for pick in picks
    ]
    return pl.pallas_call(
        functools.partial(fold_kernel, [picks for _, _, picks in groups], len(beside)),
        in_specs=[pl.BlockSpec(memory_space=pltpu.SMEM)]
        + [vmem] * len(arrays)
        + [space] * len(earlier),
        out_specs=[vmem] * len(outs),
        out_shape=outs,
        compiler_params=pltpu.CompilerParams(vmem_limit_bytes=14 * MIB),
        cost_estimate=FREE,
    )(where, *arrays, *earlier)


def sum_kernel(first_ref, a_ref, b_ref, c_ref, *refs):
    total = first_ref[...].astype(F32) + a_ref[...].astype(F32)
    total = total + b_ref[...].astype(F32) + c_ref[...].astype(F32)
    refs[-1][...] = total.astype(refs[-1].dtype)


def at(*index):
    return lambda core, chip: index


def stacked(where, arrays, rows, earlier=()):
    top = pl.ds(0, rows)
    moves = [(i, at(top), (i,)) for i in range(len(arrays))]
    return pack(where, (len(arrays), rows) + arrays[0].shape[1:], moves, arrays, earlier)


def from_shards(v):
    return [swap(v, "tensor", k) for k in range(1, lax.axis_size("tensor"))]


def halves_from_chips(where, v, between=(), sent=False, first=None):
    v_x, v_y = first or (swap(v, "dp", XBIT), swap(v, "dp", YBIT))
    half = v.shape[1] // 2
    low, high = (slice(None), pl.ds(0, half)), (slice(None), pl.ds(half, half))
    shape = (v.shape[0], half) + v.shape[2:]
    plan = [[(0, at(*low), ())], [(1, at(*high), ())]]
    on_y, on_x = packs(where, [shape, shape], plan, [v_x, v_y], between)
    got = [v, v_x, v_y, swap(on_y, "dp", YBIT), swap(on_x, "dp", XBIT)]
    return (got, [on_y, on_x]) if sent else got


def from_chips(v):
    return [v] + [swap(v, "dp", bits) for bits in (XBIT, YBIT, XBIT | YBIT)]


def shards_reduce(pieces, got, earlier=()):
    more = lax.axis_size("dp") > PLANE
    vmem, space = pl.BlockSpec(memory_space=pltpu.VMEM), pl.BlockSpec(memory_space=pl.ANY)
    total = pl.pallas_call(
        sum_kernel,
        in_specs=[vmem] * len(pieces) + [space] * len(earlier),
        out_specs=vmem,
        out_shape=jax.ShapeDtypeStruct(pieces[0].shape, F32 if more else BF16),
        compiler_params=pltpu.CompilerParams(vmem_limit_bytes=6 * MIB),
        cost_estimate=FREE,
    )(pieces[0], *got, *earlier)
    step = PLANE
    while step < lax.axis_size("dp"):
        total = total + swap(total, "dp", step)
        step *= 2
    return total.astype(BF16)


def send_pieces(pieces):
    return [swap(pieces[k], "tensor", k) for k in range(1, len(pieces))]


def relative_lanes(v, where_me, bits, block):
    width = v.shape[-1]
    spot = lax.broadcasted_iota(jnp.int32, v.shape, 1) // block
    for b in range(bits):
        shift = block << b
        right, left = pltpu.roll(v, shift, 1), pltpu.roll(v, width - shift, 1)
        flipped = jnp.where(((spot >> b) & 1) == 1, right, left)
        v = jnp.where(((where_me >> b) & 1) == 1, flipped, v)
    return v


def bias_kernel(place_ref, *refs):
    sources, (stack_ref, bq_ref, bv_ref, bh_ref) = refs[:4], refs[-4:]
    core, chip = place_ref[0], place_ref[1]
    rows = sources[0].shape[0] - 16
    width = bq_ref.shape[1]
    group = width // 4
    hidden, heads = [], []
    for k, ref in enumerate(sources):
        if k > 0:
            stack_ref[k - 1] = ref[:rows]
        tail = ref[rows : rows + 16].astype(F32)
        hidden.append(tail[0:1] + tail[1:2])
        heads.append(tail[2:3] + tail[3:4])
    hidden = jnp.concatenate(hidden + hidden, axis=0)
    hidden = relative_lanes(hidden, core * 4 + chip, 3, hidden.shape[1] // PLANE)
    half = hidden.shape[1] // 2
    for s in range(4):
        bh_ref[0:1, s * half : (s + 1) * half] = hidden[s : s + 1, :half]
        bh_ref[1:2, s * half : (s + 1) * half] = hidden[s : s + 1, half:]
    for k, out in enumerate((bq_ref, bv_ref)):
        row = jnp.concatenate([h[:, k * group : (k + 1) * group] for h in heads], axis=1)
        row = jnp.broadcast_to(row, (8, width))
        out[...] = relative_lanes(row, chip, 2, HD // 4)[0:1]


def stack_and_biases(where, sources, width, hidden, earlier):
    vmem = pl.BlockSpec(memory_space=pltpu.VMEM)
    rows = sources[0].shape[0] - 16
    return pl.pallas_call(
        bias_kernel,
        in_specs=[pl.BlockSpec(memory_space=pltpu.SMEM)]
        + [vmem] * 4
        + [pl.BlockSpec(memory_space=pl.ANY)] * len(earlier),
        out_specs=[vmem] * 4,
        out_shape=[
            jax.ShapeDtypeStruct((len(sources) - 1, rows, width), BF16),
            jax.ShapeDtypeStruct((1, width), F32),
            jax.ShapeDtypeStruct((1, width), F32),
            jax.ShapeDtypeStruct((2, 2 * hidden), F32),
        ],
        compiler_params=pltpu.CompilerParams(vmem_limit_bytes=6 * MIB),
        cost_estimate=FREE,
    )(where, *sources, *earlier)


def qkv_kernel(place_ref, own, other, x_ref, xo_ref, bq_ref, bv_ref, *refs):
    outs, scratch, sem, out_sem = refs[:7], refs[7:14], refs[14], refs[15]
    (q_ref, k_ref, v_ref), weights = scratch[:3], scratch[3:]
    core = place_ref[0]
    rows, width = x_ref.shape

    def copies(src, group):
        return [
            pltpu.make_async_copy(
                src.at[j, :, m], weights[2 * group + m].at[:, :, j], sem.at[group, m, j]
            )
            for m in range(2)
            for j in range(4)
        ]

    for group in (0, 1):

        @pl.when(core == group)
        def _():
            for copy in copies(own, group):
                copy.start()

        @pl.when(core != group)
        def _():
            for copy in copies(other, group):
                copy.start()

    def landed(group):
        @pl.when(core == group)
        def _():
            for copy in copies(own, group):
                copy.wait()

        @pl.when(core != group)
        def _():
            for copy in copies(other, group):
                copy.wait()

    leaving = [pltpu.make_async_copy(scratch[k], outs[k], out_sem.at[k]) for k in range(7)]
    landed(0)
    leaving[3].start()
    leaving[4].start()
    x, xo = x_ref[...], xo_ref[...]
    q_ref[...] = (dot_nt(x, weights[0][...].reshape(width, width)) + bq_ref[...]).astype(BF16)
    leaving[0].start()
    w = weights[1][...].reshape(width, width)
    k_ref[:rows] = dot_nt(x, w).astype(BF16)
    k_ref[rows:] = dot_nt(xo, w).astype(BF16)
    leaving[1].start()
    landed(1)
    leaving[5].start()
    leaving[6].start()
    w = weights[2][...].reshape(width, width)
    v_ref[:rows] = (dot_nt(x, w) + bv_ref[...]).astype(BF16)
    v_ref[rows:] = (dot_nt(xo, w) + bv_ref[...]).astype(BF16)
    leaving[2].start()
    for copy in leaving:
        copy.wait()


def project(where, own, other, x, xo, bq, bv):
    rows, width = x.shape
    _, shards, _, heads, part, _ = own.shape
    vmem, hbm = pl.BlockSpec(memory_space=pltpu.VMEM), pl.BlockSpec(memory_space=pltpu.HBM)
    space = pl.BlockSpec(memory_space=pl.ANY)
    shapes = [(rows, width), (2 * rows, width), (2 * rows, width)]
    shapes += [(shards, heads, 4, part, width)] * 4
    return pl.pallas_call(
        qkv_kernel,
        in_specs=[pl.BlockSpec(memory_space=pltpu.SMEM), space, space] + [vmem] * 4,
        out_specs=[hbm] * 7,
        out_shape=[jax.ShapeDtypeStruct(shape, BF16) for shape in shapes],
        scratch_shapes=[pltpu.VMEM(shape, BF16) for shape in shapes]
        + [pltpu.SemaphoreType.DMA((2, 2, 4)), pltpu.SemaphoreType.DMA((7,))],
        compiler_params=pltpu.CompilerParams(vmem_limit_bytes=18 * MIB),
        cost_estimate=FREE,
    )(where, own, other, x, xo, bq, bv)


def att_out_kernel(place_ref, own_ref, other_ref, gq_ref, gk_ref, gv_ref, go_ref, *sums):
    core, chip = place_ref[0], place_ref[1]
    head_cols, width = go_ref.shape
    heads, part = head_cols // HD, HD // 4
    extras = []
    for group in (0, 1):
        blocks = []
        for c in range(4):
            block = jnp.where(core == group, own_ref[c ^ chip], other_ref[c ^ chip])
            extras.append(block[:, width:])
            blocks.append(block)
        for m in range(2):
            pieces = [
                blocks[c][(m * heads + h) * part : (m * heads + h + 1) * part]
                for h in range(heads)
                for c in range(4)
            ]
            whole = jnp.concatenate(pieces, axis=0)
            (gq_ref, gk_ref, gv_ref, go_ref)[2 * group + m][...] = whole[:, :width].astype(F32)
            if m == 0:
                sums[group][...] = whole[:, width:].astype(F32).T[0]
    extras = jnp.concatenate(extras, axis=0).astype(F32).T
    for k in range(1, 8):
        sums[1 + k][...] = extras[k]


def att_outputs(where, own, other, head_cols, width):
    vmem = pl.BlockSpec(memory_space=pltpu.VMEM)
    weight = jax.ShapeDtypeStruct((head_cols, width), F32)
    vector = jax.ShapeDtypeStruct((width,), F32)
    few = jax.ShapeDtypeStruct((head_cols,), F32)
    return pl.pallas_call(
        att_out_kernel,
        in_specs=[pl.BlockSpec(memory_space=pltpu.SMEM), vmem, vmem],
        out_specs=[vmem] * 13,
        out_shape=[weight] * 4 + [few] * 2 + [vector] * 7,
        compiler_params=pltpu.CompilerParams(vmem_limit_bytes=14 * MIB),
    )(where, own, other)


def ffn_out_kernel(place_ref, own_ref, other_ref, back_ref, hid_ref):
    core, chip = place_ref[0], place_ref[1]
    rows = own_ref.shape[2]
    blocks = []
    for group in (0, 1):
        for c in range(4):
            block = jnp.where(core == group, own_ref[c ^ chip], other_ref[c ^ chip])
            spot = (group * 4 + c) * rows
            back_ref[spot : spot + rows] = block[0].astype(F32)
            blocks.append(block[1])
    hid_ref[...] = jnp.concatenate(blocks, axis=0).astype(F32).T


def ffn_outputs(where, own, other, hidden, width):
    vmem = pl.BlockSpec(memory_space=pltpu.VMEM)
    return pl.pallas_call(
        ffn_out_kernel,
        in_specs=[pl.BlockSpec(memory_space=pltpu.SMEM), vmem, vmem],
        out_specs=[vmem] * 2,
        out_shape=[
            jax.ShapeDtypeStruct((hidden, width), F32),
            jax.ShapeDtypeStruct((width, hidden), F32),
        ],
        compiler_params=pltpu.CompilerParams(vmem_limit_bytes=20 * MIB),
    )(where, own, other)


def live_keys(place_ref, keys, half_rows):
    spot = lax.broadcasted_iota(jnp.int32, (keys, 1), 0)
    first = place_ref[1]
    spot = jnp.where(spot < half_rows, spot + first, spot - first)
    return spot < place_ref[0]


def attend_kernel(place_ref, q_ref, k_ref, v_ref, *refs, half_rows):
    out_ref, lse_ref = refs[-2:]
    rows, keys = q_ref.shape[0], k_ref.shape[0]
    q = q_ref[...] * jnp.asarray(0.125, BF16)
    k = k_ref[...]
    v_turned = v_ref[...].T
    live = live_keys(place_ref, keys, half_rows)
    lane = lax.broadcasted_iota(jnp.int32, (rows, LANES), 1)
    outs, sums = [], []
    for h in range(LANES // HD):
        qh = jnp.where((lane // HD) == h, q, jnp.zeros_like(q))
        s = jnp.where(live, dot_nt(k, qh), -1e30)
        top = jnp.max(s, axis=0, keepdims=True)
        e = jnp.exp(s - top)
        total = jnp.sum(e, axis=0, keepdims=True)
        p = (e * (1.0 / total)).astype(BF16)
        outs.append(dot_nn(v_turned, p)[h * HD : (h + 1) * HD])
        sums.append(top + jnp.log(total))
    out_ref[...] = jnp.concatenate(outs, axis=0).T.astype(BF16)
    lse_ref[...] = jnp.concatenate(sums + [jnp.zeros((6, rows), F32)], axis=0)


def attend_back_kernel(
    place_ref, q_ref, k_ref, v_ref, lse_ref, do_ref, _, dq_ref, dk_ref, dv_ref, *, half_rows
):
    rows, keys = q_ref.shape[0], k_ref.shape[0]
    k, v, do = k_ref[...], v_ref[...], do_ref[...]
    q = q_ref[...] * jnp.asarray(0.125, BF16)
    k_turned = k.T
    live = live_keys(place_ref, keys, half_rows)
    lane = lax.broadcasted_iota(jnp.int32, (rows, LANES), 1)
    dqs, dks, dvs = [], [], []
    for h in range(LANES // HD):
        mine = (lane // HD) == h
        qh = jnp.where(mine, q, jnp.zeros_like(q))
        doh = jnp.where(mine, do, jnp.zeros_like(do))
        s = jnp.where(live, dot_nt(k, qh), -1e30)
        p = jnp.exp(s - lse_ref[h : h + 1, :])
        dp = dot_nt(v, doh)
        inner = jnp.sum(p * dp, axis=0, keepdims=True)
        ds = (p * (dp - inner)).astype(BF16)
        dqs.append(dot_nn(k_turned, ds)[h * HD : (h + 1) * HD])
        dks.append(dot_nn(ds, qh))
        dvs.append(dot_nn(p.astype(BF16), doh))
    dq_ref[...] = (jnp.concatenate(dqs, axis=0).T * 0.125).astype(BF16)
    dk_ref[...] = (dks[0] + dks[1]).astype(BF16)
    dv_ref[...] = (dvs[0] + dvs[1]).astype(BF16)


def attend(place, q, k, v, first, pairs, earlier):
    rows, width = q.shape[0], pairs * LANES
    keys = k.shape[0]
    q_spec = pl.BlockSpec((rows, LANES), lambda i: (0, i + first))
    k_spec = pl.BlockSpec((keys, LANES), lambda i: (0, i + first))
    out_spec = pl.BlockSpec((rows, LANES), lambda i: (0, i))
    lse_spec = pl.BlockSpec((8, rows), lambda i: (i, 0))
    return pl.pallas_call(
        functools.partial(attend_kernel, half_rows=rows),
        grid=(pairs,),
        in_specs=[
            pl.BlockSpec(memory_space=pltpu.SMEM),
            q_spec,
            k_spec,
            k_spec,
        ]
        + [pl.BlockSpec(memory_space=pl.ANY)] * len(earlier),
        out_specs=[out_spec, lse_spec],
        out_shape=[
            jax.ShapeDtypeStruct((rows, width), BF16),
            jax.ShapeDtypeStruct((8 * pairs, rows), F32),
        ],
        compiler_params=pltpu.CompilerParams(vmem_limit_bytes=10 * MIB),
        cost_estimate=FREE,
    )(place, q, k, v, *earlier)


def attend_back(place, q, k, v, lse, do, earlier):
    rows, width = q.shape
    keys = k.shape[0]
    q_spec = pl.BlockSpec((rows, LANES), lambda i: (0, i))
    k_spec = pl.BlockSpec((keys, LANES), lambda i: (0, i))
    lse_spec = pl.BlockSpec((8, rows), lambda i: (i, 0))
    return pl.pallas_call(
        functools.partial(attend_back_kernel, half_rows=rows),
        grid=(width // LANES,),
        in_specs=[
            pl.BlockSpec(memory_space=pltpu.SMEM),
            q_spec,
            k_spec,
            k_spec,
            lse_spec,
            q_spec,
            pl.BlockSpec(memory_space=pl.ANY),
        ],
        out_specs=[q_spec, k_spec, k_spec],
        out_shape=[
            jax.ShapeDtypeStruct((rows, width), BF16),
            jax.ShapeDtypeStruct((keys, width), BF16),
            jax.ShapeDtypeStruct((keys, width), BF16),
        ],
        compiler_params=pltpu.CompilerParams(vmem_limit_bytes=10 * MIB),
        cost_estimate=FREE,
    )(place, q, k, v, lse, do, earlier)


def weights_kernel(
    place_ref,
    dq_ref,
    dk_ref,
    dv_ref,
    context_ref,
    context_two_ref,
    ga_ref,
    x_ref,
    xo_ref,
    one_ref,
    two_ref,
    hid_ref,
    *refs,
):
    keep_ref, send_ref = refs[-2:]
    rows, width = dq_ref.shape
    shards = keep_ref.shape[1]
    group = width // shards
    heads = group // HD
    part = HD // 4
    core, chip = place_ref[0], place_ref[1]
    span = 2 * group
    lane = lax.broadcasted_iota(jnp.int32, (part, LANES), 1)
    spots = lax.broadcasted_iota(jnp.int32, (8, LANES), 0)
    spots = (spots == lax.broadcasted_iota(jnp.int32, (8, LANES), 1)).astype(BF16)
    att_rows = keep_ref.shape[2]
    half = 4 * att_rows
    whole = jnp.concatenate([jnp.zeros((2, width), F32), one_ref[...], two_ref[...]], axis=0)
    whole = relative_lanes(whole, core * 4 + chip, 3, att_rows)
    line = lax.broadcasted_iota(jnp.int32, (8, half), 0)
    extra = []
    for g in range(2):
        extra.append([])
        for s in range(shards):
            mine = hid_ref[g : g + 1, s * half : (s + 1) * half]
            mine = jnp.where(line == 1, mine, whole[:, g * half : (g + 1) * half])
            extra[g].append(dot_tn(mine.astype(BF16), spots))

    def put(which, m, left_ref, rights, with_sum):
        ones = jnp.ones((rows, LANES), BF16)
        for first in range(0, width, span):
            out, sums = None, None
            for k, right in enumerate(rights):
                if isinstance(left_ref, tuple):
                    left = left_ref[first // span][...]
                else:
                    left = left_ref[k * rows : (k + 1) * rows, first : first + span]
                more = dot_tn(left, right[...])
                out = more if out is None else out + more
                if with_sum:
                    more = dot_tn(left, ones)
                    sums = more if sums is None else sums + more

            def store(dst, base):
                for at in range(0, span, part):
                    row = first + at
                    shard, rest = row // group, row % group
                    head, j = rest // HD, (rest % HD) // part
                    spot = (m * heads + head) * part
                    dst[j, shard, spot : spot + part, :width] = out[at : at + part].astype(BF16)
                    tail = extra[base][shard][j * att_rows + spot : j * att_rows + spot + part]
                    if with_sum:
                        tail = jnp.where(lane == 0, sums[at : at + part], tail)
                    dst[j, shard, spot : spot + part, width:] = tail.astype(BF16)

            @pl.when(core == which)
            def _():
                store(keep_ref, 0)

            @pl.when(core != which)
            def _():
                store(send_ref, 1)

    put(0, 0, dq_ref, [x_ref], True)
    put(0, 1, dk_ref, [x_ref, xo_ref], False)
    put(1, 0, dv_ref, [x_ref, xo_ref], True)
    put(1, 1, (context_ref, context_two_ref), [ga_ref], False)


def attention_weight_grads(where, dq, dk, dv, contexts, ga, x, xo, sums, shards, earlier):
    width = dq.shape[1]
    full = jax.ShapeDtypeStruct((4, shards, width // (2 * shards), width + LANES), BF16)
    vmem = pl.BlockSpec(memory_space=pltpu.VMEM)
    return pl.pallas_call(
        weights_kernel,
        in_specs=[pl.BlockSpec(memory_space=pltpu.SMEM)] + [vmem] * 11 + [pl.BlockSpec(memory_space=pl.ANY)] * len(earlier),
        out_specs=[vmem, vmem],
        out_shape=[full, full],
        compiler_params=pltpu.CompilerParams(vmem_limit_bytes=22 * MIB),
        cost_estimate=FREE,
    )(where, dq, dk, dv, *contexts, ga, x, xo, *sums, *earlier)


def whole_call(kernel, outs, args, flops, earlier=()):
    vmem, space = pl.BlockSpec(memory_space=pltpu.VMEM), pl.BlockSpec(memory_space=pl.ANY)
    if earlier:
        inner, count = kernel, len(args)
        kernel = lambda *refs: inner(*refs[:count], *refs[count + len(earlier) :])
    return pl.pallas_call(
        kernel,
        in_specs=[vmem] * len(args) + [space] * len(earlier),
        out_specs=[vmem] * len(outs),
        out_shape=[jax.ShapeDtypeStruct(shape, dtype) for shape, dtype in outs],
        compiler_params=pltpu.CompilerParams(vmem_limit_bytes=22 * MIB),
        cost_estimate=FREE,
    )(*args, *earlier)


def normalize(z):
    center = z - jnp.mean(z, axis=-1, keepdims=True)
    spread = jnp.mean(center * center, axis=-1, keepdims=True)
    scale = lax.rsqrt(spread + 1e-05)
    return center * scale, scale


def norm_back(grad, zhat, scale, gain):
    e = grad * gain
    inner = jnp.mean(e * zhat, axis=-1, keepdims=True)
    return (e - jnp.mean(e, axis=-1, keepdims=True) - zhat * inner) * scale


def column_sums(v):
    return jnp.sum(v, axis=0, keepdims=True)


def mid_kernel(
    context_ref,
    context_two_ref,
    wo_ref,
    x_ref,
    b_ref,
    gain_ref,
    shift_ref,
    mid_ref,
    zhat_ref,
    scale_ref,
):
    half = context_ref.shape[1]
    z = dot_nn(context_ref[...], wo_ref[:half]) + dot_nn(context_two_ref[...], wo_ref[half:])
    z = z + b_ref[...] + x_ref[...].astype(F32)
    zhat, scale = normalize(z)
    mid_ref[...] = (zhat * gain_ref[...] + shift_ref[...]).astype(BF16)
    zhat_ref[...] = zhat
    scale_ref[...] = jnp.broadcast_to(scale, scale_ref.shape)


def hidden_kernel(mid_ref, w_ref, b_ref, act_ref, slope_ref):
    block = 512
    for first in range(0, w_ref.shape[0], block):
        cols = slice(first, first + block)
        act, slope = gelu_pair(dot_nt(mid_ref[...], w_ref[cols]) + b_ref[:, cols])
        act_ref[:, cols] = act.astype(BF16)
        slope_ref[:, cols] = slope.astype(BF16)


def branch_kernel(
    act_own_ref,
    act_other_ref,
    w_own_ref,
    w_other_ref,
    mid_ref,
    b_ref,
    gain_ref,
    shift_ref,
    cotangent_ref,
    out_ref,
    grad_ref,
    low_ref,
    sums_ref,
):
    z = dot_nn(act_own_ref[...], w_own_ref[...]) + dot_nn(act_other_ref[...], w_other_ref[...])
    zhat, scale = normalize(z + b_ref[...] + mid_ref[...].astype(F32))
    out_ref[...] = (zhat * gain_ref[...] + shift_ref[...]).astype(BF16)
    c = cotangent_ref[...].astype(F32)
    grad = norm_back(c, zhat, scale, gain_ref[...])
    low = grad.astype(BF16)
    grad_ref[...] = grad
    low_ref[...] = low
    sums_ref[...] = jnp.concatenate(
        [column_sums(low.astype(F32)), column_sums(c * zhat), column_sums(c)], axis=0
    )


def pair_grads_kernel(left_own_ref, left_other_ref, right_ref, keep_ref, send_ref):
    send_ref[...] = dot_tn(left_other_ref[...], right_ref[...]).astype(BF16)
    keep_ref[...] = dot_tn(left_own_ref[...], right_ref[...]).astype(BF16)


def input_kernel(
    dq_ref, dk_ref, dv_ref, wq_ref, wk_ref, wv_ref, first_ref, own_ref, other_ref
):
    rows = dq_ref.shape[0]
    total = dot_nn(dk_ref[rows:], wk_ref[...]) + dot_nn(dv_ref[rows:], wv_ref[...])
    other_ref[...] = total.astype(BF16)
    total = dot_nn(dk_ref[:rows], wk_ref[...]) + dot_nn(dv_ref[:rows], wv_ref[...])
    own_ref[...] = total + dot_nn(dq_ref[...], wq_ref[...]) + first_ref[...]


def pre_kernel(
    low_ref, w_own_ref, w_other_ref, slope_own_ref, slope_other_ref, own_ref, other_ref, sums_ref
):
    for k, (w, slope, out) in enumerate(
        ((w_own_ref, slope_own_ref, own_ref), (w_other_ref, slope_other_ref, other_ref))
    ):
        grad = (dot_nt(low_ref[...], w[...]) * slope[...].astype(F32)).astype(BF16)
        out[...] = grad
        sums_ref[k : k + 1] = column_sums(grad.astype(F32))


def first_kernel(
    pre_own_ref,
    pre_other_ref,
    w_own_ref,
    w_other_ref,
    grad_ref,
    zhat_ref,
    scale_ref,
    gain_ref,
    wo_ref,
    first_ref,
    low_ref,
    context_ref,
    sums_ref,
):
    grad = dot_nn(pre_own_ref[...], w_own_ref[...]) + dot_nn(pre_other_ref[...], w_other_ref[...])
    grad = grad + grad_ref[...]
    zhat = zhat_ref[...]
    first = norm_back(grad, zhat, scale_ref[:, :1], gain_ref[...])
    low = first.astype(BF16)
    first_ref[...] = first
    low_ref[...] = low
    context_ref[...] = dot_nt(low, wo_ref[...]).astype(BF16)
    sums_ref[...] = jnp.concatenate(
        [column_sums(low.astype(F32)), column_sums(grad * zhat), column_sums(grad)], axis=0
    )


def gelu_pair(v):
    cdf = 0.5 * (1.0 + lax.erf(v * (0.5**0.5)))
    density = jnp.exp(-0.5 * v * v) * 0.3989422804014327
    return v * cdf, cdf + v * density


def local(
    inputs,
    cotangent,
    lengths,
    w_query,
    w_key,
    w_value,
    b_query,
    b_value,
    w_output,
    b_output,
    gain_one,
    shift_one,
    w_hidden,
    b_hidden,
    w_back,
    b_back,
    gain_two,
    shift_two,
):
    rows, width = inputs.shape
    shards = lax.axis_size("tensor")
    head_cols = w_query.shape[1]
    hidden = w_hidden.shape[1]
    heads = head_cols // HD
    part = HD // 4
    ffn_rows = hidden // PLANE
    per_slot = shards // lengths.shape[0]
    assert per_slot == 2 and shards == 4 and lax.axis_size("dp") % PLANE == 0
    dp = lax.axis_index("dp")
    core = dp & 1
    chip = (((dp >> 2) & 1) << 1) | ((dp >> 1) & 1)
    me = core * 4 + chip
    t = lax.axis_index("tensor")

    where = jnp.stack([core, chip]).astype(jnp.int32)
    att_rows = 2 * heads * part
    far = pl.ds(1, shards - 1)

    by_head = (heads, 4, part, width)
    pair = [
        jnp.where(core == 0, w_query, w_value).T.reshape(by_head),
        jnp.where(core == 0, w_key.T, w_output).reshape(by_head),
    ]
    hid_near = lax.dynamic_slice_in_dim(w_hidden, core * (hidden // 2), hidden // 2, 1)
    hid_near = hid_near.T.reshape(4, ffn_rows, width)
    back_near = w_back.reshape(PLANE, ffn_rows, width)
    bias = jnp.pad(jnp.concatenate([b_query, b_value]), (0, width - 2 * head_cols))
    bias = jnp.stack([b_hidden, b_hidden, bias, bias])
    bias_high = lax.reduce_precision(bias, 8, 7)
    bias_rows = jnp.where(jnp.arange(4)[:, None] % 2 == 0, bias_high, bias - bias_high)
    bias_rows = jnp.pad(bias_rows.astype(BF16), ((0, 12), (0, 0)))

    def near_heads(j):
        return lambda core, chip: (slice(None), chip ^ j)

    def near_hid(j):
        return lambda core, chip: (chip ^ j,)

    def near_back(j):
        return lambda core, chip: (core * 4 + (chip ^ j),)

    ffn_send = pack(
        where,
        (2 * ffn_rows + 16, width),
        [
            (0, near_hid(0), (pl.ds(0, ffn_rows),)),
            (1, near_back(0), (pl.ds(ffn_rows, ffn_rows),)),
            (2, at(), (pl.ds(2 * ffn_rows, 16),)),
        ],
        [hid_near, back_near, bias_rows],
        (),
        2,
    )
    ffn_z = from_shards(ffn_send)
    att_send = pack(
        where, (2, heads, part, width), [(0, near_heads(0), (0,)), (1, near_heads(0), (1,))], pair, (), 2
    )
    rows_send = pack(where, inputs.shape, [(0, at(), ())], [inputs], (), 1)
    ffn_stack, bq, bv, bh = stack_and_biases(where, [ffn_send] + ffn_z, width, hidden, ())
    ffn_xy = swap(ffn_stack, "dp", XBIT), swap(ffn_stack, "dp", YBIT)
    att_z = from_shards(after(att_send.reshape(att_rows, width), *ffn_z))
    rows_other = swap(after(rows_send, *att_z), "tensor", 1)
    att_stack = stacked(where, att_z, att_rows, ())

    att_far = halves_from_chips(where, att_stack, list(ffn_xy))
    shape = (4, shards, 2, heads, part, width)
    moves = [(m, near_heads(j), (j, 0, m)) for j in range(4) for m in range(2)]
    moves += [(2 + j, at(), (j, far)) for j in range(3)]
    moves += [(5 + m, at(), (3, far, m)) for m in range(2)]
    att_far = [v.reshape(shards - 1, -1, heads, part, width) for v in att_far[:3]] + [
        v.reshape(shards - 1, heads, part, width) for v in att_far[3:]
    ]
    att_own = pack(where, shape, moves, pair + att_far, (rows_other,), 2)
    att_swap = swap(att_own, "dp", CORE)

    def ffn_half(near, near_index, first, diagonal, earlier):
        mine = pl.ds(first, ffn_rows)
        moves = [(0, near_index(j), (0, j)) for j in range(4)]
        moves += [(1 + j, at(every, mine), (far, j)) for j in range(3)]
        moves += [(4, at(), (far, 3))]
        own = pack(
            where,
            (shards, 4, ffn_rows, width),
            moves,
            [near] + ffn_far[:3] + [diagonal],
            earlier,
            1,
        )
        own = own.reshape(-1, width)
        return own, swap(own, "dp", CORE)

    every = slice(None)
    ffn_far, ffn_sent = halves_from_chips(where, ffn_stack, [], True, ffn_xy)
    queries, key_rows, values, wq, wk, wv, wo = project(
        where, att_own, att_swap, inputs, rows_other, bq, bv
    )
    wq, wk, wv, wo = (w.reshape(shards * head_cols, width) for w in (wq, wk, wv, wo))
    place = jnp.stack([lengths[t // per_slot], (t % per_slot) * rows]).astype(jnp.int32)
    pairs = width // LANES // 2
    context_one, logsum_one = attend(place, queries, key_rows, values, 0, pairs, [])
    context_two, logsum_two = attend(place, queries, key_rows, values, pairs, pairs, [context_one])
    logsum = jnp.concatenate([logsum_one, logsum_two], axis=0)
    contexts = (context_one, context_two)
    hid_own, hid_swap = ffn_half(hid_near, near_hid, 0, ffn_far[3], [context_one])
    back_own, back_swap = ffn_half(back_near, near_back, ffn_rows, ffn_far[4], [context_one])
    full, low = ((rows, width), F32), ((rows, width), BF16)
    half_low = ((rows, 2 * hidden), BF16)
    three = ((3, width), F32)
    mid, zhat_one, scale_one = whole_call(
        mid_kernel,
        [low, full, ((rows, LANES), F32)],
        (*contexts, wo, inputs, b_output[None], gain_one[None], shift_one[None]),
        2 * 10**8,
    )
    act_own, slope_own = whole_call(
        hidden_kernel, [half_low, half_low], (mid, hid_own, bh[:1]), 10**9
    )
    act_swap, slope_swap = whole_call(
        hidden_kernel, [half_low, half_low], (mid, hid_swap, bh[1:]), 10**9
    )
    outputs, grad_second, grad_branch, sums_two = whole_call(
        branch_kernel,
        [low, full, low, three],
        (
            act_own,
            act_swap,
            back_own,
            back_swap,
            mid,
            b_back[None],
            gain_two[None],
            shift_two[None],
            cotangent,
        ),
        3 * 10**9,
    )

    two = shards // 2
    low_half, high_half = pl.ds(0, two), pl.ds(two, shards - two)
    each = [(k,) for k in range(shards)]

    def first_step(keep, got, picks, earlier):
        a_keep, a_send, b_keep, b_send = fold(where, [(keep, got, picks)], earlier)
        return a_keep, b_keep, swap(a_send, "dp", XBIT), swap(b_send, "dp", YBIT), a_send

    def second_step(step, a_picks, b_picks, earlier):
        a_keep, b_keep, a_got, b_got, _ = step
        a_keep, a_send, b_keep, b_send = fold(
            where, [(a_keep, a_got, a_picks), (b_keep, b_got, b_picks)], earlier
        )
        return a_keep, b_keep, swap(a_send, "dp", YBIT), swap(b_send, "dp", XBIT), a_send

    def third_step(step, earlier, beside=()):
        a_keep, b_keep, a_got, b_got, _ = step
        groups = [(a_keep, a_got, each[:two]), (b_keep, b_got, each[: shards - two])]
        return fold(where, groups, earlier, beside)

    quarter = (shards, 2, 2, ffn_rows, width)
    ffn_picks = [
        (low_half, every, 0),
        (low_half, every, 1),
        (high_half, 0),
        (high_half, 1),
    ]
    ffn_again = [(every, 0), (every, 1)]
    pair_out = [((2 * hidden, width), BF16)] * 2
    back_keep, back_send = whole_call(
        pair_grads_kernel, pair_out, (act_own, act_swap, grad_branch), 10**9
    )
    back_got = swap(back_send, "dp", CORE)
    pre_own, pre_swap, grad_b_hidden = whole_call(
        pre_kernel,
        [half_low, half_low, ((2, 2 * hidden), F32)],
        (grad_branch, back_own, back_swap, slope_own, slope_swap),
        10**9,
    )
    back_step = first_step(back_keep.reshape(quarter), back_got.reshape(quarter), ffn_picks, ())
    hid_keep, hid_send = whole_call(
        pair_grads_kernel, pair_out, (pre_own, pre_swap, mid), 3 * 10**8, (back_step[4],)
    )
    hid_got = swap(hid_send, "dp", CORE)
    grad_first, grad_attn, grad_context, sums_one = whole_call(
        first_kernel,
        [full, low, low, three],
        (
            pre_own,
            pre_swap,
            hid_own,
            hid_swap,
            grad_second,
            zhat_one,
            scale_one,
            gain_one[None],
            wo,
        ),
        3 * 10**8,
        (hid_send,),
    )
    hid_step = first_step(
        hid_keep.reshape(quarter), hid_got.reshape(quarter), ffn_picks, (grad_first,)
    )
    grad_queries, grad_keys, grad_values = attend_back(
        place, queries, key_rows, values, logsum, grad_context, hid_step[4]
    )
    total, returned_send = whole_call(
        input_kernel,
        [full, low],
        (grad_queries, grad_keys, grad_values, wq, wk, wv, grad_first),
        3 * 10**8,
    )
    returned = swap(returned_send, "tensor", 1)
    back_step = second_step(back_step, ffn_again, ffn_again, (grad_queries,))
    att_keep, att_send = attention_weight_grads(
        where,
        grad_queries,
        grad_keys,
        grad_values,
        contexts,
        grad_attn,
        inputs,
        rows_other,
        (sums_one, sums_two, grad_b_hidden),
        shards,
        (back_step[4],),
    )
    wide = att_keep.shape[-1]

    back_pieces = third_step(back_step, (att_keep, returned))
    back_got = send_pieces(back_pieces)
    hid_step = second_step(hid_step, ffn_again, ffn_again, (back_pieces[0],))
    att_got = swap(att_send, "dp", CORE)
    att_shape = (2, 2) + att_keep.shape[1:]
    att_picks = [
        (every, 0, low_half),
        (every, 1, low_half),
        (0, every, high_half),
        (1, every, high_half),
    ]
    att_step = first_step(
        att_keep.reshape(att_shape), att_got.reshape(att_shape), att_picks, ()
    )
    hid_pieces = third_step(hid_step, ())
    back_sum = shards_reduce(back_pieces, back_got, ())
    hid_got = send_pieces(hid_pieces)
    att_step = second_step(att_step, [(0,), (1,)], [(0,), (1,)], (back_sum,))
    hid_sum = shards_reduce(hid_pieces, hid_got)
    att_pieces = third_step(att_step, (hid_sum,))
    att_got = send_pieces(att_pieces)
    top = pl.ds(0, ffn_rows)
    ffn_sum = pack(
        where,
        (2, ffn_rows, width),
        [(0, at(top), (0,)), (1, at(top), (1,))],
        [back_sum, hid_sum],
        (),
    )
    att_sum = shards_reduce(att_pieces, att_got)
    input_grad = (total + returned.astype(F32)).astype(BF16)
    att_far = from_chips(att_sum)
    ffn_far = halves_from_chips(where, ffn_sum, [att_sum])
    halves = [pl.ds(0, ffn_rows // 2), pl.ds(ffn_rows // 2, ffn_rows // 2)]
    moves = [(j, at(), (j,)) for j in range(3)]
    moves += [(3 + k, at(), (3, slice(None), halves[k])) for k in range(2)]
    ffn_out = pack(where, (4, 2, ffn_rows, width), moves, ffn_far, ())
    back_out, hid_out = ffn_outputs(where, ffn_out, swap(ffn_out, "dp", CORE), hidden, width)
    att_out = stacked(where, att_far, att_rows, (back_out,))
    gq, gk, gv, go, sum_q, sum_v, sum_hid, *vectors = att_outputs(
        where, att_out, swap(att_out, "dp", CORE), head_cols, width
    )
    return (
        outputs,
        input_grad,
        gq.T,
        gk.T,
        gv.T,
        sum_q,
        sum_v,
        go,
        vectors[0],
        vectors[1],
        vectors[2],
        hid_out,
        sum_hid,
        back_out,
        vectors[3],
        vectors[4],
        vectors[5],
    )


def solution(mesh):
    rows = P(("dp", "tensor"), None)
    columns, depth, vector = P(None, "tensor"), P("tensor", None), P("tensor")
    return jax.shard_map(
        local,
        mesh=mesh,
        in_specs=(
            rows,
            rows,
            P("dp"),
            columns,
            columns,
            columns,
            vector,
            vector,
            depth,
            P(),
            P(),
            P(),
            columns,
            vector,
            depth,
            P(),
            P(),
            P(),
        ),
        out_specs=(
            rows,
            rows,
            columns,
            columns,
            columns,
            vector,
            vector,
            depth,
            P(),
            P(),
            P(),
            columns,
            vector,
            depth,
            P(),
            P(),
            P(),
        ),
        check_vma=False,
    )
```

```python
import functools

import jax
import jax.numpy as jnp
from jax import lax
from jax.experimental import pallas as pl
from jax.experimental.pallas import tpu as pltpu
from jax.sharding import PartitionSpec as P

HD = 64
LANES = 128
PLANE = 8
CORE, XBIT, YBIT = 1, 2, 4
BF16, F32 = jnp.bfloat16, jnp.float32
MIB = 1024 * 1024
FREE = pl.CostEstimate(flops=1, bytes_accessed=1, transcendentals=0)


def dot_nn(a, b):
    return lax.dot_general(a, b, (((1,), (0,)), ((), ())), preferred_element_type=F32)


def dot_nt(a, b):
    return lax.dot_general(a, b, (((1,), (1,)), ((), ())), preferred_element_type=F32)


def dot_tn(a, b):
    return lax.dot_general(a, b, (((0,), (0,)), ((), ())), preferred_element_type=F32)


def swap(v, axis, bit):
    count = lax.axis_size(axis)
    return lax.ppermute(v, axis, [(i, i ^ bit) for i in range(count)])


def pack_kernel(plan, far, place_ref, *refs):
    outs, sem = refs[len(refs) - len(plan) - 1 : -1], refs[-1]
    core, chip = place_ref[0], place_ref[1]
    copies = []
    for out_ref, moves in zip(outs, plan):
        for which, source, target in moves:
            if which < far:
                src, dst = refs[which].at[source(core, chip)], out_ref.at[target]
                copies.append(pltpu.make_async_copy(src, dst, sem.at[len(copies)]))
    for copy in copies:
        copy.start()
    for out_ref, moves in zip(outs, plan):
        for which, source, target in moves:
            if which >= far:
                out_ref[target or ...] = refs[which][source(core, chip) or ...]
    for copy in copies:
        copy.wait()


def packs(where, shapes, plan, arrays, earlier=(), far=0):
    vmem, space = pl.BlockSpec(memory_space=pltpu.VMEM), pl.BlockSpec(memory_space=pl.ANY)
    count = sum(which < far for moves in plan for which, _, _ in moves)
    return pl.pallas_call(
        functools.partial(pack_kernel, plan, far),
        in_specs=[pl.BlockSpec(memory_space=pltpu.SMEM)]
        + [pl.BlockSpec(memory_space=pltpu.HBM)] * far
        + [vmem] * (len(arrays) - far)
        + [space] * len(earlier),
        out_specs=[vmem] * len(shapes),
        out_shape=[jax.ShapeDtypeStruct(shape, BF16) for shape in shapes],
        scratch_shapes=[pltpu.SemaphoreType.DMA((max(count, 1),))],
        compiler_params=pltpu.CompilerParams(vmem_limit_bytes=10 * MIB),
        cost_estimate=FREE,
    )(where, *arrays, *earlier)


def pack(where, shape, moves, arrays, earlier=(), far=0):
    return packs(where, [shape], [moves], arrays, earlier, far)[0]


def nothing_kernel(*refs):
    del refs


def after(v, *earlier):
    space = pl.BlockSpec(memory_space=pl.ANY)
    return pl.pallas_call(
        nothing_kernel,
        in_specs=[space] * (1 + len(earlier)),
        out_specs=space,
        out_shape=jax.ShapeDtypeStruct(v.shape, v.dtype),
        input_output_aliases={0: 0},
    )(v, *earlier)


def fold_kernel(plan, beside, place_ref, *refs):
    del place_ref
    count = sum(len(picks) for picks in plan)
    outs = refs[len(refs) - count :]
    others = refs[2 * len(plan) : 2 * len(plan) + beside]
    spot = 0
    for k, picks in enumerate(plan):
        for pick in picks:
            total = refs[2 * k][pick].astype(F32) + refs[2 * k + 1][pick].astype(F32)
            if beside:
                outs[spot][0] = others[spot][...]
                outs[spot][1] = total.astype(BF16)
            else:
                outs[spot][...] = total.astype(BF16)
            spot += 1


def fold(where, groups, earlier=(), beside=()):
    vmem, space = pl.BlockSpec(memory_space=pltpu.VMEM), pl.BlockSpec(memory_space=pl.ANY)
    arrays = [v for a, b, _ in groups for v in (a, b)] + list(beside)
    outs = [
        jax.ShapeDtypeStruct(
            ((2,) if beside else ()) + jax.eval_shape(lambda v, p=pick: v[p], a).shape, BF16
        )
        for a, _, picks in groups
        for pick in picks
    ]
    return pl.pallas_call(
        functools.partial(fold_kernel, [picks for _, _, picks in groups], len(beside)),
        in_specs=[pl.BlockSpec(memory_space=pltpu.SMEM)]
        + [vmem] * len(arrays)
        + [space] * len(earlier),
        out_specs=[vmem] * len(outs),
        out_shape=outs,
        compiler_params=pltpu.CompilerParams(vmem_limit_bytes=14 * MIB),
        cost_estimate=FREE,
    )(where, *arrays, *earlier)


def sum_kernel(first_ref, a_ref, b_ref, c_ref, *refs):
    total = first_ref[...].astype(F32) + a_ref[...].astype(F32)
    total = total + b_ref[...].astype(F32) + c_ref[...].astype(F32)
    refs[-1][...] = total.astype(refs[-1].dtype)


def at(*index):
    return lambda core, chip: index


def stacked(where, arrays, rows, earlier=()):
    top = pl.ds(0, rows)
    moves = [(i, at(top), (i,)) for i in range(len(arrays))]
    return pack(where, (len(arrays), rows) + arrays[0].shape[1:], moves, arrays, earlier)


def from_shards(v):
    return [swap(v, "tensor", k) for k in range(1, lax.axis_size("tensor"))]


def halves_from_chips(where, v, between=(), sent=False, first=None):
    v_x, v_y = first or (swap(v, "dp", XBIT), swap(v, "dp", YBIT))
    half = v.shape[1] // 2
    low, high = (slice(None), pl.ds(0, half)), (slice(None), pl.ds(half, half))
    shape = (v.shape[0], half) + v.shape[2:]
    plan = [[(0, at(*low), ())], [(1, at(*high), ())]]
    on_y, on_x = packs(where, [shape, shape], plan, [v_x, v_y], between)
    got = [v, v_x, v_y, swap(on_y, "dp", YBIT), swap(on_x, "dp", XBIT)]
    return (got, [on_y, on_x]) if sent else got


def from_chips(v):
    return [v] + [swap(v, "dp", bits) for bits in (XBIT, YBIT, XBIT | YBIT)]


def shards_reduce(pieces, got, earlier=()):
    more = lax.axis_size("dp") > PLANE
    vmem, space = pl.BlockSpec(memory_space=pltpu.VMEM), pl.BlockSpec(memory_space=pl.ANY)
    total = pl.pallas_call(
        sum_kernel,
        in_specs=[vmem] * len(pieces) + [space] * len(earlier),
        out_specs=vmem,
        out_shape=jax.ShapeDtypeStruct(pieces[0].shape, F32 if more else BF16),
        compiler_params=pltpu.CompilerParams(vmem_limit_bytes=6 * MIB),
        cost_estimate=FREE,
    )(pieces[0], *got, *earlier)
    step = PLANE
    while step < lax.axis_size("dp"):
        total = total + swap(total, "dp", step)
        step *= 2
    return total.astype(BF16)


def send_pieces(pieces):
    return [swap(pieces[k], "tensor", k) for k in range(1, len(pieces))]


def relative_lanes(v, where_me, bits, block):
    width = v.shape[-1]
    spot = lax.broadcasted_iota(jnp.int32, v.shape, 1) // block
    for b in range(bits):
        shift = block << b
        right, left = pltpu.roll(v, shift, 1), pltpu.roll(v, width - shift, 1)
        flipped = jnp.where(((spot >> b) & 1) == 1, right, left)
        v = jnp.where(((where_me >> b) & 1) == 1, flipped, v)
    return v


def bias_kernel(place_ref, *refs):
    sources, (stack_ref, bq_ref, bv_ref, bh_ref) = refs[:4], refs[-4:]
    core, chip = place_ref[0], place_ref[1]
    rows = sources[0].shape[0] - 16
    width = bq_ref.shape[1]
    group = width // 4
    hidden, heads = [], []
    for k, ref in enumerate(sources):
        if k > 0:
            stack_ref[k - 1] = ref[:rows]
        tail = ref[rows : rows + 16].astype(F32)
        hidden.append(tail[0:1] + tail[1:2])
        heads.append(tail[2:3] + tail[3:4])
    hidden = jnp.concatenate(hidden + hidden, axis=0)
    hidden = relative_lanes(hidden, core * 4 + chip, 3, hidden.shape[1] // PLANE)
    half = hidden.shape[1] // 2
    for s in range(4):
        bh_ref[0:1, s * half : (s + 1) * half] = hidden[s : s + 1, :half]
        bh_ref[1:2, s * half : (s + 1) * half] = hidden[s : s + 1, half:]
    for k, out in enumerate((bq_ref, bv_ref)):
        row = jnp.concatenate([h[:, k * group : (k + 1) * group] for h in heads], axis=1)
        row = jnp.broadcast_to(row, (8, width))
        out[...] = relative_lanes(row, chip, 2, HD // 4)[0:1]


def stack_and_biases(where, sources, width, hidden, earlier):
    vmem = pl.BlockSpec(memory_space=pltpu.VMEM)
    rows = sources[0].shape[0] - 16
    return pl.pallas_call(
        bias_kernel,
        in_specs=[pl.BlockSpec(memory_space=pltpu.SMEM)]
        + [vmem] * 4
        + [pl.BlockSpec(memory_space=pl.ANY)] * len(earlier),
        out_specs=[vmem] * 4,
        out_shape=[
            jax.ShapeDtypeStruct((len(sources) - 1, rows, width), BF16),
            jax.ShapeDtypeStruct((1, width), F32),
            jax.ShapeDtypeStruct((1, width), F32),
            jax.ShapeDtypeStruct((2, 2 * hidden), F32),
        ],
        compiler_params=pltpu.CompilerParams(vmem_limit_bytes=6 * MIB),
        cost_estimate=FREE,
    )(where, *sources, *earlier)


def qkv_kernel(place_ref, own, other, x_ref, xo_ref, bq_ref, bv_ref, *refs):
    (q_ref, k_ref, v_ref), weights, sem = refs[:3], refs[3:7], refs[7]
    core = place_ref[0]
    rows, width = x_ref.shape

    def copies(src, group):
        return [
            pltpu.make_async_copy(
                src.at[j, :, m], weights[2 * group + m].at[:, :, j], sem.at[group, m, j]
            )
            for m in range(2)
            for j in range(4)
        ]

    for group in (0, 1):

        @pl.when(core == group)
        def _():
            for copy in copies(own, group):
                copy.start()

        @pl.when(core != group)
        def _():
            for copy in copies(other, group):
                copy.start()

    def landed(group):
        @pl.when(core == group)
        def _():
            for copy in copies(own, group):
                copy.wait()

        @pl.when(core != group)
        def _():
            for copy in copies(other, group):
                copy.wait()

    landed(0)
    x, xo = x_ref[...], xo_ref[...]
    q_ref[...] = (dot_nt(x, weights[0][...].reshape(width, width)) + bq_ref[...]).astype(BF16)
    w = weights[1][...].reshape(width, width)
    k_ref[:rows] = dot_nt(x, w).astype(BF16)
    k_ref[rows:] = dot_nt(xo, w).astype(BF16)
    landed(1)
    w = weights[2][...].reshape(width, width)
    v_ref[:rows] = (dot_nt(x, w) + bv_ref[...]).astype(BF16)
    v_ref[rows:] = (dot_nt(xo, w) + bv_ref[...]).astype(BF16)


def project(where, own, other, x, xo, bq, bv):
    rows, width = x.shape
    _, shards, _, heads, part, _ = own.shape
    vmem = pl.BlockSpec(memory_space=pltpu.VMEM)
    space = pl.BlockSpec(memory_space=pl.ANY)
    shapes = [(rows, width), (2 * rows, width), (2 * rows, width)]
    shapes += [(shards, heads, 4, part, width)] * 4
    return pl.pallas_call(
        qkv_kernel,
        in_specs=[pl.BlockSpec(memory_space=pltpu.SMEM), space, space] + [vmem] * 4,
        out_specs=[vmem] * 7,
        out_shape=[jax.ShapeDtypeStruct(shape, BF16) for shape in shapes],
        scratch_shapes=[pltpu.SemaphoreType.DMA((2, 2, 4))],
        compiler_params=pltpu.CompilerParams(vmem_limit_bytes=18 * MIB),
        cost_estimate=FREE,
    )(where, own, other, x, xo, bq, bv)


def att_out_kernel(place_ref, own_ref, other_ref, gq_ref, gk_ref, gv_ref, go_ref, *sums):
    core, chip = place_ref[0], place_ref[1]
    head_cols, width = go_ref.shape
    heads, part = head_cols // HD, HD // 4
    extras = []
    for group in (0, 1):
        blocks = []
        for c in range(4):
            block = jnp.where(core == group, own_ref[c ^ chip], other_ref[c ^ chip])
            extras.append(block[:, width:])
            blocks.append(block)
        for m in range(2):
            pieces = [
                blocks[c][(m * heads + h) * part : (m * heads + h + 1) * part]
                for h in range(heads)
                for c in range(4)
            ]
            whole = jnp.concatenate(pieces, axis=0)
            (gq_ref, gk_ref, gv_ref, go_ref)[2 * group + m][...] = whole[:, :width].astype(F32)
            if m == 0:
                sums[group][...] = whole[:, width:].astype(F32).T[0]
    extras = jnp.concatenate(extras, axis=0).astype(F32).T
    for k in range(1, 8):
        sums[1 + k][...] = extras[k]


def att_outputs(where, own, other, head_cols, width):
    vmem = pl.BlockSpec(memory_space=pltpu.VMEM)
    weight = jax.ShapeDtypeStruct((head_cols, width), F32)
    vector = jax.ShapeDtypeStruct((width,), F32)
    few = jax.ShapeDtypeStruct((head_cols,), F32)
    return pl.pallas_call(
        att_out_kernel,
        in_specs=[pl.BlockSpec(memory_space=pltpu.SMEM), vmem, vmem],
        out_specs=[vmem] * 13,
        out_shape=[weight] * 4 + [few] * 2 + [vector] * 7,
        compiler_params=pltpu.CompilerParams(vmem_limit_bytes=14 * MIB),
    )(where, own, other)


def ffn_out_kernel(place_ref, own_ref, other_ref, back_ref, hid_ref):
    core, chip = place_ref[0], place_ref[1]
    rows = own_ref.shape[2]
    blocks = []
    for group in (0, 1):
        for c in range(4):
            block = jnp.where(core == group, own_ref[c ^ chip], other_ref[c ^ chip])
            spot = (group * 4 + c) * rows
            back_ref[spot : spot + rows] = block[0].astype(F32)
            blocks.append(block[1])
    hid_ref[...] = jnp.concatenate(blocks, axis=0).astype(F32).T


def ffn_outputs(where, own, other, hidden, width):
    vmem = pl.BlockSpec(memory_space=pltpu.VMEM)
    return pl.pallas_call(
        ffn_out_kernel,
        in_specs=[pl.BlockSpec(memory_space=pltpu.SMEM), vmem, vmem],
        out_specs=[vmem] * 2,
        out_shape=[
            jax.ShapeDtypeStruct((hidden, width), F32),
            jax.ShapeDtypeStruct((width, hidden), F32),
        ],
        compiler_params=pltpu.CompilerParams(vmem_limit_bytes=58 * MIB),
    )(where, own, other)


def live_keys(place_ref, keys, half_rows):
    spot = lax.broadcasted_iota(jnp.int32, (keys, 1), 0)
    first = place_ref[1]
    spot = jnp.where(spot < half_rows, spot + first, spot - first)
    return spot < place_ref[0]


def attend_kernel(place_ref, q_ref, k_ref, v_ref, *refs, half_rows):
    out_ref, lse_ref = refs[-2:]
    rows, keys = q_ref.shape[0], k_ref.shape[0]
    q = q_ref[...] * jnp.asarray(0.125, BF16)
    k = k_ref[...]
    v_turned = v_ref[...].T
    live = live_keys(place_ref, keys, half_rows)
    lane = lax.broadcasted_iota(jnp.int32, (rows, LANES), 1)
    outs, sums = [], []
    for h in range(LANES // HD):
        qh = jnp.where((lane // HD) == h, q, jnp.zeros_like(q))
        s = jnp.where(live, dot_nt(k, qh), -1e30)
        top = jnp.max(s, axis=0, keepdims=True)
        e = jnp.exp(s - top)
        total = jnp.sum(e, axis=0, keepdims=True)
        p = (e * (1.0 / total)).astype(BF16)
        outs.append(dot_nn(v_turned, p)[h * HD : (h + 1) * HD])
        sums.append(top + jnp.log(total))
    out_ref[...] = jnp.concatenate(outs, axis=0).T.astype(BF16)
    lse_ref[...] = jnp.concatenate(sums + [jnp.zeros((6, rows), F32)], axis=0)


def attend_back_kernel(
    place_ref, q_ref, k_ref, v_ref, lse_ref, do_ref, _, dq_ref, dk_ref, dv_ref, *, half_rows
):
    rows, keys = q_ref.shape[0], k_ref.shape[0]
    k, v, do = k_ref[...], v_ref[...], do_ref[...]
    q = q_ref[...] * jnp.asarray(0.125, BF16)
    k_turned = k.T
    live = live_keys(place_ref, keys, half_rows)
    lane = lax.broadcasted_iota(jnp.int32, (rows, LANES), 1)
    dqs, dks, dvs = [], [], []
    for h in range(LANES // HD):
        mine = (lane // HD) == h
        qh = jnp.where(mine, q, jnp.zeros_like(q))
        doh = jnp.where(mine, do, jnp.zeros_like(do))
        s = jnp.where(live, dot_nt(k, qh), -1e30)
        p = jnp.exp(s - lse_ref[h : h + 1, :])
        dp = dot_nt(v, doh)
        inner = jnp.sum(p * dp, axis=0, keepdims=True)
        ds = (p * (dp - inner)).astype(BF16)
        dqs.append(dot_nn(k_turned, ds)[h * HD : (h + 1) * HD])
        dks.append(dot_nn(ds, qh))
        dvs.append(dot_nn(p.astype(BF16), doh))
    dq_ref[...] = (jnp.concatenate(dqs, axis=0).T * 0.125).astype(BF16)
    dk_ref[...] = (dks[0] + dks[1]).astype(BF16)
    dv_ref[...] = (dvs[0] + dvs[1]).astype(BF16)


def attend(place, q, k, v, first, pairs, earlier):
    rows, width = q.shape[0], pairs * LANES
    keys = k.shape[0]
    q_spec = pl.BlockSpec((rows, LANES), lambda i: (0, i + first))
    k_spec = pl.BlockSpec((keys, LANES), lambda i: (0, i + first))
    out_spec = pl.BlockSpec((rows, LANES), lambda i: (0, i))
    lse_spec = pl.BlockSpec((8, rows), lambda i: (i, 0))
    return pl.pallas_call(
        functools.partial(attend_kernel, half_rows=rows),
        grid=(pairs,),
        in_specs=[
            pl.BlockSpec(memory_space=pltpu.SMEM),
            q_spec,
            k_spec,
            k_spec,
        ]
        + [pl.BlockSpec(memory_space=pl.ANY)] * len(earlier),
        out_specs=[out_spec, lse_spec],
        out_shape=[
            jax.ShapeDtypeStruct((rows, width), BF16),
            jax.ShapeDtypeStruct((8 * pairs, rows), F32),
        ],
        compiler_params=pltpu.CompilerParams(vmem_limit_bytes=10 * MIB),
        cost_estimate=FREE,
    )(place, q, k, v, *earlier)


def attend_back(place, q, k, v, lse, do, earlier):
    rows, width = q.shape
    keys = k.shape[0]
    q_spec = pl.BlockSpec((rows, LANES), lambda i: (0, i))
    k_spec = pl.BlockSpec((keys, LANES), lambda i: (0, i))
    lse_spec = pl.BlockSpec((8, rows), lambda i: (i, 0))
    return pl.pallas_call(
        functools.partial(attend_back_kernel, half_rows=rows),
        grid=(width // LANES,),
        in_specs=[
            pl.BlockSpec(memory_space=pltpu.SMEM),
            q_spec,
            k_spec,
            k_spec,
            lse_spec,
            q_spec,
            pl.BlockSpec(memory_space=pl.ANY),
        ],
        out_specs=[q_spec, k_spec, k_spec],
        out_shape=[
            jax.ShapeDtypeStruct((rows, width), BF16),
            jax.ShapeDtypeStruct((keys, width), BF16),
            jax.ShapeDtypeStruct((keys, width), BF16),
        ],
        compiler_params=pltpu.CompilerParams(vmem_limit_bytes=10 * MIB),
        cost_estimate=FREE,
    )(place, q, k, v, lse, do, earlier)


def weights_kernel(
    place_ref,
    dq_ref,
    dk_ref,
    dv_ref,
    context_ref,
    context_two_ref,
    ga_ref,
    x_ref,
    xo_ref,
    one_ref,
    two_ref,
    hid_ref,
    *refs,
):
    keep_ref, send_ref = refs[-2:]
    rows, width = dq_ref.shape
    shards = keep_ref.shape[1]
    group = width // shards
    heads = group // HD
    part = HD // 4
    core, chip = place_ref[0], place_ref[1]
    span = 2 * group
    lane = lax.broadcasted_iota(jnp.int32, (part, LANES), 1)
    spots = lax.broadcasted_iota(jnp.int32, (8, LANES), 0)
    spots = (spots == lax.broadcasted_iota(jnp.int32, (8, LANES), 1)).astype(BF16)
    att_rows = keep_ref.shape[2]
    half = 4 * att_rows
    whole = jnp.concatenate([jnp.zeros((2, width), F32), one_ref[...], two_ref[...]], axis=0)
    whole = relative_lanes(whole, core * 4 + chip, 3, att_rows)
    line = lax.broadcasted_iota(jnp.int32, (8, half), 0)
    extra = []
    for g in range(2):
        extra.append([])
        for s in range(shards):
            mine = hid_ref[g : g + 1, s * half : (s + 1) * half]
            mine = jnp.where(line == 1, mine, whole[:, g * half : (g + 1) * half])
            extra[g].append(dot_tn(mine.astype(BF16), spots))

    def put(which, m, left_ref, rights, with_sum):
        ones = jnp.ones((rows, LANES), BF16)
        for first in range(0, width, span):
            out, sums = None, None
            for k, right in enumerate(rights):
                if isinstance(left_ref, tuple):
                    left = left_ref[first // span][...]
                else:
                    left = left_ref[k * rows : (k + 1) * rows, first : first + span]
                more = dot_tn(left, right[...])
                out = more if out is None else out + more
                if with_sum:
                    more = dot_tn(left, ones)
                    sums = more if sums is None else sums + more

            def store(dst, base):
                for at in range(0, span, part):
                    row = first + at
                    shard, rest = row // group, row % group
                    head, j = rest // HD, (rest % HD) // part
                    spot = (m * heads + head) * part
                    dst[j, shard, spot : spot + part, :width] = out[at : at + part].astype(BF16)
                    tail = extra[base][shard][j * att_rows + spot : j * att_rows + spot + part]
                    if with_sum:
                        tail = jnp.where(lane == 0, sums[at : at + part], tail)
                    dst[j, shard, spot : spot + part, width:] = tail.astype(BF16)

            @pl.when(core == which)
            def _():
                store(keep_ref, 0)

            @pl.when(core != which)
            def _():
                store(send_ref, 1)

    put(0, 0, dq_ref, [x_ref], True)
    put(0, 1, dk_ref, [x_ref, xo_ref], False)
    put(1, 0, dv_ref, [x_ref, xo_ref], True)
    put(1, 1, (context_ref, context_two_ref), [ga_ref], False)


def attention_weight_grads(where, dq, dk, dv, contexts, ga, x, xo, sums, shards, earlier):
    width = dq.shape[1]
    full = jax.ShapeDtypeStruct((4, shards, width // (2 * shards), width + LANES), BF16)
    vmem = pl.BlockSpec(memory_space=pltpu.VMEM)
    return pl.pallas_call(
        weights_kernel,
        in_specs=[pl.BlockSpec(memory_space=pltpu.SMEM)] + [vmem] * 11 + [pl.BlockSpec(memory_space=pl.ANY)] * len(earlier),
        out_specs=[vmem, vmem],
        out_shape=[full, full],
        compiler_params=pltpu.CompilerParams(vmem_limit_bytes=22 * MIB),
        cost_estimate=FREE,
    )(where, dq, dk, dv, *contexts, ga, x, xo, *sums, *earlier)


def whole_call(kernel, outs, args, flops, earlier=()):
    vmem, space = pl.BlockSpec(memory_space=pltpu.VMEM), pl.BlockSpec(memory_space=pl.ANY)
    if earlier:
        inner, count = kernel, len(args)
        kernel = lambda *refs: inner(*refs[:count], *refs[count + len(earlier) :])
    return pl.pallas_call(
        kernel,
        in_specs=[vmem] * len(args) + [space] * len(earlier),
        out_specs=[vmem] * len(outs),
        out_shape=[jax.ShapeDtypeStruct(shape, dtype) for shape, dtype in outs],
        compiler_params=pltpu.CompilerParams(vmem_limit_bytes=22 * MIB),
        cost_estimate=FREE,
    )(*args, *earlier)


def normalize(z):
    center = z - jnp.mean(z, axis=-1, keepdims=True)
    spread = jnp.mean(center * center, axis=-1, keepdims=True)
    scale = lax.rsqrt(spread + 1e-05)
    return center * scale, scale


def norm_back(grad, zhat, scale, gain):
    e = grad * gain
    inner = jnp.mean(e * zhat, axis=-1, keepdims=True)
    return (e - jnp.mean(e, axis=-1, keepdims=True) - zhat * inner) * scale


def column_sums(v):
    return jnp.sum(v, axis=0, keepdims=True)


def mid_kernel(
    context_ref,
    context_two_ref,
    wo_ref,
    x_ref,
    b_ref,
    gain_ref,
    shift_ref,
    mid_ref,
    zhat_ref,
    scale_ref,
):
    half = context_ref.shape[1]
    z = dot_nn(context_ref[...], wo_ref[:half]) + dot_nn(context_two_ref[...], wo_ref[half:])
    z = z + b_ref[...] + x_ref[...].astype(F32)
    zhat, scale = normalize(z)
    mid_ref[...] = (zhat * gain_ref[...] + shift_ref[...]).astype(BF16)
    zhat_ref[...] = zhat
    scale_ref[...] = jnp.broadcast_to(scale, scale_ref.shape)


def hidden_kernel(mid_ref, w_ref, b_ref, act_ref, slope_ref):
    block = 512
    for first in range(0, w_ref.shape[0], block):
        cols = slice(first, first + block)
        act, slope = gelu_pair(dot_nt(mid_ref[...], w_ref[cols]) + b_ref[:, cols])
        act_ref[:, cols] = act.astype(BF16)
        slope_ref[:, cols] = slope.astype(BF16)


def branch_kernel(
    act_own_ref,
    act_other_ref,
    w_own_ref,
    w_other_ref,
    mid_ref,
    b_ref,
    gain_ref,
    shift_ref,
    cotangent_ref,
    out_ref,
    grad_ref,
    low_ref,
    sums_ref,
):
    z = dot_nn(act_own_ref[...], w_own_ref[...]) + dot_nn(act_other_ref[...], w_other_ref[...])
    zhat, scale = normalize(z + b_ref[...] + mid_ref[...].astype(F32))
    out_ref[...] = (zhat * gain_ref[...] + shift_ref[...]).astype(BF16)
    c = cotangent_ref[...].astype(F32)
    grad = norm_back(c, zhat, scale, gain_ref[...])
    low = grad.astype(BF16)
    grad_ref[...] = grad
    low_ref[...] = low
    sums_ref[...] = jnp.concatenate(
        [column_sums(low.astype(F32)), column_sums(c * zhat), column_sums(c)], axis=0
    )


def pair_grads_kernel(left_own_ref, left_other_ref, right_ref, keep_ref, send_ref):
    send_ref[...] = dot_tn(left_other_ref[...], right_ref[...]).astype(BF16)
    keep_ref[...] = dot_tn(left_own_ref[...], right_ref[...]).astype(BF16)


def input_kernel(
    dq_ref, dk_ref, dv_ref, wq_ref, wk_ref, wv_ref, first_ref, own_ref, other_ref
):
    rows = dq_ref.shape[0]
    total = dot_nn(dk_ref[rows:], wk_ref[...]) + dot_nn(dv_ref[rows:], wv_ref[...])
    other_ref[...] = total.astype(BF16)
    total = dot_nn(dk_ref[:rows], wk_ref[...]) + dot_nn(dv_ref[:rows], wv_ref[...])
    own_ref[...] = total + dot_nn(dq_ref[...], wq_ref[...]) + first_ref[...]


def sum_rows_kernel(total_ref, more_ref, out_ref):
    out_ref[...] = (total_ref[...] + more_ref[...].astype(F32)).astype(BF16)


def pre_kernel(
    low_ref, w_own_ref, w_other_ref, slope_own_ref, slope_other_ref, own_ref, other_ref, sums_ref
):
    for k, (w, slope, out) in enumerate(
        ((w_own_ref, slope_own_ref, own_ref), (w_other_ref, slope_other_ref, other_ref))
    ):
        grad = (dot_nt(low_ref[...], w[...]) * slope[...].astype(F32)).astype(BF16)
        out[...] = grad
        sums_ref[k : k + 1] = column_sums(grad.astype(F32))


def first_kernel(
    pre_own_ref,
    pre_other_ref,
    w_own_ref,
    w_other_ref,
    grad_ref,
    zhat_ref,
    scale_ref,
    gain_ref,
    wo_ref,
    first_ref,
    low_ref,
    context_ref,
    sums_ref,
):
    grad = dot_nn(pre_own_ref[...], w_own_ref[...]) + dot_nn(pre_other_ref[...], w_other_ref[...])
    grad = grad + grad_ref[...]
    zhat = zhat_ref[...]
    first = norm_back(grad, zhat, scale_ref[:, :1], gain_ref[...])
    low = first.astype(BF16)
    first_ref[...] = first
    low_ref[...] = low
    context_ref[...] = dot_nt(low, wo_ref[...]).astype(BF16)
    sums_ref[...] = jnp.concatenate(
        [column_sums(low.astype(F32)), column_sums(grad * zhat), column_sums(grad)], axis=0
    )


def gelu_pair(v):
    cdf = 0.5 * (1.0 + lax.erf(v * (0.5**0.5)))
    density = jnp.exp(-0.5 * v * v) * 0.3989422804014327
    return v * cdf, cdf + v * density


def local(
    inputs,
    cotangent,
    lengths,
    w_query,
    w_key,
    w_value,
    b_query,
    b_value,
    w_output,
    b_output,
    gain_one,
    shift_one,
    w_hidden,
    b_hidden,
    w_back,
    b_back,
    gain_two,
    shift_two,
):
    rows, width = inputs.shape
    shards = lax.axis_size("tensor")
    head_cols = w_query.shape[1]
    hidden = w_hidden.shape[1]
    heads = head_cols // HD
    part = HD // 4
    ffn_rows = hidden // PLANE
    per_slot = shards // lengths.shape[0]
    assert per_slot == 2 and shards == 4 and lax.axis_size("dp") % PLANE == 0
    dp = lax.axis_index("dp")
    core = dp & 1
    chip = (((dp >> 2) & 1) << 1) | ((dp >> 1) & 1)
    me = core * 4 + chip
    t = lax.axis_index("tensor")

    where = jnp.stack([core, chip]).astype(jnp.int32)
    att_rows = 2 * heads * part
    far = pl.ds(1, shards - 1)

    by_head = (heads, 4, part, width)
    pair = [
        jnp.where(core == 0, w_query, w_value).T.reshape(by_head),
        jnp.where(core == 0, w_key.T, w_output).reshape(by_head),
    ]
    hid_near = lax.dynamic_slice_in_dim(w_hidden, core * (hidden // 2), hidden // 2, 1)
    hid_near = hid_near.T.reshape(4, ffn_rows, width)
    back_near = w_back.reshape(PLANE, ffn_rows, width)
    bias = jnp.pad(jnp.concatenate([b_query, b_value]), (0, width - 2 * head_cols))
    bias = jnp.stack([b_hidden, b_hidden, bias, bias])
    bias_high = lax.reduce_precision(bias, 8, 7)
    bias_rows = jnp.where(jnp.arange(4)[:, None] % 2 == 0, bias_high, bias - bias_high)
    bias_rows = jnp.pad(bias_rows.astype(BF16), ((0, 12), (0, 0)))

    def near_heads(j):
        return lambda core, chip: (slice(None), chip ^ j)

    def near_hid(j):
        return lambda core, chip: (chip ^ j,)

    def near_back(j):
        return lambda core, chip: (core * 4 + (chip ^ j),)

    ffn_send = pack(
        where,
        (2 * ffn_rows + 16, width),
        [
            (0, near_hid(0), (pl.ds(0, ffn_rows),)),
            (1, near_back(0), (pl.ds(ffn_rows, ffn_rows),)),
            (2, at(), (pl.ds(2 * ffn_rows, 16),)),
        ],
        [hid_near, back_near, bias_rows],
        (),
        2,
    )
    ffn_z = from_shards(ffn_send)
    att_send = pack(
        where, (2, heads, part, width), [(0, near_heads(0), (0,)), (1, near_heads(0), (1,))], pair, (), 0
    )
    rows_send = pack(where, inputs.shape, [(0, at(), ())], [inputs], (), 1)
    ffn_stack, bq, bv, bh = stack_and_biases(where, [ffn_send] + ffn_z, width, hidden, ())
    ffn_xy = swap(ffn_stack, "dp", XBIT), swap(ffn_stack, "dp", YBIT)
    att_z = from_shards(after(att_send.reshape(att_rows, width), *ffn_z))
    rows_other = swap(after(rows_send, *att_z), "tensor", 1)
    att_stack = stacked(where, att_z, att_rows, ())

    att_far = halves_from_chips(where, att_stack, list(ffn_xy))
    shape = (4, shards, 2, heads, part, width)
    moves = [(m, near_heads(j), (j, 0, m)) for j in range(4) for m in range(2)]
    moves += [(2 + j, at(), (j, far)) for j in range(3)]
    moves += [(5 + m, at(), (3, far, m)) for m in range(2)]
    att_far = [v.reshape(shards - 1, -1, heads, part, width) for v in att_far[:3]] + [
        v.reshape(shards - 1, heads, part, width) for v in att_far[3:]
    ]
    att_own = pack(where, shape, moves, pair + att_far, (rows_other,), 0)
    att_swap = swap(att_own, "dp", CORE)

    def ffn_half(near, near_index, first, diagonal, earlier):
        mine = pl.ds(first, ffn_rows)
        moves = [(0, near_index(j), (0, j)) for j in range(4)]
        moves += [(1 + j, at(every, mine), (far, j)) for j in range(3)]
        moves += [(4, at(), (far, 3))]
        own = pack(
            where,
            (shards, 4, ffn_rows, width),
            moves,
            [near] + ffn_far[:3] + [diagonal],
            earlier,
            1,
        )
        own = own.reshape(-1, width)
        return own, swap(own, "dp", CORE)

    every = slice(None)
    ffn_far, ffn_sent = halves_from_chips(where, ffn_stack, [], True, ffn_xy)
    queries, key_rows, values, wq, wk, wv, wo = project(
        where, att_own, att_swap, inputs, rows_other, bq, bv
    )
    wq, wk, wv, wo = (w.reshape(shards * head_cols, width) for w in (wq, wk, wv, wo))
    place = jnp.stack([lengths[t // per_slot], (t % per_slot) * rows]).astype(jnp.int32)
    pairs = width // LANES // 2
    context_one, logsum_one = attend(place, queries, key_rows, values, 0, pairs, [])
    context_two, logsum_two = attend(place, queries, key_rows, values, pairs, pairs, [context_one])
    logsum = jnp.concatenate([logsum_one, logsum_two], axis=0)
    contexts = (context_one, context_two)
    hid_own, hid_swap = ffn_half(hid_near, near_hid, 0, ffn_far[3], [context_one])
    back_own, back_swap = ffn_half(back_near, near_back, ffn_rows, ffn_far[4], [context_one])
    full, low = ((rows, width), F32), ((rows, width), BF16)
    half_low = ((rows, 2 * hidden), BF16)
    three = ((3, width), F32)
    mid, zhat_one, scale_one = whole_call(
        mid_kernel,
        [low, full, ((rows, LANES), F32)],
        (*contexts, wo, inputs, b_output[None], gain_one[None], shift_one[None]),
        2 * 10**8,
    )
    act_own, slope_own = whole_call(
        hidden_kernel, [half_low, half_low], (mid, hid_own, bh[:1]), 10**9
    )
    act_swap, slope_swap = whole_call(
        hidden_kernel, [half_low, half_low], (mid, hid_swap, bh[1:]), 10**9
    )
    outputs, grad_second, grad_branch, sums_two = whole_call(
        branch_kernel,
        [low, full, low, three],
        (
            act_own,
            act_swap,
            back_own,
            back_swap,
            mid,
            b_back[None],
            gain_two[None],
            shift_two[None],
            cotangent,
        ),
        3 * 10**9,
    )

    two = shards // 2
    low_half, high_half = pl.ds(0, two), pl.ds(two, shards - two)
    each = [(k,) for k in range(shards)]

    def first_step(keep, got, picks, earlier):
        a_keep, a_send, b_keep, b_send = fold(where, [(keep, got, picks)], earlier)
        return a_keep, b_keep, swap(a_send, "dp", XBIT), swap(b_send, "dp", YBIT), a_send

    def second_step(step, a_picks, b_picks, earlier):
        a_keep, b_keep, a_got, b_got, _ = step
        a_keep, a_send, b_keep, b_send = fold(
            where, [(a_keep, a_got, a_picks), (b_keep, b_got, b_picks)], earlier
        )
        return a_keep, b_keep, swap(a_send, "dp", YBIT), swap(b_send, "dp", XBIT), a_send

    def third_step(step, earlier, beside=()):
        a_keep, b_keep, a_got, b_got, _ = step
        groups = [(a_keep, a_got, each[:two]), (b_keep, b_got, each[: shards - two])]
        return fold(where, groups, earlier, beside)

    quarter = (shards, 2, 2, ffn_rows, width)
    ffn_picks = [
        (low_half, every, 0),
        (low_half, every, 1),
        (high_half, 0),
        (high_half, 1),
    ]
    ffn_again = [(every, 0), (every, 1)]
    pair_out = [((2 * hidden, width), BF16)] * 2
    back_keep, back_send = whole_call(
        pair_grads_kernel, pair_out, (act_own, act_swap, grad_branch), 10**9
    )
    back_got = swap(back_send, "dp", CORE)
    pre_own, pre_swap, grad_b_hidden = whole_call(
        pre_kernel,
        [half_low, half_low, ((2, 2 * hidden), F32)],
        (grad_branch, back_own, back_swap, slope_own, slope_swap),
        10**9,
    )
    back_step = first_step(back_keep.reshape(quarter), back_got.reshape(quarter), ffn_picks, ())
    hid_keep, hid_send = whole_call(
        pair_grads_kernel, pair_out, (pre_own, pre_swap, mid), 3 * 10**8, (back_step[4],)
    )
    hid_got = swap(hid_send, "dp", CORE)
    grad_first, grad_attn, grad_context, sums_one = whole_call(
        first_kernel,
        [full, low, low, three],
        (
            pre_own,
            pre_swap,
            hid_own,
            hid_swap,
            grad_second,
            zhat_one,
            scale_one,
            gain_one[None],
            wo,
        ),
        3 * 10**8,
        (hid_send,),
    )
    hid_step = first_step(
        hid_keep.reshape(quarter), hid_got.reshape(quarter), ffn_picks, (grad_first,)
    )
    grad_queries, grad_keys, grad_values = attend_back(
        place, queries, key_rows, values, logsum, grad_context, hid_step[4]
    )
    total, returned_send = whole_call(
        input_kernel,
        [full, low],
        (grad_queries, grad_keys, grad_values, wq, wk, wv, grad_first),
        3 * 10**8,
    )
    returned = swap(returned_send, "tensor", 1)
    back_step = second_step(back_step, ffn_again, ffn_again, (grad_queries,))
    att_keep, att_send = attention_weight_grads(
        where,
        grad_queries,
        grad_keys,
        grad_values,
        contexts,
        grad_attn,
        inputs,
        rows_other,
        (sums_one, sums_two, grad_b_hidden),
        shards,
        (back_step[4],),
    )
    wide = att_keep.shape[-1]

    input_grad = whole_call(sum_rows_kernel, [low], (total, returned), 1)[0]
    back_pieces = third_step(back_step, (att_keep, returned))
    back_got = send_pieces(back_pieces)
    hid_step = second_step(hid_step, ffn_again, ffn_again, (back_pieces[0],))
    att_got = swap(att_send, "dp", CORE)
    att_shape = (2, 2) + att_keep.shape[1:]
    att_picks = [
        (every, 0, low_half),
        (every, 1, low_half),
        (0, every, high_half),
        (1, every, high_half),
    ]
    att_step = first_step(
        att_keep.reshape(att_shape), att_got.reshape(att_shape), att_picks, ()
    )
    hid_pieces = third_step(hid_step, ())
    back_sum = shards_reduce(back_pieces, back_got, ())
    hid_got = send_pieces(hid_pieces)
    att_step = second_step(att_step, [(0,), (1,)], [(0,), (1,)], (back_sum,))
    hid_sum = shards_reduce(hid_pieces, hid_got)
    att_pieces = third_step(att_step, (hid_sum,))
    att_got = send_pieces(att_pieces)
    top = pl.ds(0, ffn_rows)
    ffn_sum = pack(
        where,
        (2, ffn_rows, width),
        [(0, at(top), (0,)), (1, at(top), (1,))],
        [back_sum, hid_sum],
        (),
    )
    att_sum = shards_reduce(att_pieces, att_got)
    att_far = from_chips(att_sum)
    ffn_far = halves_from_chips(where, ffn_sum, [att_sum])
    halves = [pl.ds(0, ffn_rows // 2), pl.ds(ffn_rows // 2, ffn_rows // 2)]
    moves = [(j, at(), (j,)) for j in range(3)]
    moves += [(3 + k, at(), (3, slice(None), halves[k])) for k in range(2)]
    ffn_out = pack(where, (4, 2, ffn_rows, width), moves, ffn_far, ())
    back_out, hid_out = ffn_outputs(where, ffn_out, swap(ffn_out, "dp", CORE), hidden, width)
    att_out = stacked(where, att_far, att_rows, (back_out,))
    gq, gk, gv, go, sum_q, sum_v, sum_hid, *vectors = att_outputs(
        where, att_out, swap(att_out, "dp", CORE), head_cols, width
    )
    return (
        outputs,
        input_grad,
        gq.T,
        gk.T,
        gv.T,
        sum_q,
        sum_v,
        go,
        vectors[0],
        vectors[1],
        vectors[2],
        hid_out,
        sum_hid,
        back_out,
        vectors[3],
        vectors[4],
        vectors[5],
    )


def solution(mesh):
    rows = P(("dp", "tensor"), None)
    columns, depth, vector = P(None, "tensor"), P("tensor", None), P("tensor")
    return jax.shard_map(
        local,
        mesh=mesh,
        in_specs=(
            rows,
            rows,
            P("dp"),
            columns,
            columns,
            columns,
            vector,
            vector,
            depth,
            P(),
            P(),
            P(),
            columns,
            vector,
            depth,
            P(),
            P(),
            P(),
        ),
        out_specs=(
            rows,
            rows,
            columns,
            columns,
            columns,
            vector,
            vector,
            depth,
            P(),
            P(),
            P(),
            columns,
            vector,
            depth,
            P(),
            P(),
            P(),
        ),
        check_vma=False,
    )
```

```python
import functools

import jax
import jax.numpy as jnp
from jax import lax
from jax.experimental import pallas as pl
from jax.experimental.pallas import tpu as pltpu
from jax.sharding import PartitionSpec as P

HD = 64
LANES = 128
PLANE = 8
CORE, XBIT, YBIT = 1, 2, 4
BF16, F32 = jnp.bfloat16, jnp.float32
MIB = 1024 * 1024
FREE = pl.CostEstimate(flops=1, bytes_accessed=1, transcendentals=0)


def dot_nn(a, b):
    return lax.dot_general(a, b, (((1,), (0,)), ((), ())), preferred_element_type=F32)


def dot_nt(a, b):
    return lax.dot_general(a, b, (((1,), (1,)), ((), ())), preferred_element_type=F32)


def dot_tn(a, b):
    return lax.dot_general(a, b, (((0,), (0,)), ((), ())), preferred_element_type=F32)


def swap(v, axis, bit):
    count = lax.axis_size(axis)
    return lax.ppermute(v, axis, [(i, i ^ bit) for i in range(count)])


def pack_kernel(plan, far, place_ref, *refs):
    outs, sem = refs[len(refs) - len(plan) - 1 : -1], refs[-1]
    core, chip = place_ref[0], place_ref[1]
    copies = []
    for out_ref, moves in zip(outs, plan):
        for which, source, target in moves:
            if which < far:
                src, dst = refs[which].at[source(core, chip)], out_ref.at[target]
                copies.append(pltpu.make_async_copy(src, dst, sem.at[len(copies)]))
    for copy in copies:
        copy.start()
    for out_ref, moves in zip(outs, plan):
        for which, source, target in moves:
            if which >= far:
                out_ref[target or ...] = refs[which][source(core, chip) or ...]
    for copy in copies:
        copy.wait()


def packs(where, shapes, plan, arrays, earlier=(), far=0):
    vmem, space = pl.BlockSpec(memory_space=pltpu.VMEM), pl.BlockSpec(memory_space=pl.ANY)
    count = sum(which < far for moves in plan for which, _, _ in moves)
    return pl.pallas_call(
        functools.partial(pack_kernel, plan, far),
        in_specs=[pl.BlockSpec(memory_space=pltpu.SMEM)]
        + [pl.BlockSpec(memory_space=pltpu.HBM)] * far
        + [vmem] * (len(arrays) - far)
        + [space] * len(earlier),
        out_specs=[vmem] * len(shapes),
        out_shape=[jax.ShapeDtypeStruct(shape, BF16) for shape in shapes],
        scratch_shapes=[pltpu.SemaphoreType.DMA((max(count, 1),))],
        compiler_params=pltpu.CompilerParams(vmem_limit_bytes=10 * MIB),
        cost_estimate=FREE,
    )(where, *arrays, *earlier)


def pack(where, shape, moves, arrays, earlier=(), far=0):
    return packs(where, [shape], [moves], arrays, earlier, far)[0]


def nothing_kernel(*refs):
    del refs


def after(v, *earlier):
    space = pl.BlockSpec(memory_space=pl.ANY)
    return pl.pallas_call(
        nothing_kernel,
        in_specs=[space] * (1 + len(earlier)),
        out_specs=space,
        out_shape=jax.ShapeDtypeStruct(v.shape, v.dtype),
        input_output_aliases={0: 0},
    )(v, *earlier)


def fold_kernel(plan, beside, place_ref, *refs):
    del place_ref
    count = sum(len(picks) for picks in plan)
    outs = refs[len(refs) - count :]
    others = refs[2 * len(plan) : 2 * len(plan) + beside]
    spot = 0
    for k, picks in enumerate(plan):
        for pick in picks:
            total = refs[2 * k][pick].astype(F32) + refs[2 * k + 1][pick].astype(F32)
            if beside:
                outs[spot][0] = others[spot][...]
                outs[spot][1] = total.astype(BF16)
            else:
                outs[spot][...] = total.astype(BF16)
            spot += 1


def fold(where, groups, earlier=(), beside=()):
    vmem, space = pl.BlockSpec(memory_space=pltpu.VMEM), pl.BlockSpec(memory_space=pl.ANY)
    arrays = [v for a, b, _ in groups for v in (a, b)] + list(beside)
    outs = [
        jax.ShapeDtypeStruct(
            ((2,) if beside else ()) + jax.eval_shape(lambda v, p=pick: v[p], a).shape, BF16
        )
        for a, _, picks in groups
        for pick in picks
    ]
    return pl.pallas_call(
        functools.partial(fold_kernel, [picks for _, _, picks in groups], len(beside)),
        in_specs=[pl.BlockSpec(memory_space=pltpu.SMEM)]
        + [vmem] * len(arrays)
        + [space] * len(earlier),
        out_specs=[vmem] * len(outs),
        out_shape=outs,
        compiler_params=pltpu.CompilerParams(vmem_limit_bytes=14 * MIB),
        cost_estimate=FREE,
    )(where, *arrays, *earlier)


def sum_kernel(first_ref, a_ref, b_ref, c_ref, *refs):
    total = first_ref[...].astype(F32) + a_ref[...].astype(F32)
    total = total + b_ref[...].astype(F32) + c_ref[...].astype(F32)
    refs[-1][...] = total.astype(refs[-1].dtype)


def at(*index):
    return lambda core, chip: index


def stacked(where, arrays, rows, earlier=()):
    top = pl.ds(0, rows)
    moves = [(i, at(top), (i,)) for i in range(len(arrays))]
    return pack(where, (len(arrays), rows) + arrays[0].shape[1:], moves, arrays, earlier)


def from_shards(v):
    return [swap(v, "tensor", k) for k in range(1, lax.axis_size("tensor"))]


def halves_from_chips(where, v, between=(), sent=False, first=None):
    v_x, v_y = first or (swap(v, "dp", XBIT), swap(v, "dp", YBIT))
    half = v.shape[1] // 2
    low, high = (slice(None), pl.ds(0, half)), (slice(None), pl.ds(half, half))
    shape = (v.shape[0], half) + v.shape[2:]
    plan = [[(0, at(*low), ())], [(1, at(*high), ())]]
    on_y, on_x = packs(where, [shape, shape], plan, [v_x, v_y], between)
    got = [v, v_x, v_y, swap(on_y, "dp", YBIT), swap(on_x, "dp", XBIT)]
    return (got, [on_y, on_x]) if sent else got


def from_chips(v):
    return [v] + [swap(v, "dp", bits) for bits in (XBIT, YBIT, XBIT | YBIT)]


def shards_reduce(pieces, got, earlier=()):
    more = lax.axis_size("dp") > PLANE
    vmem, space = pl.BlockSpec(memory_space=pltpu.VMEM), pl.BlockSpec(memory_space=pl.ANY)
    total = pl.pallas_call(
        sum_kernel,
        in_specs=[vmem] * len(pieces) + [space] * len(earlier),
        out_specs=vmem,
        out_shape=jax.ShapeDtypeStruct(pieces[0].shape, F32 if more else BF16),
        compiler_params=pltpu.CompilerParams(vmem_limit_bytes=6 * MIB),
        cost_estimate=FREE,
    )(pieces[0], *got, *earlier)
    step = PLANE
    while step < lax.axis_size("dp"):
        total = total + swap(total, "dp", step)
        step *= 2
    return total.astype(BF16)


def send_pieces(pieces):
    return [swap(pieces[k], "tensor", k) for k in range(1, len(pieces))]


def relative_lanes(v, where_me, bits, block):
    width = v.shape[-1]
    spot = lax.broadcasted_iota(jnp.int32, v.shape, 1) // block
    for b in range(bits):
        shift = block << b
        right, left = pltpu.roll(v, shift, 1), pltpu.roll(v, width - shift, 1)
        flipped = jnp.where(((spot >> b) & 1) == 1, right, left)
        v = jnp.where(((where_me >> b) & 1) == 1, flipped, v)
    return v


def bias_kernel(place_ref, *refs):
    sources, (stack_ref, bq_ref, bv_ref, bh_ref) = refs[:4], refs[-4:]
    core, chip = place_ref[0], place_ref[1]
    rows = sources[0].shape[0] - 16
    width = bq_ref.shape[1]
    group = width // 4
    hidden, heads = [], []
    for k, ref in enumerate(sources):
        if k > 0:
            stack_ref[k - 1] = ref[:rows]
        tail = ref[rows : rows + 16].astype(F32)
        hidden.append(tail[0:1] + tail[1:2])
        heads.append(tail[2:3] + tail[3:4])
    hidden = jnp.concatenate(hidden + hidden, axis=0)
    hidden = relative_lanes(hidden, core * 4 + chip, 3, hidden.shape[1] // PLANE)
    half = hidden.shape[1] // 2
    for s in range(4):
        bh_ref[0:1, s * half : (s + 1) * half] = hidden[s : s + 1, :half]
        bh_ref[1:2, s * half : (s + 1) * half] = hidden[s : s + 1, half:]
    for k, out in enumerate((bq_ref, bv_ref)):
        row = jnp.concatenate([h[:, k * group : (k + 1) * group] for h in heads], axis=1)
        row = jnp.broadcast_to(row, (8, width))
        out[...] = relative_lanes(row, chip, 2, HD // 4)[0:1]


def stack_and_biases(where, sources, width, hidden, earlier):
    vmem = pl.BlockSpec(memory_space=pltpu.VMEM)
    rows = sources[0].shape[0] - 16
    return pl.pallas_call(
        bias_kernel,
        in_specs=[pl.BlockSpec(memory_space=pltpu.SMEM)]
        + [vmem] * 4
        + [pl.BlockSpec(memory_space=pl.ANY)] * len(earlier),
        out_specs=[vmem] * 4,
        out_shape=[
            jax.ShapeDtypeStruct((len(sources) - 1, rows, width), BF16),
            jax.ShapeDtypeStruct((1, width), F32),
            jax.ShapeDtypeStruct((1, width), F32),
            jax.ShapeDtypeStruct((2, 2 * hidden), F32),
        ],
        compiler_params=pltpu.CompilerParams(vmem_limit_bytes=6 * MIB),
        cost_estimate=FREE,
    )(where, *sources, *earlier)


def qkv_kernel(place_ref, own, other, x_ref, xo_ref, bq_ref, bv_ref, *refs):
    (q_ref, k_ref, v_ref), weights, sem = refs[:3], refs[3:7], refs[7]
    core = place_ref[0]
    rows, width = x_ref.shape

    def copies(src, group):
        return [
            pltpu.make_async_copy(
                src.at[j, :, m], weights[2 * group + m].at[:, :, j], sem.at[group, m, j]
            )
            for m in range(2)
            for j in range(4)
        ]

    for group in (0, 1):

        @pl.when(core == group)
        def _():
            for copy in copies(own, group):
                copy.start()

        @pl.when(core != group)
        def _():
            for copy in copies(other, group):
                copy.start()

    def landed(group):
        @pl.when(core == group)
        def _():
            for copy in copies(own, group):
                copy.wait()

        @pl.when(core != group)
        def _():
            for copy in copies(other, group):
                copy.wait()

    landed(0)
    x, xo = x_ref[...], xo_ref[...]
    q_ref[...] = (dot_nt(x, weights[0][...].reshape(width, width)) + bq_ref[...]).astype(BF16)
    w = weights[1][...].reshape(width, width)
    k_ref[:rows] = dot_nt(x, w).astype(BF16)
    k_ref[rows:] = dot_nt(xo, w).astype(BF16)
    landed(1)
    w = weights[2][...].reshape(width, width)
    v_ref[:rows] = (dot_nt(x, w) + bv_ref[...]).astype(BF16)
    v_ref[rows:] = (dot_nt(xo, w) + bv_ref[...]).astype(BF16)


def project(where, own, other, x, xo, bq, bv):
    rows, width = x.shape
    _, shards, _, heads, part, _ = own.shape
    vmem = pl.BlockSpec(memory_space=pltpu.VMEM)
    space = pl.BlockSpec(memory_space=pl.ANY)
    shapes = [(rows, width), (2 * rows, width), (2 * rows, width)]
    shapes += [(shards, heads, 4, part, width)] * 4
    return pl.pallas_call(
        qkv_kernel,
        in_specs=[pl.BlockSpec(memory_space=pltpu.SMEM), space, space] + [vmem] * 4,
        out_specs=[vmem] * 7,
        out_shape=[jax.ShapeDtypeStruct(shape, BF16) for shape in shapes],
        scratch_shapes=[pltpu.SemaphoreType.DMA((2, 2, 4))],
        compiler_params=pltpu.CompilerParams(vmem_limit_bytes=18 * MIB),
        cost_estimate=FREE,
    )(where, own, other, x, xo, bq, bv)


def att_out_kernel(place_ref, own_ref, other_ref, gq_ref, gk_ref, gv_ref, go_ref, *sums):
    core, chip = place_ref[0], place_ref[1]
    head_cols, width = go_ref.shape
    heads, part = head_cols // HD, HD // 4
    extras = []
    for group in (0, 1):
        blocks = []
        for c in range(4):
            block = jnp.where(core == group, own_ref[c ^ chip], other_ref[c ^ chip])
            extras.append(block[:, width:])
            blocks.append(block)
        for m in range(2):
            pieces = [
                blocks[c][(m * heads + h) * part : (m * heads + h + 1) * part]
                for h in range(heads)
                for c in range(4)
            ]
            whole = jnp.concatenate(pieces, axis=0)
            (gq_ref, gk_ref, gv_ref, go_ref)[2 * group + m][...] = whole[:, :width].astype(F32)
            if m == 0:
                sums[group][...] = whole[:, width:].astype(F32).T[0]
    extras = jnp.concatenate(extras, axis=0).astype(F32).T
    for k in range(1, 8):
        sums[1 + k][...] = extras[k]


def att_outputs(where, own, other, head_cols, width):
    vmem = pl.BlockSpec(memory_space=pltpu.VMEM)
    weight = jax.ShapeDtypeStruct((head_cols, width), F32)
    vector = jax.ShapeDtypeStruct((width,), F32)
    few = jax.ShapeDtypeStruct((head_cols,), F32)
    return pl.pallas_call(
        att_out_kernel,
        in_specs=[pl.BlockSpec(memory_space=pltpu.SMEM), vmem, vmem],
        out_specs=[vmem] * 13,
        out_shape=[weight] * 4 + [few] * 2 + [vector] * 7,
        compiler_params=pltpu.CompilerParams(vmem_limit_bytes=14 * MIB),
    )(where, own, other)


def ffn_out_kernel(place_ref, own_ref, other_ref, back_ref, hid_ref):
    core, chip = place_ref[0], place_ref[1]
    rows = own_ref.shape[2]
    blocks = []
    for group in (0, 1):
        for c in range(4):
            block = jnp.where(core == group, own_ref[c ^ chip], other_ref[c ^ chip])
            spot = (group * 4 + c) * rows
            back_ref[spot : spot + rows] = block[0].astype(F32)
            blocks.append(block[1])
    hid_ref[...] = jnp.concatenate(blocks, axis=0).astype(F32).T


def ffn_outputs(where, own, other, hidden, width):
    vmem = pl.BlockSpec(memory_space=pltpu.VMEM)
    return pl.pallas_call(
        ffn_out_kernel,
        in_specs=[pl.BlockSpec(memory_space=pltpu.SMEM), vmem, vmem],
        out_specs=[vmem] * 2,
        out_shape=[
            jax.ShapeDtypeStruct((hidden, width), F32),
            jax.ShapeDtypeStruct((width, hidden), F32),
        ],
        compiler_params=pltpu.CompilerParams(vmem_limit_bytes=58 * MIB),
    )(where, own, other)


def live_keys(place_ref, keys, half_rows):
    spot = lax.broadcasted_iota(jnp.int32, (keys, 1), 0)
    first = place_ref[1]
    spot = jnp.where(spot < half_rows, spot + first, spot - first)
    return spot < place_ref[0]


def attend_kernel(place_ref, q_ref, k_ref, v_ref, *refs, half_rows):
    out_ref, lse_ref = refs[-2:]
    rows, keys = q_ref.shape[0], k_ref.shape[0]
    q = q_ref[...] * jnp.asarray(0.125, BF16)
    k = k_ref[...]
    v_turned = v_ref[...].T
    live = live_keys(place_ref, keys, half_rows)
    lane = lax.broadcasted_iota(jnp.int32, (rows, LANES), 1)
    outs, sums = [], []
    for h in range(LANES // HD):
        qh = jnp.where((lane // HD) == h, q, jnp.zeros_like(q))
        s = jnp.where(live, dot_nt(k, qh), -1e30)
        top = jnp.max(s, axis=0, keepdims=True)
        e = jnp.exp(s - top)
        total = jnp.sum(e, axis=0, keepdims=True)
        out = dot_nn(v_turned, e.astype(BF16))[h * HD : (h + 1) * HD]
        outs.append(out * (1.0 / total))
        sums.append(top + jnp.log(total))
    out_ref[...] = jnp.concatenate(outs, axis=0).T.astype(BF16)
    lse_ref[...] = jnp.concatenate(sums + [jnp.zeros((6, rows), F32)], axis=0)


def attend_back_kernel(
    place_ref, q_ref, k_ref, v_ref, lse_ref, do_ref, _, dq_ref, dk_ref, dv_ref, *, half_rows
):
    rows, keys = q_ref.shape[0], k_ref.shape[0]
    k, v, do = k_ref[...], v_ref[...], do_ref[...]
    q = q_ref[...] * jnp.asarray(0.125, BF16)
    k_turned = k.T
    live = live_keys(place_ref, keys, half_rows)
    lane = lax.broadcasted_iota(jnp.int32, (rows, LANES), 1)
    dqs, dks, dvs = [], [], []
    for h in range(LANES // HD):
        mine = (lane // HD) == h
        qh = jnp.where(mine, q, jnp.zeros_like(q))
        doh = jnp.where(mine, do, jnp.zeros_like(do))
        s = jnp.where(live, dot_nt(k, qh), -1e30)
        p = jnp.exp(s - lse_ref[h : h + 1, :])
        dp = dot_nt(v, doh)
        inner = jnp.sum(p * dp, axis=0, keepdims=True)
        ds = (p * (dp - inner)).astype(BF16)
        dqs.append(dot_nn(k_turned, ds)[h * HD : (h + 1) * HD])
        dks.append(dot_nn(ds, qh))
        dvs.append(dot_nn(p.astype(BF16), doh))
    dq_ref[...] = (jnp.concatenate(dqs, axis=0).T * 0.125).astype(BF16)
    dk_ref[...] = (dks[0] + dks[1]).astype(BF16)
    dv_ref[...] = (dvs[0] + dvs[1]).astype(BF16)


def attend(place, q, k, v, first, pairs, earlier):
    rows, width = q.shape[0], pairs * LANES
    keys = k.shape[0]
    q_spec = pl.BlockSpec((rows, LANES), lambda i: (0, i + first))
    k_spec = pl.BlockSpec((keys, LANES), lambda i: (0, i + first))
    out_spec = pl.BlockSpec((rows, LANES), lambda i: (0, i))
    lse_spec = pl.BlockSpec((8, rows), lambda i: (i, 0))
    return pl.pallas_call(
        functools.partial(attend_kernel, half_rows=rows),
        grid=(pairs,),
        in_specs=[
            pl.BlockSpec(memory_space=pltpu.SMEM),
            q_spec,
            k_spec,
            k_spec,
        ]
        + [pl.BlockSpec(memory_space=pl.ANY)] * len(earlier),
        out_specs=[out_spec, lse_spec],
        out_shape=[
            jax.ShapeDtypeStruct((rows, width), BF16),
            jax.ShapeDtypeStruct((8 * pairs, rows), F32),
        ],
        compiler_params=pltpu.CompilerParams(vmem_limit_bytes=10 * MIB),
        cost_estimate=FREE,
    )(place, q, k, v, *earlier)


def attend_back(place, q, k, v, lse, do, earlier):
    rows, width = q.shape
    keys = k.shape[0]
    q_spec = pl.BlockSpec((rows, LANES), lambda i: (0, i))
    k_spec = pl.BlockSpec((keys, LANES), lambda i: (0, i))
    lse_spec = pl.BlockSpec((8, rows), lambda i: (i, 0))
    return pl.pallas_call(
        functools.partial(attend_back_kernel, half_rows=rows),
        grid=(width // LANES,),
        in_specs=[
            pl.BlockSpec(memory_space=pltpu.SMEM),
            q_spec,
            k_spec,
            k_spec,
            lse_spec,
            q_spec,
            pl.BlockSpec(memory_space=pl.ANY),
        ],
        out_specs=[q_spec, k_spec, k_spec],
        out_shape=[
            jax.ShapeDtypeStruct((rows, width), BF16),
            jax.ShapeDtypeStruct((keys, width), BF16),
            jax.ShapeDtypeStruct((keys, width), BF16),
        ],
        compiler_params=pltpu.CompilerParams(vmem_limit_bytes=10 * MIB),
        cost_estimate=FREE,
    )(place, q, k, v, lse, do, earlier)


def weights_kernel(
    place_ref,
    dq_ref,
    dk_ref,
    dv_ref,
    context_ref,
    context_two_ref,
    ga_ref,
    x_ref,
    xo_ref,
    one_ref,
    two_ref,
    hid_ref,
    *refs,
):
    keep_ref, send_ref = refs[-2:]
    rows, width = dq_ref.shape
    shards = keep_ref.shape[1]
    group = width // shards
    heads = group // HD
    part = HD // 4
    core, chip = place_ref[0], place_ref[1]
    span = 2 * group
    lane = lax.broadcasted_iota(jnp.int32, (part, LANES), 1)
    spots = lax.broadcasted_iota(jnp.int32, (8, LANES), 0)
    spots = (spots == lax.broadcasted_iota(jnp.int32, (8, LANES), 1)).astype(BF16)
    att_rows = keep_ref.shape[2]
    half = 4 * att_rows
    whole = jnp.concatenate([jnp.zeros((2, width), F32), one_ref[...], two_ref[...]], axis=0)
    whole = relative_lanes(whole, core * 4 + chip, 3, att_rows)
    line = lax.broadcasted_iota(jnp.int32, (8, half), 0)
    extra = []
    for g in range(2):
        extra.append([])
        for s in range(shards):
            mine = hid_ref[g : g + 1, s * half : (s + 1) * half]
            mine = jnp.where(line == 1, mine, whole[:, g * half : (g + 1) * half])
            extra[g].append(dot_tn(mine.astype(BF16), spots))

    def put(which, m, left_ref, rights, with_sum):
        ones = jnp.ones((rows, LANES), BF16)
        for first in range(0, width, span):
            out, sums = None, None
            for k, right in enumerate(rights):
                if isinstance(left_ref, tuple):
                    left = left_ref[first // span][...]
                else:
                    left = left_ref[k * rows : (k + 1) * rows, first : first + span]
                more = dot_tn(left, right[...])
                out = more if out is None else out + more
                if with_sum:
                    more = dot_tn(left, ones)
                    sums = more if sums is None else sums + more

            def store(dst, base):
                for at in range(0, span, part):
                    row = first + at
                    shard, rest = row // group, row % group
                    head, j = rest // HD, (rest % HD) // part
                    spot = (m * heads + head) * part
                    dst[j, shard, spot : spot + part, :width] = out[at : at + part].astype(BF16)
                    tail = extra[base][shard][j * att_rows + spot : j * att_rows + spot + part]
                    if with_sum:
                        tail = jnp.where(lane == 0, sums[at : at + part], tail)
                    dst[j, shard, spot : spot + part, width:] = tail.astype(BF16)

            @pl.when(core == which)
            def _():
                store(keep_ref, 0)

            @pl.when(core != which)
            def _():
                store(send_ref, 1)

    put(0, 0, dq_ref, [x_ref], True)
    put(0, 1, dk_ref, [x_ref, xo_ref], False)
    put(1, 0, dv_ref, [x_ref, xo_ref], True)
    put(1, 1, (context_ref, context_two_ref), [ga_ref], False)


def attention_weight_grads(where, dq, dk, dv, contexts, ga, x, xo, sums, shards, earlier):
    width = dq.shape[1]
    full = jax.ShapeDtypeStruct((4, shards, width // (2 * shards), width + LANES), BF16)
    vmem = pl.BlockSpec(memory_space=pltpu.VMEM)
    return pl.pallas_call(
        weights_kernel,
        in_specs=[pl.BlockSpec(memory_space=pltpu.SMEM)] + [vmem] * 11 + [pl.BlockSpec(memory_space=pl.ANY)] * len(earlier),
        out_specs=[vmem, vmem],
        out_shape=[full, full],
        compiler_params=pltpu.CompilerParams(vmem_limit_bytes=22 * MIB),
        cost_estimate=FREE,
    )(where, dq, dk, dv, *contexts, ga, x, xo, *sums, *earlier)


def whole_call(kernel, outs, args, flops, earlier=()):
    vmem, space = pl.BlockSpec(memory_space=pltpu.VMEM), pl.BlockSpec(memory_space=pl.ANY)
    if earlier:
        inner, count = kernel, len(args)
        kernel = lambda *refs: inner(*refs[:count], *refs[count + len(earlier) :])
    return pl.pallas_call(
        kernel,
        in_specs=[vmem] * len(args) + [space] * len(earlier),
        out_specs=[vmem] * len(outs),
        out_shape=[jax.ShapeDtypeStruct(shape, dtype) for shape, dtype in outs],
        compiler_params=pltpu.CompilerParams(vmem_limit_bytes=22 * MIB),
        cost_estimate=FREE,
    )(*args, *earlier)


def normalize(z):
    center = z - jnp.mean(z, axis=-1, keepdims=True)
    spread = jnp.mean(center * center, axis=-1, keepdims=True)
    scale = lax.rsqrt(spread + 1e-05)
    return center * scale, scale


def norm_back(grad, zhat, scale, gain):
    e = grad * gain
    inner = jnp.mean(e * zhat, axis=-1, keepdims=True)
    return (e - jnp.mean(e, axis=-1, keepdims=True) - zhat * inner) * scale


def column_sums(v):
    return jnp.sum(v, axis=0, keepdims=True)


def mid_kernel(
    context_ref,
    context_two_ref,
    wo_ref,
    x_ref,
    b_ref,
    gain_ref,
    shift_ref,
    mid_ref,
    zhat_ref,
    scale_ref,
):
    half = context_ref.shape[1]
    z = dot_nn(context_ref[...], wo_ref[:half]) + dot_nn(context_two_ref[...], wo_ref[half:])
    z = z + b_ref[...] + x_ref[...].astype(F32)
    zhat, scale = normalize(z)
    mid_ref[...] = (zhat * gain_ref[...] + shift_ref[...]).astype(BF16)
    zhat_ref[...] = zhat
    scale_ref[...] = jnp.broadcast_to(scale, scale_ref.shape)


def hidden_kernel(mid_ref, w_ref, b_ref, act_ref, slope_ref):
    block = 512
    for first in range(0, w_ref.shape[0], block):
        cols = slice(first, first + block)
        act, slope = gelu_pair(dot_nt(mid_ref[...], w_ref[cols]) + b_ref[:, cols])
        act_ref[:, cols] = act.astype(BF16)
        slope_ref[:, cols] = slope.astype(BF16)


def branch_kernel(
    act_own_ref,
    act_other_ref,
    w_own_ref,
    w_other_ref,
    mid_ref,
    b_ref,
    gain_ref,
    shift_ref,
    cotangent_ref,
    out_ref,
    grad_ref,
    low_ref,
    sums_ref,
):
    z = dot_nn(act_own_ref[...], w_own_ref[...]) + dot_nn(act_other_ref[...], w_other_ref[...])
    zhat, scale = normalize(z + b_ref[...] + mid_ref[...].astype(F32))
    out_ref[...] = (zhat * gain_ref[...] + shift_ref[...]).astype(BF16)
    c = cotangent_ref[...].astype(F32)
    grad = norm_back(c, zhat, scale, gain_ref[...])
    low = grad.astype(BF16)
    grad_ref[...] = grad
    low_ref[...] = low
    sums_ref[...] = jnp.concatenate(
        [column_sums(low.astype(F32)), column_sums(c * zhat), column_sums(c)], axis=0
    )


def pair_grads_kernel(left_own_ref, left_other_ref, right_ref, keep_ref, send_ref):
    send_ref[...] = dot_tn(left_other_ref[...], right_ref[...]).astype(BF16)
    keep_ref[...] = dot_tn(left_own_ref[...], right_ref[...]).astype(BF16)


def input_kernel(
    dq_ref, dk_ref, dv_ref, wq_ref, wk_ref, wv_ref, first_ref, own_ref, other_ref
):
    rows = dq_ref.shape[0]
    total = dot_nn(dk_ref[rows:], wk_ref[...]) + dot_nn(dv_ref[rows:], wv_ref[...])
    other_ref[...] = total.astype(BF16)
    total = dot_nn(dk_ref[:rows], wk_ref[...]) + dot_nn(dv_ref[:rows], wv_ref[...])
    own_ref[...] = total + dot_nn(dq_ref[...], wq_ref[...]) + first_ref[...]


def sum_rows_kernel(total_ref, more_ref, out_ref):
    out_ref[...] = (total_ref[...] + more_ref[...].astype(F32)).astype(BF16)


def pre_kernel(
    low_ref, w_own_ref, w_other_ref, slope_own_ref, slope_other_ref, own_ref, other_ref, sums_ref
):
    for k, (w, slope, out) in enumerate(
        ((w_own_ref, slope_own_ref, own_ref), (w_other_ref, slope_other_ref, other_ref))
    ):
        grad = (dot_nt(low_ref[...], w[...]) * slope[...].astype(F32)).astype(BF16)
        out[...] = grad
        sums_ref[k : k + 1] = column_sums(grad.astype(F32))


def first_kernel(
    pre_own_ref,
    pre_other_ref,
    w_own_ref,
    w_other_ref,
    grad_ref,
    zhat_ref,
    scale_ref,
    gain_ref,
    wo_ref,
    first_ref,
    low_ref,
    context_ref,
    sums_ref,
):
    grad = dot_nn(pre_own_ref[...], w_own_ref[...]) + dot_nn(pre_other_ref[...], w_other_ref[...])
    grad = grad + grad_ref[...]
    zhat = zhat_ref[...]
    first = norm_back(grad, zhat, scale_ref[:, :1], gain_ref[...])
    low = first.astype(BF16)
    first_ref[...] = first
    low_ref[...] = low
    context_ref[...] = dot_nt(low, wo_ref[...]).astype(BF16)
    sums_ref[...] = jnp.concatenate(
        [column_sums(low.astype(F32)), column_sums(grad * zhat), column_sums(grad)], axis=0
    )


def gelu_pair(v):
    cdf = 0.5 * (1.0 + lax.erf(v * (0.5**0.5)))
    density = jnp.exp(-0.5 * v * v) * 0.3989422804014327
    return v * cdf, cdf + v * density


def local(
    inputs,
    cotangent,
    lengths,
    w_query,
    w_key,
    w_value,
    b_query,
    b_value,
    w_output,
    b_output,
    gain_one,
    shift_one,
    w_hidden,
    b_hidden,
    w_back,
    b_back,
    gain_two,
    shift_two,
):
    rows, width = inputs.shape
    shards = lax.axis_size("tensor")
    head_cols = w_query.shape[1]
    hidden = w_hidden.shape[1]
    heads = head_cols // HD
    part = HD // 4
    ffn_rows = hidden // PLANE
    per_slot = shards // lengths.shape[0]
    assert per_slot == 2 and shards == 4 and lax.axis_size("dp") % PLANE == 0
    dp = lax.axis_index("dp")
    core = dp & 1
    chip = (((dp >> 2) & 1) << 1) | ((dp >> 1) & 1)
    me = core * 4 + chip
    t = lax.axis_index("tensor")

    where = jnp.stack([core, chip]).astype(jnp.int32)
    att_rows = 2 * heads * part
    far = pl.ds(1, shards - 1)

    by_head = (heads, 4, part, width)
    pair = [
        jnp.where(core == 0, w_query, w_value).T.reshape(by_head),
        jnp.where(core == 0, w_key.T, w_output).reshape(by_head),
    ]
    hid_near = lax.dynamic_slice_in_dim(w_hidden, core * (hidden // 2), hidden // 2, 1)
    hid_near = hid_near.T.reshape(4, ffn_rows, width)
    back_near = w_back.reshape(PLANE, ffn_rows, width)
    bias = jnp.pad(jnp.concatenate([b_query, b_value]), (0, width - 2 * head_cols))
    bias = jnp.stack([b_hidden, b_hidden, bias, bias])
    bias_high = lax.reduce_precision(bias, 8, 7)
    bias_rows = jnp.where(jnp.arange(4)[:, None] % 2 == 0, bias_high, bias - bias_high)
    bias_rows = jnp.pad(bias_rows.astype(BF16), ((0, 12), (0, 0)))

    def near_heads(j):
        return lambda core, chip: (slice(None), chip ^ j)

    def near_hid(j):
        return lambda core, chip: (chip ^ j,)

    def near_back(j):
        return lambda core, chip: (core * 4 + (chip ^ j),)

    ffn_send = pack(
        where,
        (2 * ffn_rows + 16, width),
        [
            (0, near_hid(0), (pl.ds(0, ffn_rows),)),
            (1, near_back(0), (pl.ds(ffn_rows, ffn_rows),)),
            (2, at(), (pl.ds(2 * ffn_rows, 16),)),
        ],
        [hid_near, back_near, bias_rows],
        (),
        2,
    )
    ffn_z = from_shards(ffn_send)
    att_send = pack(
        where, (2, heads, part, width), [(0, near_heads(0), (0,)), (1, near_heads(0), (1,))], pair, (), 0
    )
    rows_send = pack(where, inputs.shape, [(0, at(), ())], [inputs], (), 1)
    ffn_stack, bq, bv, bh = stack_and_biases(where, [ffn_send] + ffn_z, width, hidden, ())
    ffn_xy = swap(ffn_stack, "dp", XBIT), swap(ffn_stack, "dp", YBIT)
    att_z = from_shards(after(att_send.reshape(att_rows, width), *ffn_z))
    rows_other = swap(after(rows_send, *att_z), "tensor", 1)
    att_stack = stacked(where, att_z, att_rows, ())

    att_far = halves_from_chips(where, att_stack, list(ffn_xy))
    shape = (4, shards, 2, heads, part, width)
    moves = [(m, near_heads(j), (j, 0, m)) for j in range(4) for m in range(2)]
    moves += [(2 + j, at(), (j, far)) for j in range(3)]
    moves += [(5 + m, at(), (3, far, m)) for m in range(2)]
    att_far = [v.reshape(shards - 1, -1, heads, part, width) for v in att_far[:3]] + [
        v.reshape(shards - 1, heads, part, width) for v in att_far[3:]
    ]
    att_own = pack(where, shape, moves, pair + att_far, (rows_other,), 0)
    att_swap = swap(att_own, "dp", CORE)

    def ffn_half(near, near_index, first, diagonal, earlier):
        mine = pl.ds(first, ffn_rows)
        moves = [(0, near_index(j), (0, j)) for j in range(4)]
        moves += [(1 + j, at(every, mine), (far, j)) for j in range(3)]
        moves += [(4, at(), (far, 3))]
        own = pack(
            where,
            (shards, 4, ffn_rows, width),
            moves,
            [near] + ffn_far[:3] + [diagonal],
            earlier,
            1,
        )
        own = own.reshape(-1, width)
        return own, swap(own, "dp", CORE)

    every = slice(None)
    ffn_far, ffn_sent = halves_from_chips(where, ffn_stack, [], True, ffn_xy)
    queries, key_rows, values, wq, wk, wv, wo = project(
        where, att_own, att_swap, inputs, rows_other, bq, bv
    )
    wq, wk, wv, wo = (w.reshape(shards * head_cols, width) for w in (wq, wk, wv, wo))
    place = jnp.stack([lengths[t // per_slot], (t % per_slot) * rows]).astype(jnp.int32)
    pairs = width // LANES // 2
    context_one, logsum_one = attend(place, queries, key_rows, values, 0, pairs, [])
    context_two, logsum_two = attend(place, queries, key_rows, values, pairs, pairs, [context_one])
    logsum = jnp.concatenate([logsum_one, logsum_two], axis=0)
    contexts = (context_one, context_two)
    hid_own, hid_swap = ffn_half(hid_near, near_hid, 0, ffn_far[3], [context_one])
    back_own, back_swap = ffn_half(back_near, near_back, ffn_rows, ffn_far[4], [context_one])
    full, low = ((rows, width), F32), ((rows, width), BF16)
    half_low = ((rows, 2 * hidden), BF16)
    three = ((3, width), F32)
    mid, zhat_one, scale_one = whole_call(
        mid_kernel,
        [low, full, ((rows, LANES), F32)],
        (*contexts, wo, inputs, b_output[None], gain_one[None], shift_one[None]),
        2 * 10**8,
    )
    act_own, slope_own = whole_call(
        hidden_kernel, [half_low, half_low], (mid, hid_own, bh[:1]), 10**9
    )
    act_swap, slope_swap = whole_call(
        hidden_kernel, [half_low, half_low], (mid, hid_swap, bh[1:]), 10**9
    )
    outputs, grad_second, grad_branch, sums_two = whole_call(
        branch_kernel,
        [low, full, low, three],
        (
            act_own,
            act_swap,
            back_own,
            back_swap,
            mid,
            b_back[None],
            gain_two[None],
            shift_two[None],
            cotangent,
        ),
        3 * 10**9,
    )

    two = shards // 2
    low_half, high_half = pl.ds(0, two), pl.ds(two, shards - two)
    each = [(k,) for k in range(shards)]

    def first_step(keep, got, picks, earlier):
        a_keep, a_send, b_keep, b_send = fold(where, [(keep, got, picks)], earlier)
        return a_keep, b_keep, swap(a_send, "dp", XBIT), swap(b_send, "dp", YBIT), a_send

    def second_step(step, a_picks, b_picks, earlier):
        a_keep, b_keep, a_got, b_got, _ = step
        a_keep, a_send, b_keep, b_send = fold(
            where, [(a_keep, a_got, a_picks), (b_keep, b_got, b_picks)], earlier
        )
        return a_keep, b_keep, swap(a_send, "dp", YBIT), swap(b_send, "dp", XBIT), a_send

    def third_step(step, earlier, beside=()):
        a_keep, b_keep, a_got, b_got, _ = step
        groups = [(a_keep, a_got, each[:two]), (b_keep, b_got, each[: shards - two])]
        return fold(where, groups, earlier, beside)

    quarter = (shards, 2, 2, ffn_rows, width)
    ffn_picks = [
        (low_half, every, 0),
        (low_half, every, 1),
        (high_half, 0),
        (high_half, 1),
    ]
    ffn_again = [(every, 0), (every, 1)]
    pair_out = [((2 * hidden, width), BF16)] * 2
    back_keep, back_send = whole_call(
        pair_grads_kernel, pair_out, (act_own, act_swap, grad_branch), 10**9
    )
    back_got = swap(back_send, "dp", CORE)
    pre_own, pre_swap, grad_b_hidden = whole_call(
        pre_kernel,
        [half_low, half_low, ((2, 2 * hidden), F32)],
        (grad_branch, back_own, back_swap, slope_own, slope_swap),
        10**9,
    )
    back_step = first_step(back_keep.reshape(quarter), back_got.reshape(quarter), ffn_picks, ())
    hid_keep, hid_send = whole_call(
        pair_grads_kernel, pair_out, (pre_own, pre_swap, mid), 3 * 10**8, (back_step[4],)
    )
    hid_got = swap(hid_send, "dp", CORE)
    grad_first, grad_attn, grad_context, sums_one = whole_call(
        first_kernel,
        [full, low, low, three],
        (
            pre_own,
            pre_swap,
            hid_own,
            hid_swap,
            grad_second,
            zhat_one,
            scale_one,
            gain_one[None],
            wo,
        ),
        3 * 10**8,
        (hid_send,),
    )
    hid_step = first_step(
        hid_keep.reshape(quarter), hid_got.reshape(quarter), ffn_picks, (grad_first,)
    )
    grad_queries, grad_keys, grad_values = attend_back(
        place, queries, key_rows, values, logsum, grad_context, hid_step[4]
    )
    total, returned_send = whole_call(
        input_kernel,
        [full, low],
        (grad_queries, grad_keys, grad_values, wq, wk, wv, grad_first),
        3 * 10**8,
    )
    returned = swap(returned_send, "tensor", 1)
    back_step = second_step(back_step, ffn_again, ffn_again, (grad_queries,))
    att_keep, att_send = attention_weight_grads(
        where,
        grad_queries,
        grad_keys,
        grad_values,
        contexts,
        grad_attn,
        inputs,
        rows_other,
        (sums_one, sums_two, grad_b_hidden),
        shards,
        (back_step[4],),
    )
    wide = att_keep.shape[-1]

    input_grad = whole_call(sum_rows_kernel, [low], (total, returned), 1)[0]
    back_pieces = third_step(back_step, (att_keep, returned))
    back_got = send_pieces(back_pieces)
    hid_step = second_step(hid_step, ffn_again, ffn_again, (back_pieces[0],))
    att_got = swap(att_send, "dp", CORE)
    att_shape = (2, 2) + att_keep.shape[1:]
    att_picks = [
        (every, 0, low_half),
        (every, 1, low_half),
        (0, every, high_half),
        (1, every, high_half),
    ]
    att_step = first_step(
        att_keep.reshape(att_shape), att_got.reshape(att_shape), att_picks, ()
    )
    hid_pieces = third_step(hid_step, ())
    back_sum = shards_reduce(back_pieces, back_got, ())
    hid_got = send_pieces(hid_pieces)
    att_step = second_step(att_step, [(0,), (1,)], [(0,), (1,)], (back_sum,))
    hid_sum = shards_reduce(hid_pieces, hid_got)
    att_pieces = third_step(att_step, (hid_sum,))
    att_got = send_pieces(att_pieces)
    top = pl.ds(0, ffn_rows)
    ffn_sum = pack(
        where,
        (2, ffn_rows, width),
        [(0, at(top), (0,)), (1, at(top), (1,))],
        [back_sum, hid_sum],
        (),
    )
    att_sum = shards_reduce(att_pieces, att_got)
    att_far = from_chips(att_sum)
    ffn_far = halves_from_chips(where, ffn_sum, [att_sum])
    halves = [pl.ds(0, ffn_rows // 2), pl.ds(ffn_rows // 2, ffn_rows // 2)]
    moves = [(j, at(), (j,)) for j in range(3)]
    moves += [(3 + k, at(), (3, slice(None), halves[k])) for k in range(2)]
    ffn_out = pack(where, (4, 2, ffn_rows, width), moves, ffn_far, ())
    back_out, hid_out = ffn_outputs(where, ffn_out, swap(ffn_out, "dp", CORE), hidden, width)
    att_out = stacked(where, att_far, att_rows, (back_out,))
    gq, gk, gv, go, sum_q, sum_v, sum_hid, *vectors = att_outputs(
        where, att_out, swap(att_out, "dp", CORE), head_cols, width
    )
    return (
        outputs,
        input_grad,
        gq.T,
        gk.T,
        gv.T,
        sum_q,
        sum_v,
        go,
        vectors[0],
        vectors[1],
        vectors[2],
        hid_out,
        sum_hid,
        back_out,
        vectors[3],
        vectors[4],
        vectors[5],
    )


def solution(mesh):
    rows = P(("dp", "tensor"), None)
    columns, depth, vector = P(None, "tensor"), P("tensor", None), P("tensor")
    return jax.shard_map(
        local,
        mesh=mesh,
        in_specs=(
            rows,
            rows,
            P("dp"),
            columns,
            columns,
            columns,
            vector,
            vector,
            depth,
            P(),
            P(),
            P(),
            columns,
            vector,
            depth,
            P(),
            P(),
            P(),
        ),
        out_specs=(
            rows,
            rows,
            columns,
            columns,
            columns,
            vector,
            vector,
            depth,
            P(),
            P(),
            P(),
            columns,
            vector,
            depth,
            P(),
            P(),
            P(),
        ),
        check_vma=False,
    )
```
